32 devices in a mesh: groups: 2 (over y), tx: 4 (over z), ty: 2 (over x), rep: 2 (over core).
Axes of the slice: x: 2, y: 2, z: 4, core: 2. Of those that a mesh axis runs over, the one named last changes fastest.
Arguments:
- features: bfloat16 [65536, 128], P(('groups', 'tx', 'ty', 'rep')), parts along dimension 0, may hold values from -6 to 6
- conv_weight: bfloat16 [27, 128, 128], replicated, may hold values from -0.109375 to 0.109375
- classifier: bfloat16 [128, 19], replicated, may hold values from -0.5 to 0.5
- send_rows: int32 [128, 128], P(('groups', 'tx', 'ty', 'rep')), parts along dimension 0, may hold values from 0 to 2048
- neighbour_map: int32 [27, 65536], P(None, ('groups', 'tx', 'ty', 'rep')), parts along dimension 1, may hold values from 0 to 2560
- labels: int32 [65536], P(('groups', 'tx', 'ty', 'rep')), parts along dimension 0, may hold values from 0 to 18
Outputs:
- grad_input: float32 [65536, 128], P(('groups', 'tx', 'ty', 'rep')), parts along dimension 0
- grad_conv: float32 [54, 128, 128], P('groups'), parts along dimension 0
- grad_head: float32 [256, 19], P('groups'), parts along dimension 0
The draws below stay inside these ranges and needn't reach their ends.
There are 2 independent parts, one for each index of `groups`. The reference program is written for one: setup_inputs(seed, part) draws one part's arguments, and reference() takes and returns one part's arrays. A program takes and returns all parts, laid end to end along the dimension named above; an argument that names none is the same for every part. Nothing has to cross between parts.
Inputs may be any that keep to these rules, and one draw needn't show every extreme that they name: `send_rows`: an entry 2048 is padding; other entries are rows of the sending tile. `neighbour_map`: rows below 2048 are the tile's own voxels, row 2048 is zero, then 128 received rows from each of the four neighbours in the order lower tx, higher tx, lower ty, higher ty.
All inputs are finite; a program needn't handle non-finite values.
Results may differ from the reference program's by a relative error of at most 0.0035.
Values may be sent and summed in bfloat16 or wider, within the bound.
No kernel may reach another device: no remote copies, remote signals or barrier semaphores. Data moves between devices by JAX's collectives and lax.ppermute only.
A program may use at most 128 MiB of HBM per device.

```python
import jax
import jax.numpy as jnp
from jax import lax

C = 128
NCLS = 19
KOFF = 27
V = 2048
B = 128
VOXELS = 32768
N_TX = 4
N_TY = 2
N_REP = 2


def place_ends(values, own_key, least, high):
    extent = values.shape
    index_at = [jax.random.randint(jax.random.fold_in(own_key, axis), (), 0, extent[axis]) for axis in range(len(extent))]
    values = values.at[tuple(index_at)].set(least)
    longest = extent.index(max(extent))
    index_at[longest] = (index_at[longest] + 1) % extent[longest]
    return values.at[tuple(index_at)].set(high)


def level_of(rng, extent, pieces, smallest, largest):
    loudness = 1.0
    for dim, parts in pieces:
        heights = jax.random.uniform(jax.random.fold_in(jax.random.fold_in(rng, 6), dim), (parts,), jnp.float32, smallest / len(pieces), largest / len(pieces))
        loudness = loudness * jnp.repeat(jnp.exp(heights), extent[dim] // parts).reshape((-1,) + (1,) * (len(extent) - 1 - dim))
    return loudness


def scatter_about(rng, extent, deviation, reach, cuts=(), dtype=jnp.bfloat16):
    result = jax.random.normal(rng, extent, jnp.float32) * deviation
    if len(cuts) > 0:
        result = level_of(rng, extent, cuts, -0.22, 0.18) * result
    return jnp.clip(result, min=-reach, max=reach).astype(dtype)


def setup_inputs(seed: int = 0, part: int = 0) -> dict:
    key_list = jax.random.split(jax.random.key(seed), 7)
    part_splits = jax.random.split(jax.random.fold_in(key_list[6], part), 7)
    return {
        "features": scatter_about(part_splits[0], (VOXELS, C), 1.0, 6.0, ((0, 16),)),
        "conv_weight": scatter_about(key_list[1], (KOFF, C, C), (KOFF * C) ** -0.5, 0.109375),
        "classifier": scatter_about(key_list[2], (C, NCLS), C ** -0.5, 0.5),
        "send_rows": place_ends(jax.random.randint(part_splits[3], (4 * N_TX * N_TY * N_REP, B), 0, V + 1), jax.random.fold_in(part_splits[3], 1), 0, V).astype(jnp.int32),
        "neighbour_map": place_ends(jax.random.randint(part_splits[4], (KOFF, VOXELS), 0, V + 1 + 4 * B), jax.random.fold_in(part_splits[4], 1), 0, (V + 1 + 4 * B) - 1).astype(jnp.int32),
        "labels": place_ends(jax.random.randint(part_splits[5], (VOXELS,), 0, NCLS), jax.random.fold_in(part_splits[5], 1), 0, NCLS - 1).astype(jnp.int32),
    }


def move_tiles(block, axis, step):
    zero = jnp.zeros_like(lax.slice_in_dim(block, 0, 1, axis=axis))
    count = block.shape[axis]
    if step == 1:
        return jnp.concatenate([zero, lax.slice_in_dim(block, 0, count - 1, axis=axis)], axis=axis)
    return jnp.concatenate([lax.slice_in_dim(block, 1, count, axis=axis), zero], axis=axis)

def local_pass(padded, incoming, neighbour_map, labels, conv_weight, classifier):
    extended = jnp.concatenate([padded, incoming.reshape(-1, C)], axis=0)
    own = padded[:V]

    def forward_step(total, index):
        piece = extended[neighbour_map[index]]
        return (total + jnp.dot(piece, conv_weight[index], preferred_element_type=jnp.float32), None)
    pre, _ = lax.scan(forward_step, jnp.zeros((V, C), jnp.float32), jnp.arange(KOFF))
    sig = jax.nn.sigmoid(pre)
    mixed = (own.astype(jnp.float32) + pre * sig).astype(jnp.bfloat16)
    logits = jnp.dot(mixed, classifier, preferred_element_type=jnp.float32)
    probs = jax.nn.softmax(logits, axis=-1)
    onehot = (labels[:, None] == jnp.arange(NCLS)[None, :]).astype(jnp.float32)
    dlogits = (probs - onehot).astype(jnp.bfloat16)
    head_part = lax.dot_general(mixed, dlogits, (((0,), (0,)), ((), ())), preferred_element_type=jnp.float32)
    dmixed = lax.dot_general(dlogits, classifier, (((1,), (1,)), ((), ())), preferred_element_type=jnp.float32)
    dpre = (dmixed * sig * (1.0 + pre * (1.0 - sig))).astype(jnp.bfloat16)

    def backward_step(table, index):
        piece = extended[neighbour_map[index]]
        wpart = lax.dot_general(piece, dpre, (((0,), (0,)), ((), ())), preferred_element_type=jnp.float32)
        dpiece = lax.dot_general(dpre, conv_weight[index], (((1,), (1,)), ((), ())), preferred_element_type=jnp.float32)
        return (table.at[neighbour_map[index]].add(dpiece), wpart)
    dext, conv_part = lax.scan(backward_step, jnp.zeros((V + 1 + 4 * B, C), jnp.float32), jnp.arange(KOFF))
    return (dmixed, dext, conv_part, head_part)

def reference(features, conv_weight, classifier, send_rows, neighbour_map, labels):
    shards = N_TX * N_TY * N_REP
    grid = features.reshape(N_TX, N_TY, N_REP, V, C)
    padded = jnp.concatenate([grid, jnp.zeros((N_TX, N_TY, N_REP, 1, C), jnp.bfloat16)], axis=3)
    sends = send_rows.reshape(N_TX, N_TY, N_REP, 4 * B)
    outgoing = jnp.take_along_axis(padded, sends[..., None], axis=3).reshape(N_TX, N_TY, N_REP, 4, B, C)
    incoming = jnp.stack([move_tiles(outgoing[:, :, :, 0], 0, 1), move_tiles(outgoing[:, :, :, 1], 0, -1), move_tiles(outgoing[:, :, :, 2], 1, 1), move_tiles(outgoing[:, :, :, 3], 1, -1)], axis=3)
    maps = neighbour_map.reshape(KOFF, N_TX, N_TY, N_REP, V).transpose(1, 2, 3, 0, 4).reshape(shards, KOFF, V)
    flat_pad = padded.reshape(shards, V + 1, C)
    flat_in = incoming.reshape(shards, 4, B, C)
    flat_labels = labels.reshape(shards, V)

    def tile_step(carry, item):
        dmixed, dext, conv_part, head_part = local_pass(item[0], item[1], item[2], item[3], conv_weight, classifier)
        return ((carry[0] + conv_part, carry[1] + head_part), (dmixed, dext))
    start = (jnp.zeros((KOFF, C, C), jnp.float32), jnp.zeros((C, NCLS), jnp.float32))
    totals, outs = lax.scan(tile_step, start, (flat_pad, flat_in, maps, flat_labels))
    dmixed, dext = outs
    back = dext[:, V + 1:].reshape(N_TX, N_TY, N_REP, 4, B, C)
    returned = jnp.stack([move_tiles(back[:, :, :, 0], 0, -1), move_tiles(back[:, :, :, 1], 0, 1), move_tiles(back[:, :, :, 2], 1, -1), move_tiles(back[:, :, :, 3], 1, 1)], axis=3)
    returned = returned.reshape(shards, 4 * B, C)
    flat_sends = sends.reshape(shards, 4 * B)
    dpad = jax.vmap(lambda table, rows, values: table.at[rows].add(values))(dext[:, :V + 1], flat_sends, returned)
    grad_input = (dpad[:, :V] + dmixed).reshape(shards * V, C)
    scale = 1.0 / jnp.sqrt(jnp.float32(shards * V))
    return (grad_input, totals[0] * scale, totals[1] * scale)
```

```python
import functools
import math

import jax
import jax.numpy as jnp
from jax import lax
from jax.experimental import pallas as pl
from jax.experimental.pallas import tpu as pltpu
from jax.sharding import PartitionSpec as P

STREAMS = 4
SEGMENT = 64
GAP = 16
CHUNKS = 3
HEAD_ROWS = 32
VMEM = pl.BlockSpec(memory_space=pltpu.VMEM)
HBM = pl.BlockSpec(memory_space=pl.ANY)
NN = (((1,), (0,)), ((), ()))
NT = (((1,), (1,)), ((), ()))
TN = (((0,), (0,)), ((), ()))


def dot(a, b, dims):
    return lax.dot_general(a, b, dims, preferred_element_type=jnp.float32)


def fetch(map_hbm, index, sems, first, length):
    copies = []
    for n, ref in enumerate(index):
        copy = pltpu.make_async_copy(
            map_hbm.at[pl.ds((first + n) * length, length)], ref, sems.at[n]
        )
        copy.start()
        copies.append(copy)
    return copies


def forward_kernel(
    classes, map_hbm, own_ref, halo_refs, weight_ref, class_ref, label_ref,
    dpre_ref, dmixed_ref, conv_ref, table, rows, wide, total, sems, *index,
):
    voxels, chans = dpre_ref.shape
    offsets = len(index) // STREAMS
    stream = voxels // STREAMS
    block = STREAMS * SEGMENT
    copies = fetch(map_hbm, index, sems, 0, stream)
    width = halo_refs[0].shape[0]
    table[:voxels, :] = own_ref[...].astype(jnp.float32)
    table[voxels : voxels + GAP, :] = jnp.zeros((GAP, chans), jnp.float32)
    for n, halo in enumerate(halo_refs):
        start = voxels + GAP + n * width
        table[start : start + width, :] = halo[...].astype(jnp.float32)
    total[...] = jnp.zeros_like(total)
    conv_ref[pl.ds(offsets * chans, conv_ref.shape[0] - offsets * chans), :] = jnp.zeros(
        (conv_ref.shape[0] - offsets * chans, chans), jnp.float32
    )
    for copy in copies:
        copy.wait()

    def block_step(b, carry):
        def gather_step(i, carry):
            at = i - b * SEGMENT
            for u in range(STREAMS):
                for k in range(offsets):
                    rows[k, pl.ds(u * SEGMENT + at, 1), :] = table[
                        pl.ds(index[k * STREAMS + u][i], 1), :
                    ]
            return carry

        lax.fori_loop(b * SEGMENT, (b + 1) * SEGMENT, gather_step, 0)
        for k in range(offsets):
            wide[:, k * chans : (k + 1) * chans] = rows[k].astype(jnp.bfloat16)
        pre = dot(wide[...], weight_ref[...], NN)
        starts = [pl.multiple_of(u * stream + b * SEGMENT, SEGMENT) for u in range(STREAMS)]
        own = jnp.concatenate([table[pl.ds(s, SEGMENT), :] for s in starts], axis=0)
        sig = jax.nn.sigmoid(pre)
        mixed = (own + pre * sig).astype(jnp.bfloat16)
        logits = dot(class_ref[...], mixed, NT)
        which = lax.broadcasted_iota(jnp.int32, logits.shape, 0)
        logits = jnp.where(which < classes, logits, -1e30)
        high = jnp.max(logits, axis=0, keepdims=True)
        expd = jnp.exp(logits - high)
        probs = expd / jnp.sum(expd, axis=0, keepdims=True)
        onehot = (which == label_ref[b]).astype(jnp.float32)
        dlogits = (probs - onehot).astype(jnp.bfloat16)
        conv_ref[pl.ds(offsets * chans, HEAD_ROWS), :] += dot(dlogits, mixed, NN)
        dmixed = dot(dlogits, class_ref[...], TN)
        dpre = (dmixed * sig * (1.0 + pre * (1.0 - sig))).astype(jnp.bfloat16)
        full = dpre.astype(jnp.float32)
        for u, s in enumerate(starts):
            dmixed_ref[pl.ds(s, SEGMENT), :] = dmixed[u * SEGMENT : (u + 1) * SEGMENT]
            dpre_ref[pl.ds(s, SEGMENT), :] = full[u * SEGMENT : (u + 1) * SEGMENT]
        total[...] += dot(full.T.astype(jnp.bfloat16), wide[...], NN)
        return carry

    lax.fori_loop(0, voxels // block, block_step, 0)
    for k in range(offsets):
        conv_ref[k * chans : (k + 1) * chans, :] = total[:, k * chans : (k + 1) * chans].T


def forward(map_flat, features, incoming, weights, class_t, label_blocks, classes, reduce_rows, table_rows):
    voxels, chans = features.shape
    offsets = weights.shape[0] // chans
    stream = voxels // STREAMS
    block = STREAMS * SEGMENT
    return pl.pallas_call(
        functools.partial(forward_kernel, classes),
        out_shape=(
            jax.ShapeDtypeStruct((voxels, chans), jnp.float32),
            jax.ShapeDtypeStruct((voxels, chans), jnp.float32),
            jax.ShapeDtypeStruct((reduce_rows, chans), jnp.float32),
        ),
        in_specs=[HBM, VMEM, [VMEM] * 4, VMEM, VMEM, VMEM],
        out_specs=(VMEM, VMEM, VMEM),
        scratch_shapes=[
            pltpu.VMEM((table_rows, chans), jnp.float32),
            pltpu.VMEM((offsets, block, chans), jnp.float32),
            pltpu.VMEM((block, offsets * chans), jnp.bfloat16),
            pltpu.VMEM((chans, offsets * chans), jnp.float32),
            pltpu.SemaphoreType.DMA((offsets * STREAMS,)),
        ]
        + [pltpu.SMEM((stream,), jnp.int32)] * (offsets * STREAMS),
        compiler_params=pltpu.CompilerParams(vmem_limit_bytes=40 << 20),
        cost_estimate=pl.CostEstimate(
            flops=4 * voxels * offsets * chans * chans, bytes_accessed=150 << 20, transcendentals=0
        ),
        name="forward",
    )(map_flat, features, incoming, weights, class_t, label_blocks)


def scatter_kernel(first, has_before, map_hbm, dpre_ref, weight_ref, *refs):
    refs = list(refs)
    before = refs.pop(0) if has_before else None
    out_ref, sems = refs[0], refs[1]
    offsets = weight_ref.shape[0] // weight_ref.shape[1]
    tables = refs[2 : 2 + offsets]
    index = refs[2 + offsets :]
    voxels, chans = dpre_ref.shape
    stream = voxels // STREAMS
    copies = fetch(map_hbm, index, sems, first * STREAMS, stream)
    for table in tables:
        table[...] = jnp.zeros_like(table)
    for copy in copies:
        copy.wait()

    def step(i, carry):
        for u in range(STREAMS):
            row = dpre_ref[pl.ds(u * stream + i, 1), :]
            for k in range(offsets):
                at = pl.ds(index[k * STREAMS + u][i], 1)
                tables[k][at, :] = tables[k][at, :] + row
        return carry

    lax.fori_loop(0, stream, step, 0)
    tiles = 3
    height = out_ref.shape[0] // tiles

    def finish(t, carry):
        at = pl.ds(pl.multiple_of(t * height, 16), height)
        wide = jnp.concatenate([table[at, :].astype(jnp.bfloat16) for table in tables], axis=1)
        result = dot(wide, weight_ref[...], NN)
        out_ref[at, :] = result + before[at, :] if has_before else result
        return carry

    lax.fori_loop(0, tiles, finish, 0)


def scatter(map_flat, dpre, weights_t, before, first, table_rows):
    voxels, chans = dpre.shape
    offsets = weights_t.shape[0] // chans
    stream = voxels // STREAMS
    has_before = before is not None
    return pl.pallas_call(
        functools.partial(scatter_kernel, first, has_before),
        out_shape=jax.ShapeDtypeStruct((table_rows, chans), jnp.float32),
        in_specs=[HBM, VMEM, VMEM] + ([VMEM] if has_before else []),
        out_specs=VMEM,
        scratch_shapes=[pltpu.SemaphoreType.DMA((offsets * STREAMS,))]
        + [pltpu.VMEM((table_rows, chans), jnp.float32)] * offsets
        + [pltpu.SMEM((stream,), jnp.int32)] * (offsets * STREAMS),
        compiler_params=pltpu.CompilerParams(vmem_limit_bytes=40 << 20),
        cost_estimate=pl.CostEstimate(
            flops=2 * voxels * offsets * chans * chans, bytes_accessed=40 << 20, transcendentals=0
        ),
        name=f"scatter_{first}",
    )(map_flat, dpre, weights_t, *([before] if has_before else []))


def finish_kernel(dmixed_ref, dext_ref, send_ref, back_ref, out_ref):
    voxels, chans = out_ref.shape
    height = voxels // 8

    def step(t, carry):
        at = pl.ds(pl.multiple_of(t * height, height), height)
        row = lax.broadcasted_iota(jnp.int32, (height, send_ref.shape[1]), 0) + t * height
        chosen = (row == send_ref[...]).astype(jnp.float32).astype(jnp.bfloat16)
        out_ref[at, :] = dmixed_ref[at, :] + dext_ref[at, :] + dot(chosen, back_ref[...], NN)
        return carry

    lax.fori_loop(0, voxels // height, step, 0)


def finish(dmixed, dext, send_flat, back):
    return pl.pallas_call(
        finish_kernel,
        out_shape=jax.ShapeDtypeStruct(dmixed.shape, jnp.float32),
        in_specs=[VMEM] * 4,
        out_specs=VMEM,
        compiler_params=pltpu.CompilerParams(vmem_limit_bytes=40 << 20),
        cost_estimate=pl.CostEstimate(flops=1 << 28, bytes_accessed=4 << 20, transcendentals=0),
        name="finish",
    )(dmixed, dext, send_flat, back)


def exchange(shard, axis, distance):
    devices = lax.axis_size(axis)
    return lax.ppermute(shard, axis, [(i, i ^ distance) for i in range(devices)])


def swap_edges(down, up, axis):
    devices = lax.axis_size(axis)
    odd = (lax.axis_index(axis) & 1) != 0
    even_pairs = [(i, i ^ 1) for i in range(devices) if (i ^ 1) < devices]
    odd_pairs = [(i, ((i + 1) ^ 1) - 1) for i in range(1, devices) if ((i + 1) ^ 1) - 1 < devices]
    first = lax.ppermute(jnp.where(odd, down, up), axis, even_pairs)
    if odd_pairs:
        second = lax.ppermute(jnp.where(odd, up, down), axis, odd_pairs)
    else:
        second = jnp.zeros_like(first)
    return jnp.where(odd, first, second), jnp.where(odd, second, first)


def on_device(features, conv_weight, classifier, send_rows, neighbour_map, labels):
    voxels, chans = features.shape
    width = send_rows.shape[1]
    offsets = conv_weight.shape[0]
    classes = classifier.shape[1]
    block = STREAMS * SEGMENT
    table_rows = -(-(voxels + GAP + 4 * width) // 48) * 48
    reduce_rows = -(-(offsets * chans + HEAD_ROWS) // 64) * 64

    outgoing = jnp.where(
        (send_rows < voxels)[..., None], features[jnp.minimum(send_rows, voxels - 1)], 0
    )
    low_y, high_y = swap_edges(outgoing[3], outgoing[2], "ty")
    low_x, high_x = swap_edges(outgoing[1], outgoing[0], "tx")

    map_flat = jnp.where(neighbour_map > voxels, neighbour_map + (GAP - 1), neighbour_map).reshape(-1)
    weights = conv_weight.reshape(offsets * chans, chans)
    weights_t = conv_weight.transpose(0, 2, 1).reshape(offsets * chans, chans)
    class_t = jnp.pad(classifier.T, ((0, HEAD_ROWS - classes), (0, 0)))
    label_blocks = (
        labels.reshape(STREAMS, voxels // block, SEGMENT).transpose(1, 0, 2)
        .reshape(voxels // block, 1, block)
    )
    dpre, dmixed, part = forward(
        map_flat, features, [low_x, high_x, low_y, high_y], weights, class_t, label_blocks,
        classes, reduce_rows, table_rows,
    )

    chunks = [
        (c * offsets // CHUNKS, (c + 1) * offsets // CHUNKS) for c in range(CHUNKS)
    ]
    dext = None

    def scatter_beside(sent, before):
        if not chunks:
            return sent, before
        first, last = chunks.pop(0)
        held = (sent, dpre) if before is None else (sent, dpre, before)
        held = lax.optimization_barrier(held)
        return held[0], scatter(
            map_flat, held[1], weights_t[first * chans : last * chans],
            None if before is None else held[2], first, table_rows,
        )

    halved = []
    for axis, kind in (("rep", jnp.float32), ("ty", jnp.bfloat16)):
        distance = lax.axis_size(axis) // 2
        while distance:
            halved.append((axis, distance))
            upper = (lax.axis_index(axis) & distance) != 0
            half = part.shape[0] // 2
            low, high = part[:half], part[half:]
            sent = jnp.where(upper, low, high).astype(kind)
            if axis != "rep":
                sent, dext = scatter_beside(sent, dext)
            got = exchange(sent, axis, distance)
            if dext is not None:
                got, dext = lax.optimization_barrier((got, dext))
            part = jnp.where(upper, high, low) + got.astype(jnp.float32)
            distance //= 2
    distance = lax.axis_size("tx") // 2
    kind = jnp.bfloat16
    while distance:
        sent, dext = scatter_beside(part.astype(kind), dext)
        got, dext = lax.optimization_barrier((exchange(sent, "tx", distance), dext))
        part = sent.astype(jnp.float32) + got.astype(jnp.float32)
        distance //= 2
        kind = jnp.float32
    while chunks:
        part, dext = scatter_beside(part, dext)
    total = part.astype(jnp.bfloat16)
    for axis, distance in reversed(halved):
        upper = (lax.axis_index(axis) & distance) != 0
        got = exchange(total, axis, distance)
        total = jnp.where(
            upper, jnp.concatenate([got, total], axis=0), jnp.concatenate([total, got], axis=0)
        )

    start = voxels + GAP
    halo = dext[start : start + 4 * width].astype(jnp.bfloat16).reshape(4, width, chans)
    back_3, back_2 = swap_edges(halo[2], halo[3], "ty")
    back_1, back_0 = swap_edges(halo[0], halo[1], "tx")
    back = jnp.concatenate([back_0, back_1, back_2, back_3], axis=0)
    grad_input = finish(dmixed, dext, send_rows.reshape(1, -1), back)

    count = voxels * lax.axis_size("tx") * lax.axis_size("ty") * lax.axis_size("rep")
    scale = 1.0 / math.sqrt(count)
    total = total.astype(jnp.float32) * scale
    grad_conv = total[: offsets * chans].reshape(offsets, chans, chans)
    grad_head = total[offsets * chans : offsets * chans + classes].T
    return grad_input, grad_conv, grad_head


def solution(mesh):
    placed = (
        P(("groups", "tx", "ty", "rep"), None),
        P(),
        P(),
        P(("groups", "tx", "ty", "rep"), None),
        P(None, ("groups", "tx", "ty", "rep")),
        P(("groups", "tx", "ty", "rep")),
    )
    return jax.shard_map(
        on_device,
        mesh=mesh,
        in_specs=placed,
        out_specs=(
            P(("groups", "tx", "ty", "rep"), None),
            P("groups", None, None),
            P("groups", None),
        ),
        check_vma=False,
    )
```

```python
import functools
import math

import jax
import jax.numpy as jnp
from jax import lax
from jax.experimental import pallas as pl
from jax.experimental.pallas import tpu as pltpu
from jax.sharding import PartitionSpec as P

STREAMS = 4
SCATTER_STREAMS = 8
SEGMENT = 64
GAP = 16
CHUNKS = 3
HEAD_ROWS = 32
VMEM = pl.BlockSpec(memory_space=pltpu.VMEM)
HBM = pl.BlockSpec(memory_space=pl.ANY)
NN = (((1,), (0,)), ((), ()))
NT = (((1,), (1,)), ((), ()))
TN = (((0,), (0,)), ((), ()))


def dot(a, b, dims):
    return lax.dot_general(a, b, dims, preferred_element_type=jnp.float32)


def fetch(map_hbm, index, sems, first, length, parts):
    stages = []
    for part, (start, stop) in enumerate(zip(parts[:-1], parts[1:])):
        stage = []
        for n, ref in enumerate(index):
            at = (first + n) * length + start
            stage.append(
                pltpu.make_async_copy(
                    map_hbm.at[pl.ds(at, stop - start)], ref.at[pl.ds(start, stop - start)],
                    sems.at[part, n],
                )
            )
        for copy in stage:
            copy.start()
        stages.append(stage)
    return stages


def forward_kernel(
    classes, map_hbm, own_ref, halo_refs, weight_ref, class_ref, label_ref,
    dpre_ref, dmixed_ref, conv_ref, flipped_ref, table, rows, wide, total, sems, *index,
):
    voxels, chans = dpre_ref.shape
    offsets = len(index) // STREAMS
    stream = voxels // STREAMS
    block = STREAMS * SEGMENT
    ready, later = fetch(map_hbm, index, sems, 0, stream, (0, 128, stream))
    width = halo_refs[0].shape[0]
    table[:voxels, :] = own_ref[...].astype(jnp.float32)
    table[voxels : voxels + GAP, :] = jnp.zeros((GAP, chans), jnp.float32)
    for n, halo in enumerate(halo_refs):
        start = voxels + GAP + n * width
        table[start : start + width, :] = halo[...].astype(jnp.float32)
    total[...] = jnp.zeros_like(total)
    conv_ref[pl.ds(offsets * chans, conv_ref.shape[0] - offsets * chans), :] = jnp.zeros(
        (conv_ref.shape[0] - offsets * chans, chans), jnp.float32
    )
    for k in range(offsets):
        at = slice(k * chans, (k + 1) * chans)
        flipped_ref[at, :] = weight_ref[at, :].T
    for copy in ready:
        copy.wait()

    def block_step(b, carry):
        @pl.when(b == 128 // SEGMENT)
        def _():
            for copy in later:
                copy.wait()

        def gather_step(i, carry):
            at = i - b * SEGMENT
            for u in range(STREAMS):
                for k in range(offsets):
                    rows[k, pl.ds(u * SEGMENT + at, 1), :] = table[
                        pl.ds(index[k * STREAMS + u][i], 1), :
                    ]
            return carry

        lax.fori_loop(b * SEGMENT, (b + 1) * SEGMENT, gather_step, 0)
        for k in range(offsets):
            wide[:, k * chans : (k + 1) * chans] = rows[k].astype(jnp.bfloat16)
        pre = dot(wide[...], weight_ref[...], NN)
        starts = [pl.multiple_of(u * stream + b * SEGMENT, SEGMENT) for u in range(STREAMS)]
        own = jnp.concatenate([table[pl.ds(s, SEGMENT), :] for s in starts], axis=0)
        sig = jax.nn.sigmoid(pre)
        mixed = (own + pre * sig).astype(jnp.bfloat16)
        logits = dot(class_ref[...], mixed, NT)
        which = lax.broadcasted_iota(jnp.int32, logits.shape, 0)
        logits = jnp.where(which < classes, logits, -1e30)
        high = jnp.max(logits, axis=0, keepdims=True)
        expd = jnp.exp(logits - high)
        probs = expd / jnp.sum(expd, axis=0, keepdims=True)
        onehot = (which == label_ref[b]).astype(jnp.float32)
        dlogits = (probs - onehot).astype(jnp.bfloat16)
        conv_ref[pl.ds(offsets * chans, HEAD_ROWS), :] += dot(dlogits, mixed, NN)
        dmixed = dot(dlogits, class_ref[...], TN)
        dpre = (dmixed * sig * (1.0 + pre * (1.0 - sig))).astype(jnp.bfloat16)
        full = dpre.astype(jnp.float32)
        for u, s in enumerate(starts):
            dmixed_ref[pl.ds(s, SEGMENT), :] = dmixed[u * SEGMENT : (u + 1) * SEGMENT]
            dpre_ref[pl.ds(s, SEGMENT), :] = full[u * SEGMENT : (u + 1) * SEGMENT]
        total[...] += dot(full.T.astype(jnp.bfloat16), wide[...], NN)
        return carry

    lax.fori_loop(0, voxels // block, block_step, 0)
    for k in range(offsets):
        conv_ref[k * chans : (k + 1) * chans, :] = total[:, k * chans : (k + 1) * chans].T


def forward(map_flat, features, incoming, weights, class_t, label_blocks, classes, reduce_rows, table_rows):
    voxels, chans = features.shape
    offsets = weights.shape[0] // chans
    stream = voxels // STREAMS
    block = STREAMS * SEGMENT
    return pl.pallas_call(
        functools.partial(forward_kernel, classes),
        out_shape=(
            jax.ShapeDtypeStruct((voxels, chans), jnp.float32),
            jax.ShapeDtypeStruct((voxels, chans), jnp.float32),
            jax.ShapeDtypeStruct((reduce_rows, chans), jnp.float32),
            jax.ShapeDtypeStruct(weights.shape, jnp.bfloat16),
        ),
        in_specs=[HBM, VMEM, [VMEM] * 4, VMEM, VMEM, VMEM],
        out_specs=(VMEM, VMEM, VMEM, VMEM),
        scratch_shapes=[
            pltpu.VMEM((table_rows, chans), jnp.float32),
            pltpu.VMEM((offsets, block, chans), jnp.float32),
            pltpu.VMEM((block, offsets * chans), jnp.bfloat16),
            pltpu.VMEM((chans, offsets * chans), jnp.float32),
            pltpu.SemaphoreType.DMA((2, offsets * STREAMS)),
        ]
        + [pltpu.SMEM((stream,), jnp.int32)] * (offsets * STREAMS),
        compiler_params=pltpu.CompilerParams(vmem_limit_bytes=40 << 20),
        cost_estimate=pl.CostEstimate(
            flops=4 * voxels * offsets * chans * chans, bytes_accessed=150 << 20, transcendentals=0
        ),
        name="forward",
    )(map_flat, features, incoming, weights, class_t, label_blocks)


def scatter_kernel(first, offsets, has_before, map_hbm, dpre_ref, weight_ref, *refs):
    refs = list(refs)
    before = refs.pop(0) if has_before else None
    out_ref, sems = refs[0], refs[1]
    tables = refs[2 : 2 + offsets]
    index = refs[2 + offsets :]
    voxels, chans = dpre_ref.shape
    stream = voxels // SCATTER_STREAMS
    ready, later = fetch(map_hbm, index, sems, first * SCATTER_STREAMS, stream, (0, 128, stream))
    for table in tables:
        table[...] = jnp.zeros_like(table)
    for copy in ready:
        copy.wait()

    def step(i, carry):
        for u in range(SCATTER_STREAMS):
            row = dpre_ref[pl.ds(u * stream + i, 1), :]
            for k in range(offsets):
                at = pl.ds(index[k * SCATTER_STREAMS + u][i], 1)
                tables[k][at, :] = tables[k][at, :] + row
        return carry

    lax.fori_loop(0, 128, step, 0)
    for copy in later:
        copy.wait()
    lax.fori_loop(128, stream, step, 0)
    tiles = 3
    height = out_ref.shape[0] // tiles

    def finish(t, carry):
        at = pl.ds(pl.multiple_of(t * height, 16), height)
        wide = jnp.concatenate([table[at, :].astype(jnp.bfloat16) for table in tables], axis=1)
        result = dot(wide, weight_ref[first * chans : (first + offsets) * chans, :], NN)
        out_ref[at, :] = result + before[at, :] if has_before else result
        return carry

    lax.fori_loop(0, tiles, finish, 0)


def scatter(map_flat, dpre, flipped, before, first, offsets, table_rows):
    voxels, chans = dpre.shape
    stream = voxels // SCATTER_STREAMS
    has_before = before is not None
    return pl.pallas_call(
        functools.partial(scatter_kernel, first, offsets, has_before),
        out_shape=jax.ShapeDtypeStruct((table_rows, chans), jnp.float32),
        in_specs=[HBM, VMEM, VMEM] + ([VMEM] if has_before else []),
        out_specs=VMEM,
        scratch_shapes=[pltpu.SemaphoreType.DMA((2, offsets * SCATTER_STREAMS))]
        + [pltpu.VMEM((table_rows, chans), jnp.float32)] * offsets
        + [pltpu.SMEM((stream,), jnp.int32)] * (offsets * SCATTER_STREAMS),
        compiler_params=pltpu.CompilerParams(vmem_limit_bytes=40 << 20),
        cost_estimate=pl.CostEstimate(
            flops=2 * voxels * offsets * chans * chans, bytes_accessed=40 << 20, transcendentals=0
        ),
        name=f"scatter_{first}",
    )(map_flat, dpre, flipped, *([before] if has_before else []))


def finish_kernel(dmixed_ref, dext_ref, send_ref, back_ref, out_ref):
    voxels, chans = out_ref.shape
    height = voxels // 8

    def step(t, carry):
        at = pl.ds(pl.multiple_of(t * height, height), height)
        row = lax.broadcasted_iota(jnp.int32, (height, send_ref.shape[1]), 0) + t * height
        chosen = (row == send_ref[...]).astype(jnp.float32).astype(jnp.bfloat16)
        out_ref[at, :] = dmixed_ref[at, :] + dext_ref[at, :] + dot(chosen, back_ref[...], NN)
        return carry

    lax.fori_loop(0, voxels // height, step, 0)


def finish(dmixed, dext, send_flat, back):
    return pl.pallas_call(
        finish_kernel,
        out_shape=jax.ShapeDtypeStruct(dmixed.shape, jnp.float32),
        in_specs=[VMEM] * 4,
        out_specs=VMEM,
        compiler_params=pltpu.CompilerParams(vmem_limit_bytes=40 << 20),
        cost_estimate=pl.CostEstimate(flops=1 << 28, bytes_accessed=4 << 20, transcendentals=0),
        name="finish",
    )(dmixed, dext, send_flat, back)


def exchange(shard, axis, distance):
    devices = lax.axis_size(axis)
    return lax.ppermute(shard, axis, [(i, i ^ distance) for i in range(devices)])


def swap_edges(down, up, axis):
    devices = lax.axis_size(axis)
    odd = (lax.axis_index(axis) & 1) != 0
    even_pairs = [(i, i ^ 1) for i in range(devices) if (i ^ 1) < devices]
    odd_pairs = [(i, ((i + 1) ^ 1) - 1) for i in range(1, devices) if ((i + 1) ^ 1) - 1 < devices]
    first = lax.ppermute(jnp.where(odd, down, up), axis, even_pairs)
    if odd_pairs:
        second = lax.ppermute(jnp.where(odd, up, down), axis, odd_pairs)
    else:
        second = jnp.zeros_like(first)
    return jnp.where(odd, first, second), jnp.where(odd, second, first)


def on_device(features, conv_weight, classifier, send_rows, neighbour_map, labels):
    voxels, chans = features.shape
    width = send_rows.shape[1]
    offsets = conv_weight.shape[0]
    classes = classifier.shape[1]
    block = STREAMS * SEGMENT
    table_rows = -(-(voxels + GAP + 4 * width) // 48) * 48
    reduce_rows = -(-(offsets * chans + HEAD_ROWS) // 64) * 64

    outgoing = jnp.where(
        (send_rows < voxels)[..., None], features[jnp.minimum(send_rows, voxels - 1)], 0
    )
    low_y, high_y = swap_edges(outgoing[3], outgoing[2], "ty")
    low_x, high_x = swap_edges(outgoing[1], outgoing[0], "tx")

    map_flat = jnp.where(neighbour_map > voxels, neighbour_map + (GAP - 1), neighbour_map).reshape(-1)
    weights = conv_weight.reshape(offsets * chans, chans)
    class_t = jnp.pad(classifier.T, ((0, HEAD_ROWS - classes), (0, 0)))
    label_blocks = (
        labels.reshape(STREAMS, voxels // block, SEGMENT).transpose(1, 0, 2)
        .reshape(voxels // block, 1, block)
    )
    dpre, dmixed, part, flipped = forward(
        map_flat, features, [low_x, high_x, low_y, high_y], weights, class_t, label_blocks,
        classes, reduce_rows, table_rows,
    )

    chunks = [
        (c * offsets // CHUNKS, (c + 1) * offsets // CHUNKS) for c in range(CHUNKS)
    ]
    dext = None

    def scatter_beside(sent, before):
        if not chunks:
            return sent, before
        first, last = chunks.pop(0)
        held = (sent, dpre) if before is None else (sent, dpre, before)
        held = lax.optimization_barrier(held)
        return held[0], scatter(
            map_flat, held[1], flipped, None if before is None else held[2],
            first, last - first, table_rows,
        )

    halved = []
    for axis, kind in (("rep", jnp.float32), ("ty", jnp.bfloat16)):
        distance = lax.axis_size(axis) // 2
        while distance:
            halved.append((axis, distance))
            upper = (lax.axis_index(axis) & distance) != 0
            half = part.shape[0] // 2
            low, high = part[:half], part[half:]
            sent = jnp.where(upper, low, high).astype(kind)
            if axis != "rep":
                sent, dext = scatter_beside(sent, dext)
            got = exchange(sent, axis, distance)
            if dext is not None:
                got, dext = lax.optimization_barrier((got, dext))
            part = jnp.where(upper, high, low) + got.astype(jnp.float32)
            distance //= 2
    distance = lax.axis_size("tx") // 2
    kind = jnp.bfloat16
    while distance:
        sent, dext = scatter_beside(part.astype(kind), dext)
        got, dext = lax.optimization_barrier((exchange(sent, "tx", distance), dext))
        part = sent.astype(jnp.float32) + got.astype(jnp.float32)
        distance //= 2
        kind = jnp.float32
    while chunks:
        part, dext = scatter_beside(part, dext)
    total = part.astype(jnp.bfloat16)
    for axis, distance in reversed(halved):
        upper = (lax.axis_index(axis) & distance) != 0
        total_before, got = total, exchange(total, axis, distance)
        low, high = jnp.where(upper, got, total), jnp.where(upper, total, got)
        total = jnp.concatenate([low, high], axis=0)

    start = voxels + GAP
    halo = dext[start : start + 4 * width].astype(jnp.bfloat16).reshape(4, width, chans)
    back_3, back_2 = swap_edges(halo[2], halo[3], "ty")
    back_1, back_0 = swap_edges(halo[0], halo[1], "tx")
    back = jnp.concatenate([back_0, back_1, back_2, back_3], axis=0)
    grad_input = finish(dmixed, dext, send_rows.reshape(1, -1), back)

    count = voxels * lax.axis_size("tx") * lax.axis_size("ty") * lax.axis_size("rep")
    scale = 1.0 / math.sqrt(count)
    split = offsets * chans - low.shape[0]
    grad_conv = jnp.concatenate([low, high[:split]], axis=0).astype(jnp.float32) * scale
    grad_conv = grad_conv.reshape(offsets, chans, chans)
    grad_head = jnp.where(
        upper, total_before[split : split + classes], got[split : split + classes]
    ).T.astype(jnp.float32) * scale
    return grad_input, grad_conv, grad_head


def solution(mesh):
    placed = (
        P(("groups", "tx", "ty", "rep"), None),
        P(),
        P(),
        P(("groups", "tx", "ty", "rep"), None),
        P(None, ("groups", "tx", "ty", "rep")),
        P(("groups", "tx", "ty", "rep")),
    )
    return jax.shard_map(
        on_device,
        mesh=mesh,
        in_specs=placed,
        out_specs=(
            P(("groups", "tx", "ty", "rep"), None),
            P("groups", None, None),
            P("groups", None),
        ),
        check_vma=False,
    )
```

```python
import functools
import math

import jax
import jax.numpy as jnp
from jax import lax
from jax.experimental import pallas as pl
from jax.experimental.pallas import tpu as pltpu
from jax.sharding import PartitionSpec as P

STREAMS = 4
SCATTER_STREAMS = 8
SEGMENT = 64
BY_MATMUL = 8
GAP = 16
CHUNKS = 3
HEAD_ROWS = 32
VMEM = pl.BlockSpec(memory_space=pltpu.VMEM)
HBM = pl.BlockSpec(memory_space=pl.ANY)
NN = (((1,), (0,)), ((), ()))
NT = (((1,), (1,)), ((), ()))
TN = (((0,), (0,)), ((), ()))


def dot(a, b, dims):
    return lax.dot_general(a, b, dims, preferred_element_type=jnp.float32)


def fetch(map_hbm, index, sems, first, length, parts):
    stages = []
    for part, (start, stop) in enumerate(zip(parts[:-1], parts[1:])):
        stage = []
        for n, ref in enumerate(index):
            at = (first + n) * length + start
            stage.append(
                pltpu.make_async_copy(
                    map_hbm.at[pl.ds(at, stop - start)], ref.at[pl.ds(start, stop - start)],
                    sems.at[part, n],
                )
            )
        for copy in stage:
            copy.start()
        stages.append(stage)
    return stages


def forward_kernel(
    classes, map_hbm, sparse_ref, own_ref, halo_refs, weight_ref, class_ref, label_ref,
    dpre_ref, dmixed_ref, conv_ref, flipped_ref,
    table, turned, rows, wide, columns, side, total, sems, *index,
):
    voxels, chans = dpre_ref.shape
    looped = len(index) // STREAMS
    offsets = looped + BY_MATMUL
    stream = voxels // STREAMS
    block = STREAMS * SEGMENT
    share = SEGMENT // BY_MATMUL
    ready, later = fetch(map_hbm, index, sems, 0, stream, (0, 128, stream))
    width = halo_refs[0].shape[0]
    table[:voxels, :] = own_ref[...].astype(jnp.float32)
    for n, halo in enumerate(halo_refs):
        start = voxels + n * width
        table[start : start + width, :] = halo[...].astype(jnp.float32)
    filled = voxels + 4 * width
    table[filled:, :] = jnp.zeros((table.shape[0] - filled, chans), jnp.float32)
    for n in range(filled // chans):
        at = slice(n * chans, (n + 1) * chans)
        turned[:, at] = table[at, :].T.astype(jnp.bfloat16)
    total[...] = jnp.zeros_like(total)
    conv_ref[pl.ds(offsets * chans, conv_ref.shape[0] - offsets * chans), :] = jnp.zeros(
        (conv_ref.shape[0] - offsets * chans, chans), jnp.float32
    )
    for k in range(offsets):
        at = slice(k * chans, (k + 1) * chans)
        turned_weight = weight_ref[at, :].T
        flipped_ref[at, :] = turned_weight
        if k >= looped:
            side[:, (k - looped) * chans : (k - looped + 1) * chans] = turned_weight
    for copy in ready:
        copy.wait()

    def block_step(b, carry):
        @pl.when(b == 128 // SEGMENT)
        def _():
            for copy in later:
                copy.wait()

        def gather_step(j, carry):
            row = lax.broadcasted_iota(jnp.int32, (filled, block), 0)
            chosen = (row == sparse_ref[b, pl.ds(j, 1), :]).astype(jnp.float32)
            at = pl.ds(pl.multiple_of(j * chans, chans), chans)
            columns[at, :] = dot(turned[...], chosen.astype(jnp.bfloat16), NN).astype(jnp.bfloat16)
            for n in range(share):
                to = j * share + n
                i = b * SEGMENT + to
                for u in range(STREAMS):
                    for k in range(looped):
                        rows[k, pl.ds(u * SEGMENT + to, 1), :] = table[
                            pl.ds(index[k * STREAMS + u][i], 1), :
                        ]
            return carry

        lax.fori_loop(0, BY_MATMUL, gather_step, 0)
        for k in range(looped):
            wide[:, k * chans : (k + 1) * chans] = rows[k].astype(jnp.bfloat16)
        pre = dot(wide[...], weight_ref[: looped * chans, :], NN)
        pre = pre + dot(side[...], columns[...], NN).T
        starts = [pl.multiple_of(u * stream + b * SEGMENT, SEGMENT) for u in range(STREAMS)]
        own = jnp.concatenate([table[pl.ds(s, SEGMENT), :] for s in starts], axis=0)
        sig = jax.nn.sigmoid(pre)
        mixed = (own + pre * sig).astype(jnp.bfloat16)
        logits = dot(class_ref[...], mixed, NT)
        which = lax.broadcasted_iota(jnp.int32, logits.shape, 0)
        logits = jnp.where(which < classes, logits, -1e30)
        high = jnp.max(logits, axis=0, keepdims=True)
        expd = jnp.exp(logits - high)
        probs = expd / jnp.sum(expd, axis=0, keepdims=True)
        onehot = (which == label_ref[b]).astype(jnp.float32)
        dlogits = (probs - onehot).astype(jnp.bfloat16)
        conv_ref[pl.ds(offsets * chans, HEAD_ROWS), :] += dot(dlogits, mixed, NN)
        dmixed = dot(dlogits, class_ref[...], TN)
        dpre = (dmixed * sig * (1.0 + pre * (1.0 - sig))).astype(jnp.bfloat16)
        full = dpre.astype(jnp.float32)
        for u, s in enumerate(starts):
            dmixed_ref[pl.ds(s, SEGMENT), :] = dmixed[u * SEGMENT : (u + 1) * SEGMENT]
            dpre_ref[pl.ds(s, SEGMENT), :] = full[u * SEGMENT : (u + 1) * SEGMENT]
        full_t = full.T.astype(jnp.bfloat16)
        total[:, : looped * chans] += dot(full_t, wide[...], NN)
        total[:, looped * chans :] += dot(full_t, columns[...], NT)
        return carry

    lax.fori_loop(0, voxels // block, block_step, 0)
    for k in range(offsets):
        conv_ref[k * chans : (k + 1) * chans, :] = total[:, k * chans : (k + 1) * chans].T


def forward(map_flat, sparse, features, incoming, weights, class_t, label_blocks, classes, reduce_rows, table_rows):
    voxels, chans = features.shape
    offsets = weights.shape[0] // chans
    looped = offsets - BY_MATMUL
    stream = voxels // STREAMS
    block = STREAMS * SEGMENT
    filled = voxels + sum(halo.shape[0] for halo in incoming)
    return pl.pallas_call(
        functools.partial(forward_kernel, classes),
        out_shape=(
            jax.ShapeDtypeStruct((voxels, chans), jnp.float32),
            jax.ShapeDtypeStruct((voxels, chans), jnp.float32),
            jax.ShapeDtypeStruct((reduce_rows, chans), jnp.float32),
            jax.ShapeDtypeStruct(weights.shape, jnp.bfloat16),
        ),
        in_specs=[HBM, VMEM, VMEM, [VMEM] * 4, VMEM, VMEM, VMEM],
        out_specs=(VMEM, VMEM, VMEM, VMEM),
        scratch_shapes=[
            pltpu.VMEM((table_rows, chans), jnp.float32),
            pltpu.VMEM((chans, filled), jnp.bfloat16),
            pltpu.VMEM((looped, block, chans), jnp.float32),
            pltpu.VMEM((block, looped * chans), jnp.bfloat16),
            pltpu.VMEM((BY_MATMUL * chans, block), jnp.bfloat16),
            pltpu.VMEM((chans, BY_MATMUL * chans), jnp.bfloat16),
            pltpu.VMEM((chans, offsets * chans), jnp.float32),
            pltpu.SemaphoreType.DMA((2, looped * STREAMS)),
        ]
        + [pltpu.SMEM((stream,), jnp.int32)] * (looped * STREAMS),
        compiler_params=pltpu.CompilerParams(vmem_limit_bytes=40 << 20),
        cost_estimate=pl.CostEstimate(
            flops=4 * voxels * offsets * chans * chans, bytes_accessed=150 << 20, transcendentals=0
        ),
        name="forward",
    )(map_flat, sparse, features, incoming, weights, class_t, label_blocks)


def scatter_kernel(first, offsets, has_before, map_hbm, dpre_ref, weight_ref, *refs):
    refs = list(refs)
    before = refs.pop(0) if has_before else None
    out_ref, sems = refs[0], refs[1]
    tables = refs[2 : 2 + offsets]
    index = refs[2 + offsets :]
    voxels, chans = dpre_ref.shape
    stream = voxels // SCATTER_STREAMS
    ready, later = fetch(map_hbm, index, sems, first * SCATTER_STREAMS, stream, (0, 128, stream))
    for table in tables:
        table[...] = jnp.zeros_like(table)
    for copy in ready:
        copy.wait()

    def step(i, carry):
        for u in range(SCATTER_STREAMS):
            row = dpre_ref[pl.ds(u * stream + i, 1), :]
            for k in range(offsets):
                at = pl.ds(index[k * SCATTER_STREAMS + u][i], 1)
                tables[k][at, :] = tables[k][at, :] + row
        return carry

    lax.fori_loop(0, 128, step, 0)
    for copy in later:
        copy.wait()
    lax.fori_loop(128, stream, step, 0)
    tiles = 3
    height = out_ref.shape[0] // tiles

    def finish(t, carry):
        at = pl.ds(pl.multiple_of(t * height, 16), height)
        wide = jnp.concatenate([table[at, :].astype(jnp.bfloat16) for table in tables], axis=1)
        result = dot(wide, weight_ref[first * chans : (first + offsets) * chans, :], NN)
        out_ref[at, :] = result + before[at, :] if has_before else result
        return carry

    lax.fori_loop(0, tiles, finish, 0)


def scatter(map_flat, dpre, flipped, before, first, offsets, table_rows):
    voxels, chans = dpre.shape
    stream = voxels // SCATTER_STREAMS
    has_before = before is not None
    return pl.pallas_call(
        functools.partial(scatter_kernel, first, offsets, has_before),
        out_shape=jax.ShapeDtypeStruct((table_rows, chans), jnp.float32),
        in_specs=[HBM, VMEM, VMEM] + ([VMEM] if has_before else []),
        out_specs=VMEM,
        scratch_shapes=[pltpu.SemaphoreType.DMA((2, offsets * SCATTER_STREAMS))]
        + [pltpu.VMEM((table_rows, chans), jnp.float32)] * offsets
        + [pltpu.SMEM((stream,), jnp.int32)] * (offsets * SCATTER_STREAMS),
        compiler_params=pltpu.CompilerParams(vmem_limit_bytes=40 << 20),
        cost_estimate=pl.CostEstimate(
            flops=2 * voxels * offsets * chans * chans, bytes_accessed=40 << 20, transcendentals=0
        ),
        name=f"scatter_{first}",
    )(map_flat, dpre, flipped, *([before] if has_before else []))


def finish_kernel(dmixed_ref, dext_ref, send_ref, back_ref, out_ref):
    voxels, chans = out_ref.shape
    height = voxels // 8

    def step(t, carry):
        at = pl.ds(pl.multiple_of(t * height, height), height)
        row = lax.broadcasted_iota(jnp.int32, (height, send_ref.shape[1]), 0) + t * height
        chosen = (row == send_ref[...]).astype(jnp.float32).astype(jnp.bfloat16)
        out_ref[at, :] = dmixed_ref[at, :] + dext_ref[at, :] + dot(chosen, back_ref[...], NN)
        return carry

    lax.fori_loop(0, voxels // height, step, 0)


def finish(dmixed, dext, send_flat, back):
    return pl.pallas_call(
        finish_kernel,
        out_shape=jax.ShapeDtypeStruct(dmixed.shape, jnp.float32),
        in_specs=[VMEM] * 4,
        out_specs=VMEM,
        compiler_params=pltpu.CompilerParams(vmem_limit_bytes=40 << 20),
        cost_estimate=pl.CostEstimate(flops=1 << 28, bytes_accessed=4 << 20, transcendentals=0),
        name="finish",
    )(dmixed, dext, send_flat, back)


def exchange(shard, axis, distance):
    devices = lax.axis_size(axis)
    return lax.ppermute(shard, axis, [(i, i ^ distance) for i in range(devices)])


def swap_edges(down, up, axis):
    devices = lax.axis_size(axis)
    odd = (lax.axis_index(axis) & 1) != 0
    even_pairs = [(i, i ^ 1) for i in range(devices) if (i ^ 1) < devices]
    odd_pairs = [(i, ((i + 1) ^ 1) - 1) for i in range(1, devices) if ((i + 1) ^ 1) - 1 < devices]
    first = lax.ppermute(jnp.where(odd, down, up), axis, even_pairs)
    if odd_pairs:
        second = lax.ppermute(jnp.where(odd, up, down), axis, odd_pairs)
    else:
        second = jnp.zeros_like(first)
    return jnp.where(odd, first, second), jnp.where(odd, second, first)


def on_device(features, conv_weight, classifier, send_rows, neighbour_map, labels):
    voxels, chans = features.shape
    width = send_rows.shape[1]
    offsets = conv_weight.shape[0]
    classes = classifier.shape[1]
    block = STREAMS * SEGMENT
    table_rows = -(-(voxels + GAP + 4 * width) // 48) * 48
    reduce_rows = -(-(offsets * chans + HEAD_ROWS) // 64) * 64

    outgoing = jnp.where(
        (send_rows < voxels)[..., None], features[jnp.minimum(send_rows, voxels - 1)], 0
    )
    low_y, high_y = swap_edges(outgoing[3], outgoing[2], "ty")
    low_x, high_x = swap_edges(outgoing[1], outgoing[0], "tx")

    zero_row = voxels + 4 * width
    moved = jnp.where(neighbour_map > voxels, neighbour_map - 1, neighbour_map)
    moved = jnp.where(neighbour_map == voxels, zero_row, moved)
    map_flat = moved.reshape(-1)
    sparse = (
        moved[offsets - BY_MATMUL :].reshape(BY_MATMUL, STREAMS, voxels // block, SEGMENT)
        .transpose(2, 0, 1, 3).reshape(voxels // block, BY_MATMUL, block)
    )
    weights = conv_weight.reshape(offsets * chans, chans)
    class_t = jnp.pad(classifier.T, ((0, HEAD_ROWS - classes), (0, 0)))
    label_blocks = (
        labels.reshape(STREAMS, voxels // block, SEGMENT).transpose(1, 0, 2)
        .reshape(voxels // block, 1, block)
    )
    dpre, dmixed, part, flipped = forward(
        map_flat, sparse, features, [low_x, high_x, low_y, high_y], weights, class_t, label_blocks,
        classes, reduce_rows, table_rows,
    )

    chunks = [
        (c * offsets // CHUNKS, (c + 1) * offsets // CHUNKS) for c in range(CHUNKS)
    ]
    dext = None

    def scatter_beside(sent, before):
        if not chunks:
            return sent, before
        first, last = chunks.pop(0)
        held = (sent, dpre) if before is None else (sent, dpre, before)
        held = lax.optimization_barrier(held)
        return held[0], scatter(
            map_flat, held[1], flipped, None if before is None else held[2],
            first, last - first, table_rows,
        )

    halved = []
    for axis, kind in (("rep", jnp.float32), ("ty", jnp.bfloat16)):
        distance = lax.axis_size(axis) // 2
        while distance:
            halved.append((axis, distance))
            upper = (lax.axis_index(axis) & distance) != 0
            half = part.shape[0] // 2
            low, high = part[:half], part[half:]
            sent = jnp.where(upper, low, high).astype(kind)
            if axis != "rep":
                sent, dext = scatter_beside(sent, dext)
            got = exchange(sent, axis, distance)
            if dext is not None:
                got, dext = lax.optimization_barrier((got, dext))
            part = jnp.where(upper, high, low) + got.astype(jnp.float32)
            distance //= 2
    distance = lax.axis_size("tx") // 2
    kind = jnp.bfloat16
    while distance:
        sent, dext = scatter_beside(part.astype(kind), dext)
        got, dext = lax.optimization_barrier((exchange(sent, "tx", distance), dext))
        part = sent.astype(jnp.float32) + got.astype(jnp.float32)
        distance //= 2
        kind = jnp.float32
    while chunks:
        part, dext = scatter_beside(part, dext)
    total = part.astype(jnp.bfloat16)
    for axis, distance in reversed(halved):
        upper = (lax.axis_index(axis) & distance) != 0
        total_before, got = total, exchange(total, axis, distance)
        low, high = jnp.where(upper, got, total), jnp.where(upper, total, got)
        total = jnp.concatenate([low, high], axis=0)

    halo = dext[voxels : voxels + 4 * width].astype(jnp.bfloat16).reshape(4, width, chans)
    back_3, back_2 = swap_edges(halo[2], halo[3], "ty")
    back_1, back_0 = swap_edges(halo[0], halo[1], "tx")
    back = jnp.concatenate([back_0, back_1, back_2, back_3], axis=0)
    grad_input = finish(dmixed, dext, send_rows.reshape(1, -1), back)

    count = voxels * lax.axis_size("tx") * lax.axis_size("ty") * lax.axis_size("rep")
    scale = 1.0 / math.sqrt(count)
    split = offsets * chans - low.shape[0]
    grad_conv = jnp.concatenate([low, high[:split]], axis=0).astype(jnp.float32) * scale
    grad_conv = grad_conv.reshape(offsets, chans, chans)
    grad_head = jnp.where(
        upper, total_before[split : split + classes], got[split : split + classes]
    ).T.astype(jnp.float32) * scale
    return grad_input, grad_conv, grad_head


def solution(mesh):
    placed = (
        P(("groups", "tx", "ty", "rep"), None),
        P(),
        P(),
        P(("groups", "tx", "ty", "rep"), None),
        P(None, ("groups", "tx", "ty", "rep")),
        P(("groups", "tx", "ty", "rep")),
    )
    return jax.shard_map(
        on_device,
        mesh=mesh,
        in_specs=placed,
        out_specs=(
            P(("groups", "tx", "ty", "rep"), None),
            P("groups", None, None),
            P("groups", None),
        ),
        check_vma=False,
    )
```

```python
import functools
import math

import jax
import jax.numpy as jnp
from jax import lax
from jax.experimental import pallas as pl
from jax.experimental.pallas import tpu as pltpu
from jax.sharding import PartitionSpec as P

STREAMS = 1
SCATTER_STREAMS = 2
SEGMENT = 256
BY_MATMUL = 8
SCATTER_STEPS = 64
FIRST_PART = 512
CHUNKS = 2
HEAD_ROWS = 32
VMEM = pl.BlockSpec(memory_space=pltpu.VMEM)
HBM = pl.BlockSpec(memory_space=pl.ANY)
NN = (((1,), (0,)), ((), ()))
NT = (((1,), (1,)), ((), ()))
TN = (((0,), (0,)), ((), ()))


def dot(a, b, dims):
    return lax.dot_general(a, b, dims, preferred_element_type=jnp.float32)


def fetch(map_hbm, index, sems, first, length, parts):
    stages = []
    for part, (start, stop) in enumerate(zip(parts[:-1], parts[1:])):
        stage = []
        for n, ref in enumerate(index):
            at = (first + n) * length + start
            stage.append(
                pltpu.make_async_copy(
                    map_hbm.at[pl.ds(at, stop - start)], ref.at[pl.ds(start, stop - start)],
                    sems.at[part, n],
                )
            )
        for copy in stage:
            copy.start()
        stages.append(stage)
    return stages


def forward_kernel(
    classes, map_hbm, sparse_ref, own_ref, halo_refs, weight_ref, class_ref, label_ref,
    dpre_ref, dmixed_ref, conv_ref, flipped_ref,
    table, turned, rows, wide, columns, side, total, sems, *index,
):
    voxels, chans = dpre_ref.shape
    looped = len(index) // STREAMS
    offsets = looped + BY_MATMUL
    stream = voxels // STREAMS
    block = STREAMS * SEGMENT
    share = SEGMENT // BY_MATMUL
    ready, later = fetch(map_hbm, index, sems, 0, stream, (0, FIRST_PART, stream))
    width = halo_refs[0].shape[0]
    table[:voxels, :] = own_ref[...].astype(jnp.float32)
    for n, halo in enumerate(halo_refs):
        start = voxels + n * width
        table[start : start + width, :] = halo[...].astype(jnp.float32)
    filled = voxels + 4 * width
    table[filled:, :] = jnp.zeros((table.shape[0] - filled, chans), jnp.float32)
    for n in range(filled // chans):
        at = slice(n * chans, (n + 1) * chans)
        turned[:, at] = table[at, :].T.astype(jnp.bfloat16)
    total[...] = jnp.zeros_like(total)
    conv_ref[pl.ds(offsets * chans, conv_ref.shape[0] - offsets * chans), :] = jnp.zeros(
        (conv_ref.shape[0] - offsets * chans, chans), jnp.float32
    )
    for k in range(offsets):
        at = slice(k * chans, (k + 1) * chans)
        turned_weight = weight_ref[at, :].T
        flipped_ref[at, :] = turned_weight
        if k >= looped:
            side[:, (k - looped) * chans : (k - looped + 1) * chans] = turned_weight
    for copy in ready:
        copy.wait()

    def block_step(b, carry):
        @pl.when(b == FIRST_PART // SEGMENT)
        def _():
            for copy in later:
                copy.wait()

        def gather_step(j, carry):
            row = lax.broadcasted_iota(jnp.int32, (filled, block), 0)
            chosen = (row == sparse_ref[b, pl.ds(j, 1), :]).astype(jnp.float32)
            at = pl.ds(pl.multiple_of(j * chans, chans), chans)
            columns[at, :] = dot(turned[...], chosen.astype(jnp.bfloat16), NN).astype(jnp.bfloat16)
            for n in range(share):
                to = j * share + n
                i = b * SEGMENT + to
                for u in range(STREAMS):
                    for k in range(looped):
                        rows[k, pl.ds(u * SEGMENT + to, 1), :] = table[
                            pl.ds(index[k * STREAMS + u][i], 1), :
                        ]
            return carry

        lax.fori_loop(0, BY_MATMUL, gather_step, 0)
        for k in range(looped):
            wide[:, k * chans : (k + 1) * chans] = rows[k].astype(jnp.bfloat16)
        pre = dot(wide[...], weight_ref[: looped * chans, :], NN)
        pre = pre + dot(side[...], columns[...], NN).T
        starts = [pl.multiple_of(u * stream + b * SEGMENT, SEGMENT) for u in range(STREAMS)]
        own = jnp.concatenate([table[pl.ds(s, SEGMENT), :] for s in starts], axis=0)
        sig = jax.nn.sigmoid(pre)
        mixed = (own + pre * sig).astype(jnp.bfloat16)
        logits = dot(class_ref[...], mixed, NT)
        which = lax.broadcasted_iota(jnp.int32, logits.shape, 0)
        logits = jnp.where(which < classes, logits, -1e30)
        high = jnp.max(logits, axis=0, keepdims=True)
        expd = jnp.exp(logits - high)
        probs = expd / jnp.sum(expd, axis=0, keepdims=True)
        onehot = (which == label_ref[b]).astype(jnp.float32)
        dlogits = (probs - onehot).astype(jnp.bfloat16)
        conv_ref[pl.ds(offsets * chans, HEAD_ROWS), :] += dot(dlogits, mixed, NN)
        dmixed = dot(dlogits, class_ref[...], TN)
        dpre = (dmixed * sig * (1.0 + pre * (1.0 - sig))).astype(jnp.bfloat16)
        full = dpre.astype(jnp.float32)
        for u, s in enumerate(starts):
            dmixed_ref[pl.ds(s, SEGMENT), :] = dmixed[u * SEGMENT : (u + 1) * SEGMENT]
            dpre_ref[pl.ds(s, SEGMENT), :] = full[u * SEGMENT : (u + 1) * SEGMENT]
        full_t = full.T.astype(jnp.bfloat16)
        total[:, : looped * chans] += dot(full_t, wide[...], NN)
        total[:, looped * chans :] += dot(full_t, columns[...], NT)
        return carry

    lax.fori_loop(0, voxels // block, block_step, 0)
    for k in range(offsets):
        conv_ref[k * chans : (k + 1) * chans, :] = total[:, k * chans : (k + 1) * chans].T


def forward(map_flat, sparse, features, incoming, weights, class_t, label_blocks, classes, reduce_rows, table_rows):
    voxels, chans = features.shape
    offsets = weights.shape[0] // chans
    looped = offsets - BY_MATMUL
    stream = voxels // STREAMS
    block = STREAMS * SEGMENT
    filled = voxels + sum(halo.shape[0] for halo in incoming)
    return pl.pallas_call(
        functools.partial(forward_kernel, classes),
        out_shape=(
            jax.ShapeDtypeStruct((voxels, chans), jnp.float32),
            jax.ShapeDtypeStruct((voxels, chans), jnp.float32),
            jax.ShapeDtypeStruct((reduce_rows, chans), jnp.float32),
            jax.ShapeDtypeStruct(weights.shape, jnp.bfloat16),
        ),
        in_specs=[HBM, VMEM, VMEM, [VMEM] * 4, VMEM, VMEM, VMEM],
        out_specs=(VMEM, VMEM, VMEM, VMEM),
        scratch_shapes=[
            pltpu.VMEM((table_rows, chans), jnp.float32),
            pltpu.VMEM((chans, filled), jnp.bfloat16),
            pltpu.VMEM((looped, block, chans), jnp.float32),
            pltpu.VMEM((block, looped * chans), jnp.bfloat16),
            pltpu.VMEM((BY_MATMUL * chans, block), jnp.bfloat16),
            pltpu.VMEM((chans, BY_MATMUL * chans), jnp.bfloat16),
            pltpu.VMEM((chans, offsets * chans), jnp.float32),
            pltpu.SemaphoreType.DMA((2, looped * STREAMS)),
        ]
        + [pltpu.SMEM((stream,), jnp.int32)] * (looped * STREAMS),
        compiler_params=pltpu.CompilerParams(vmem_limit_bytes=40 << 20),
        cost_estimate=pl.CostEstimate(
            flops=4 * voxels * offsets * chans * chans, bytes_accessed=150 << 20, transcendentals=0
        ),
        name="forward",
    )(map_flat, sparse, features, incoming, weights, class_t, label_blocks)


def scatter_kernel(first, offsets, has_before, map_hbm, dpre_ref, weight_ref, *refs):
    refs = list(refs)
    before = refs.pop(0) if has_before else None
    out_ref, sems = refs[:2]
    tables = refs[2 : 2 + offsets]
    index = refs[2 + offsets :]
    streams, stream, chans = dpre_ref.shape
    share = stream // SCATTER_STEPS
    copies, = fetch(map_hbm, index, sems, first * streams, stream, (0, stream))
    for table in tables:
        table[...] = jnp.zeros_like(table)
    for copy in copies:
        copy.wait()

    def step(j, carry):
        for n in range(share):
            i = j * share + n
            for u in range(streams):
                value = dpre_ref[u, pl.ds(i, 1), :]
                for k in range(offsets):
                    where = pl.ds(index[k * streams + u][i], 1)
                    tables[k][where, :] = tables[k][where, :] + value
        return carry

    lax.fori_loop(0, SCATTER_STEPS, step, 0)
    tiles = 3
    height = out_ref.shape[0] // tiles

    def finish(t, carry):
        at = pl.ds(pl.multiple_of(t * height, 16), height)
        wide = jnp.concatenate([table[at, :].astype(jnp.bfloat16) for table in tables], axis=1)
        result = dot(wide, weight_ref[first * chans : (first + offsets) * chans, :], NN)
        out_ref[at, :] = result + before[at, :] if has_before else result
        return carry

    lax.fori_loop(0, tiles, finish, 0)


def scatter(map_flat, dpre, flipped, before, first, offsets, table_rows):
    voxels, chans = dpre.shape
    stream = voxels // SCATTER_STREAMS
    has_before = before is not None
    return pl.pallas_call(
        functools.partial(scatter_kernel, first, offsets, has_before),
        out_shape=jax.ShapeDtypeStruct((table_rows, chans), jnp.float32),
        in_specs=[HBM, VMEM, VMEM] + ([VMEM] if has_before else []),
        out_specs=VMEM,
        scratch_shapes=[
            pltpu.SemaphoreType.DMA((1, offsets * SCATTER_STREAMS)),
        ]
        + [pltpu.VMEM((table_rows, chans), jnp.float32)] * offsets
        + [pltpu.SMEM((stream,), jnp.int32)] * (offsets * SCATTER_STREAMS),
        compiler_params=pltpu.CompilerParams(vmem_limit_bytes=40 << 20),
        cost_estimate=pl.CostEstimate(
            flops=2 * voxels * offsets * chans * chans, bytes_accessed=40 << 20, transcendentals=0
        ),
        name=f"scatter_{first}",
    )(
        map_flat, dpre.reshape(SCATTER_STREAMS, stream, chans), flipped,
        *([before] if has_before else []),
    )


def finish_kernel(dmixed_ref, dext_ref, send_ref, back_ref, out_ref):
    voxels, chans = out_ref.shape
    height = voxels // 8

    def step(t, carry):
        at = pl.ds(pl.multiple_of(t * height, height), height)
        row = lax.broadcasted_iota(jnp.int32, (height, send_ref.shape[1]), 0) + t * height
        chosen = (row == send_ref[...]).astype(jnp.float32).astype(jnp.bfloat16)
        out_ref[at, :] = dmixed_ref[at, :] + dext_ref[at, :] + dot(chosen, back_ref[...], NN)
        return carry

    lax.fori_loop(0, voxels // height, step, 0)


def finish(dmixed, dext, send_flat, back):
    return pl.pallas_call(
        finish_kernel,
        out_shape=jax.ShapeDtypeStruct(dmixed.shape, jnp.float32),
        in_specs=[VMEM] * 4,
        out_specs=VMEM,
        compiler_params=pltpu.CompilerParams(vmem_limit_bytes=40 << 20),
        cost_estimate=pl.CostEstimate(flops=1 << 28, bytes_accessed=4 << 20, transcendentals=0),
        name="finish",
    )(dmixed, dext, send_flat, back)


def outgoing_kernel(axes, send_ref, own_ref, *refs):
    *out_refs, table, sent = refs
    voxels, chans = own_ref.shape
    width = send_ref.shape[1]
    table[:voxels, :] = own_ref[...].astype(jnp.float32)
    table[voxels:, :] = jnp.zeros((table.shape[0] - voxels, chans), jnp.float32)
    for s in range(4):

        def step(t, carry, s=s):
            for n in range(32):
                i = t * 32 + n
                sent[pl.ds(s * width + i, 1), :] = table[pl.ds(send_ref[s, i], 1), :]
            return carry

        lax.fori_loop(0, width // 32, step, 0)
    lists = [sent[s * width : (s + 1) * width, :] for s in range(4)]
    picked = []
    for axis, (up, down) in zip(axes, ((2, 3), (0, 1))):
        odd = (lax.axis_index(axis) & 1) != 0
        picked.append(jnp.where(odd, lists[down], lists[up]))
        picked.append(jnp.where(odd, lists[up], lists[down]))
    for out_ref, value in zip(out_refs, picked):
        out_ref[...] = value.astype(jnp.bfloat16)


def outgoing(send_rows, features):
    voxels, chans = features.shape
    width = send_rows.shape[1]
    return pl.pallas_call(
        functools.partial(outgoing_kernel, ("ty", "tx")),
        out_shape=[jax.ShapeDtypeStruct((width, chans), jnp.bfloat16)] * 4,
        in_specs=[pl.BlockSpec(memory_space=pltpu.SMEM), VMEM],
        out_specs=[VMEM] * 4,
        scratch_shapes=[
            pltpu.VMEM((voxels + 8, chans), jnp.float32),
            pltpu.VMEM((4 * width, chans), jnp.float32),
        ],
        compiler_params=pltpu.CompilerParams(vmem_limit_bytes=16 << 20),
        name="outgoing",
    )(send_rows, features)


def assemble_kernel(axes, scale, conv_rows, *refs):
    *piece_refs, conv_ref, head_ref = refs
    pieces = len(piece_refs)
    height = piece_refs[0].shape[0]
    mine = group_index(axes)
    for d, piece_ref in enumerate(piece_refs):
        for p in range(pieces):

            @pl.when((mine ^ d) == p)
            def _(p=p, piece_ref=piece_ref):
                start = p * height
                inside = max(0, min(height, conv_rows - start))
                if inside:
                    value = piece_ref[:inside, :].astype(jnp.float32) * scale
                    conv_ref[start : start + inside, :] = value
                if start <= conv_rows < start + height:
                    at = conv_rows - start
                    value = piece_ref[at : at + HEAD_ROWS, :].astype(jnp.float32) * scale
                    head_ref[...] = value


def assemble(pieces, axes, scale, conv_rows):
    chans = pieces[0].shape[1]
    return pl.pallas_call(
        functools.partial(assemble_kernel, axes, scale, conv_rows),
        out_shape=(
            jax.ShapeDtypeStruct((conv_rows, chans), jnp.float32),
            jax.ShapeDtypeStruct((HEAD_ROWS, chans), jnp.float32),
        ),
        in_specs=[VMEM] * len(pieces),
        out_specs=(VMEM, VMEM),
        compiler_params=pltpu.CompilerParams(vmem_limit_bytes=16 << 20),
        name="assemble",
    )(*pieces)


def group_index(axes):
    at = 0
    for axis in axes:
        at = at * lax.axis_size(axis) + lax.axis_index(axis)
    return at


def group_size(axes):
    return math.prod(lax.axis_size(axis) for axis in axes)


def exchange(shard, axes, distance):
    return lax.ppermute(shard, axes, [(i, i ^ distance) for i in range(group_size(axes))])


def edge_pairs(axis):
    devices = lax.axis_size(axis)
    even = [(i, i ^ 1) for i in range(devices) if (i ^ 1) < devices]
    odd = [(i, ((i + 1) ^ 1) - 1) for i in range(1, devices) if ((i + 1) ^ 1) - 1 < devices]
    return even, odd


def swap_edges(over_even, over_odd, axis):
    even_pairs, odd_pairs = edge_pairs(axis)
    odd = (lax.axis_index(axis) & 1) != 0
    first = lax.ppermute(over_even, axis, even_pairs)
    if odd_pairs:
        second = lax.ppermute(over_odd, axis, odd_pairs)
    else:
        second = jnp.zeros_like(first)
    return jnp.where(odd, first, second), jnp.where(odd, second, first)


def by_parity(down, up, axis):
    odd = (lax.axis_index(axis) & 1) != 0
    return jnp.where(odd, down, up), jnp.where(odd, up, down)


def on_device(features, conv_weight, classifier, send_rows, neighbour_map, labels):
    voxels, chans = features.shape
    width = send_rows.shape[1]
    offsets = conv_weight.shape[0]
    classes = classifier.shape[1]
    block = STREAMS * SEGMENT
    table_rows = -(-(voxels + 4 * width + 1) // 48) * 48
    square = ("ty", "rep")
    pieces = group_size(square)
    unit = 16 * pieces
    reduce_rows = -(-(offsets * chans + HEAD_ROWS) // unit) * unit
    height = reduce_rows // pieces

    even_y, odd_y, even_x, odd_x = outgoing(send_rows, features)
    low_y, high_y = swap_edges(even_y, odd_y, "ty")
    low_x, high_x = swap_edges(even_x, odd_x, "tx")

    zero_row = voxels + 4 * width
    moved = jnp.where(neighbour_map > voxels, neighbour_map - 1, neighbour_map)
    moved = jnp.where(neighbour_map == voxels, zero_row, moved)
    map_flat = moved.reshape(-1)
    sparse = (
        moved[offsets - BY_MATMUL :].reshape(BY_MATMUL, STREAMS, voxels // block, SEGMENT)
        .transpose(2, 0, 1, 3).reshape(voxels // block, BY_MATMUL, block)
    )
    weights = conv_weight.reshape(offsets * chans, chans)
    class_t = jnp.pad(classifier.T, ((0, HEAD_ROWS - classes), (0, 0)))
    label_blocks = (
        labels.reshape(STREAMS, voxels // block, SEGMENT).transpose(1, 0, 2)
        .reshape(voxels // block, 1, block)
    )
    dpre, dmixed, part, flipped = forward(
        map_flat, sparse, features, [low_x, high_x, low_y, high_y], weights, class_t, label_blocks,
        classes, reduce_rows, table_rows,
    )

    chunks = [(c * offsets // CHUNKS, (c + 1) * offsets // CHUNKS) for c in range(CHUNKS)]

    def scatter_beside(sent, before):
        first, last = chunks.pop(0)
        held = (sent, dpre) if before is None else (sent, dpre, before)
        held = lax.optimization_barrier(held)
        return held[0], scatter(
            map_flat, held[1], flipped, None if before is None else held[2],
            first, last - first, table_rows,
        )

    mine = group_index(square)
    sent = []
    for d in range(1, pieces):
        piece = lax.dynamic_slice_in_dim(part, (mine ^ d) * height, height, axis=0)
        sent.append(piece.astype(jnp.bfloat16))
    own = lax.dynamic_slice_in_dim(part, mine * height, height, axis=0)
    sent, dext = scatter_beside(sent, None)
    got = [exchange(piece, square, d + 1) for d, piece in enumerate(sent)]
    got, dext = lax.optimization_barrier((got, dext))
    own = own + sum(piece.astype(jnp.float32) for piece in got)

    stride = 1
    while stride < lax.axis_size("tx"):
        radix = min(4, lax.axis_size("tx") // stride)
        own = own.astype(jnp.bfloat16)
        if chunks:
            own, dext = scatter_beside(own, dext)
        got = [own] + [exchange(own, ("tx",), m * stride) for m in range(1, radix)]
        got, dext = lax.optimization_barrier((got, dext))
        got = [piece.astype(jnp.float32) for piece in got]
        while len(got) > 1:
            got = [a + b for a, b in zip(got[::2], got[1::2])]
        own = got[0]
        stride *= radix
    while chunks:
        own, dext = scatter_beside(own, dext)

    halo = dext[voxels : voxels + 4 * width].astype(jnp.bfloat16).reshape(4, width, chans)
    back_3, back_2 = swap_edges(*by_parity(halo[2], halo[3], "ty"), "ty")
    back_1, back_0 = swap_edges(*by_parity(halo[0], halo[1], "tx"), "tx")
    back = jnp.concatenate([back_0, back_1, back_2, back_3], axis=0)
    grad_input = finish(dmixed, dext, send_rows.reshape(1, -1), back)

    own = own.astype(jnp.bfloat16)
    everywhere = [own] + [exchange(own, square, d) for d in range(1, pieces)]
    count = voxels * lax.axis_size("tx") * lax.axis_size("ty") * lax.axis_size("rep")
    conv, head = assemble(everywhere, square, 1.0 / math.sqrt(count), offsets * chans)
    return grad_input, conv.reshape(offsets, chans, chans), head[:classes].T


def solution(mesh):
    placed = (
        P(("groups", "tx", "ty", "rep"), None),
        P(),
        P(),
        P(("groups", "tx", "ty", "rep"), None),
        P(None, ("groups", "tx", "ty", "rep")),
        P(("groups", "tx", "ty", "rep")),
    )
    return jax.shard_map(
        on_device,
        mesh=mesh,
        in_specs=placed,
        out_specs=(
            P(("groups", "tx", "ty", "rep"), None),
            P("groups", None, None),
            P("groups", None),
        ),
        check_vma=False,
    )
```

```python
import functools
import math

import jax
import jax.numpy as jnp
from jax import lax
from jax.experimental import pallas as pl
from jax.experimental.pallas import tpu as pltpu
from jax.sharding import PartitionSpec as P

STREAMS = 1
SCATTER_STREAMS = 2
SEGMENT = 256
BY_MATMUL = 8
SCATTER_STEPS = 64
FIRST_PART = 512
CHUNKS = 2
HEAD_ROWS = 32
VMEM = pl.BlockSpec(memory_space=pltpu.VMEM)
HBM = pl.BlockSpec(memory_space=pl.ANY)
NN = (((1,), (0,)), ((), ()))
NT = (((1,), (1,)), ((), ()))
TN = (((0,), (0,)), ((), ()))


def dot(a, b, dims):
    return lax.dot_general(a, b, dims, preferred_element_type=jnp.float32)


def from_neighbours(refs, axis):
    odd = (lax.axis_index(axis) & 1) != 0
    first = refs[0][...].astype(jnp.float32)
    second = refs[1][...].astype(jnp.float32) if len(refs) > 1 else jnp.zeros_like(first)
    return jnp.where(odd, first, second), jnp.where(odd, second, first)


def over_edges(down, up, axis):
    odd = (lax.axis_index(axis) & 1) != 0
    return jnp.where(odd, down, up), jnp.where(odd, up, down)


def fetch(map_hbm, index, sems, first, length, parts):
    stages = []
    for part, (start, stop) in enumerate(zip(parts[:-1], parts[1:])):
        stage = []
        for n, ref in enumerate(index):
            at = (first + n) * length + start
            stage.append(
                pltpu.make_async_copy(
                    map_hbm.at[pl.ds(at, stop - start)], ref.at[pl.ds(start, stop - start)],
                    sems.at[part, n],
                )
            )
        for copy in stage:
            copy.start()
        stages.append(stage)
    return stages


def forward_kernel(
    classes, map_hbm, sparse_ref, own_hbm, x_refs, y_refs, weight_hbm, class_ref, label_ref,
    dpre_ref, dmixed_ref, conv_ref, flipped_ref,
    own_ref, weight_ref, load_sems, table, turned, rows, wide, columns, side, total, sems, *index,
):
    voxels, chans = dpre_ref.shape
    looped = len(index) // STREAMS
    offsets = looped + BY_MATMUL
    stream = voxels // STREAMS
    block = STREAMS * SEGMENT
    share = SEGMENT // BY_MATMUL
    own_copy = pltpu.make_async_copy(own_hbm, own_ref, load_sems.at[0])
    own_copy.start()
    weight_copy = pltpu.make_async_copy(weight_hbm, weight_ref, load_sems.at[1])
    weight_copy.start()
    ready, later = fetch(map_hbm, index, sems, 0, stream, (0, FIRST_PART, stream))
    own_copy.wait()
    width = x_refs[0].shape[0]
    table[:voxels, :] = own_ref[...].astype(jnp.float32)
    halos = from_neighbours(x_refs, "tx") + from_neighbours(y_refs, "ty")
    for n, halo in enumerate(halos):
        start = voxels + n * width
        table[start : start + width, :] = halo
    filled = voxels + 4 * width
    table[filled:, :] = jnp.zeros((table.shape[0] - filled, chans), jnp.float32)
    for n in range(filled // chans):
        at = slice(n * chans, (n + 1) * chans)
        turned[:, at] = table[at, :].T.astype(jnp.bfloat16)
    total[...] = jnp.zeros_like(total)
    conv_ref[pl.ds(offsets * chans, conv_ref.shape[0] - offsets * chans), :] = jnp.zeros(
        (conv_ref.shape[0] - offsets * chans, chans), jnp.float32
    )
    weight_copy.wait()
    for k in range(offsets):
        at = slice(k * chans, (k + 1) * chans)
        turned_weight = weight_ref[at, :].T
        flipped_ref[at, :] = turned_weight
        if k >= looped:
            side[:, (k - looped) * chans : (k - looped + 1) * chans] = turned_weight
    for copy in ready:
        copy.wait()

    def block_step(b, carry):
        @pl.when(b == FIRST_PART // SEGMENT)
        def _():
            for copy in later:
                copy.wait()

        def gather_step(j, carry):
            row = lax.broadcasted_iota(jnp.int32, (filled, block), 0)
            chosen = (row == sparse_ref[b, pl.ds(j, 1), :]).astype(jnp.float32)
            at = pl.ds(pl.multiple_of(j * chans, chans), chans)
            columns[at, :] = dot(turned[...], chosen.astype(jnp.bfloat16), NN).astype(jnp.bfloat16)
            for n in range(share):
                to = j * share + n
                i = b * SEGMENT + to
                for u in range(STREAMS):
                    for k in range(looped):
                        rows[k, pl.ds(u * SEGMENT + to, 1), :] = table[
                            pl.ds(index[k * STREAMS + u][i], 1), :
                        ]
            return carry

        lax.fori_loop(0, BY_MATMUL, gather_step, 0)
        for k in range(looped):
            wide[:, k * chans : (k + 1) * chans] = rows[k].astype(jnp.bfloat16)
        pre = dot(wide[...], weight_ref[: looped * chans, :], NN)
        pre = pre + dot(side[...], columns[...], NN).T
        starts = [pl.multiple_of(u * stream + b * SEGMENT, SEGMENT) for u in range(STREAMS)]
        own = jnp.concatenate([table[pl.ds(s, SEGMENT), :] for s in starts], axis=0)
        sig = jax.nn.sigmoid(pre)
        mixed = (own + pre * sig).astype(jnp.bfloat16)
        logits = dot(class_ref[...], mixed, NT)
        which = lax.broadcasted_iota(jnp.int32, logits.shape, 0)
        logits = jnp.where(which < classes, logits, -1e30)
        high = jnp.max(logits, axis=0, keepdims=True)
        expd = jnp.exp(logits - high)
        probs = expd / jnp.sum(expd, axis=0, keepdims=True)
        onehot = (which == label_ref[b]).astype(jnp.float32)
        dlogits = (probs - onehot).astype(jnp.bfloat16)
        conv_ref[pl.ds(offsets * chans, HEAD_ROWS), :] += dot(dlogits, mixed, NN)
        dmixed = dot(dlogits, class_ref[...], TN)
        dpre = (dmixed * sig * (1.0 + pre * (1.0 - sig))).astype(jnp.bfloat16)
        full = dpre.astype(jnp.float32)
        for u, s in enumerate(starts):
            dmixed_ref[pl.ds(s, SEGMENT), :] = dmixed[u * SEGMENT : (u + 1) * SEGMENT]
            dpre_ref[pl.ds(s, SEGMENT), :] = full[u * SEGMENT : (u + 1) * SEGMENT]
        full_t = full.T.astype(jnp.bfloat16)
        total[:, : looped * chans] += dot(full_t, wide[...], NN)
        total[:, looped * chans :] += dot(full_t, columns[...], NT)
        return carry

    lax.fori_loop(0, voxels // block, block_step, 0)
    for k in range(offsets):
        conv_ref[k * chans : (k + 1) * chans, :] = total[:, k * chans : (k + 1) * chans].T


def forward(map_flat, sparse, features, from_x, from_y, weights, class_t, label_blocks, classes, reduce_rows, table_rows):
    voxels, chans = features.shape
    offsets = weights.shape[0] // chans
    looped = offsets - BY_MATMUL
    stream = voxels // STREAMS
    block = STREAMS * SEGMENT
    filled = voxels + 4 * from_x[0].shape[0]
    return pl.pallas_call(
        functools.partial(forward_kernel, classes),
        out_shape=(
            jax.ShapeDtypeStruct((voxels, chans), jnp.float32),
            jax.ShapeDtypeStruct((voxels, chans), jnp.float32),
            jax.ShapeDtypeStruct((reduce_rows, chans), jnp.float32),
            jax.ShapeDtypeStruct(weights.shape, jnp.bfloat16),
        ),
        in_specs=[HBM, VMEM, HBM, [VMEM] * len(from_x), [VMEM] * len(from_y), HBM, VMEM, VMEM],
        out_specs=(VMEM, VMEM, VMEM, VMEM),
        scratch_shapes=[
            pltpu.VMEM(features.shape, jnp.bfloat16),
            pltpu.VMEM(weights.shape, jnp.bfloat16),
            pltpu.SemaphoreType.DMA((2,)),
            pltpu.VMEM((table_rows, chans), jnp.float32),
            pltpu.VMEM((chans, filled), jnp.bfloat16),
            pltpu.VMEM((looped, block, chans), jnp.float32),
            pltpu.VMEM((block, looped * chans), jnp.bfloat16),
            pltpu.VMEM((BY_MATMUL * chans, block), jnp.bfloat16),
            pltpu.VMEM((chans, BY_MATMUL * chans), jnp.bfloat16),
            pltpu.VMEM((chans, offsets * chans), jnp.float32),
            pltpu.SemaphoreType.DMA((2, looped * STREAMS)),
        ]
        + [pltpu.SMEM((stream,), jnp.int32)] * (looped * STREAMS),
        compiler_params=pltpu.CompilerParams(vmem_limit_bytes=20 << 20),
        cost_estimate=pl.CostEstimate(
            flops=4 * voxels * offsets * chans * chans, bytes_accessed=150 << 20, transcendentals=0
        ),
        name="forward",
    )(map_flat, sparse, features, from_x, from_y, weights, class_t, label_blocks)


def scatter_kernel(first, offsets, has_before, map_hbm, dpre_ref, weight_ref, *refs):
    refs = list(refs)
    before = refs.pop(0) if has_before else None
    out_ref = refs.pop(0)
    back_refs = [refs.pop(0) for _ in range(4)] if has_before else []
    sems = refs.pop(0)
    tables = refs[:offsets]
    index = refs[offsets:]
    streams, stream, chans = dpre_ref.shape
    share = stream // SCATTER_STEPS
    copies, = fetch(map_hbm, index, sems, first * streams, stream, (0, stream))
    for table in tables:
        table[...] = jnp.zeros_like(table)
    for copy in copies:
        copy.wait()

    def step(j, carry):
        for n in range(share):
            i = j * share + n
            for u in range(streams):
                value = dpre_ref[u, pl.ds(i, 1), :]
                for k in range(offsets):
                    where = pl.ds(index[k * streams + u][i], 1)
                    tables[k][where, :] = tables[k][where, :] + value
        return carry

    lax.fori_loop(0, SCATTER_STEPS, step, 0)
    tiles = 3
    height = out_ref.shape[0] // tiles

    def finish(t, carry):
        at = pl.ds(pl.multiple_of(t * height, 16), height)
        wide = jnp.concatenate([table[at, :].astype(jnp.bfloat16) for table in tables], axis=1)
        result = dot(wide, weight_ref[first * chans : (first + offsets) * chans, :], NN)
        out_ref[at, :] = result + before[at, :] if has_before else result
        return carry

    lax.fori_loop(0, tiles, finish, 0)
    if back_refs:
        width = back_refs[0].shape[0]
        voxels = streams * stream
        halos = [out_ref[voxels + n * width : voxels + (n + 1) * width, :] for n in range(4)]
        picked = over_edges(halos[2], halos[3], "ty") + over_edges(halos[0], halos[1], "tx")
        for back_ref, value in zip(back_refs, picked):
            back_ref[...] = value.astype(jnp.bfloat16)


def scatter(map_flat, dpre, flipped, before, first, offsets, table_rows, width):
    voxels, chans = dpre.shape
    stream = voxels // SCATTER_STREAMS
    has_before = before is not None
    return pl.pallas_call(
        functools.partial(scatter_kernel, first, offsets, has_before),
        out_shape=[jax.ShapeDtypeStruct((table_rows, chans), jnp.float32)]
        + [jax.ShapeDtypeStruct((width, chans), jnp.bfloat16)] * (4 if has_before else 0),
        in_specs=[HBM, VMEM, VMEM] + ([VMEM] if has_before else []),
        out_specs=[VMEM] * (5 if has_before else 1),
        scratch_shapes=[
            pltpu.SemaphoreType.DMA((1, offsets * SCATTER_STREAMS)),
        ]
        + [pltpu.VMEM((table_rows, chans), jnp.float32)] * offsets
        + [pltpu.SMEM((stream,), jnp.int32)] * (offsets * SCATTER_STREAMS),
        compiler_params=pltpu.CompilerParams(vmem_limit_bytes=28 << 20),
        cost_estimate=pl.CostEstimate(
            flops=2 * voxels * offsets * chans * chans, bytes_accessed=40 << 20, transcendentals=0
        ),
        name=f"scatter_{first}",
    )(
        map_flat, dpre.reshape(SCATTER_STREAMS, stream, chans), flipped,
        *([before] if has_before else []),
    )


def finish_kernel(dmixed_ref, dext_ref, send_ref, x_refs, y_refs, out_ref, back_ref):
    voxels, chans = out_ref.shape
    width = x_refs[0].shape[0]
    low_x, high_x = from_neighbours(x_refs, "tx")
    low_y, high_y = from_neighbours(y_refs, "ty")
    for n, value in enumerate((high_x, low_x, high_y, low_y)):
        back_ref[n * width : (n + 1) * width, :] = value.astype(jnp.bfloat16)
    height = voxels // 8

    def step(t, carry):
        at = pl.ds(pl.multiple_of(t * height, height), height)
        row = lax.broadcasted_iota(jnp.int32, (height, send_ref.shape[1]), 0) + t * height
        chosen = (row == send_ref[...]).astype(jnp.float32).astype(jnp.bfloat16)
        out_ref[at, :] = dmixed_ref[at, :] + dext_ref[at, :] + dot(chosen, back_ref[...], NN)
        return carry

    lax.fori_loop(0, voxels // height, step, 0)


def finish(dmixed, dext, send_flat, from_x, from_y):
    return pl.pallas_call(
        finish_kernel,
        out_shape=jax.ShapeDtypeStruct(dmixed.shape, jnp.float32),
        in_specs=[VMEM, VMEM, VMEM, [VMEM] * len(from_x), [VMEM] * len(from_y)],
        out_specs=VMEM,
        scratch_shapes=[pltpu.VMEM((send_flat.shape[1], dmixed.shape[1]), jnp.bfloat16)],
        compiler_params=pltpu.CompilerParams(vmem_limit_bytes=12 << 20),
        cost_estimate=pl.CostEstimate(flops=1 << 28, bytes_accessed=4 << 20, transcendentals=0),
        name="finish",
    )(dmixed, dext, send_flat, from_x, from_y)


def outgoing_kernel(axes, send_hbm, own_hbm, *refs):
    *out_refs, send_ref, own_ref, sems, table, sent = refs
    voxels, chans = own_ref.shape
    send_copy = pltpu.make_async_copy(send_hbm, send_ref, sems.at[0])
    send_copy.start()
    own_copy = pltpu.make_async_copy(own_hbm, own_ref, sems.at[1])
    own_copy.start()
    own_copy.wait()
    width = send_ref.shape[1]
    table[:voxels, :] = own_ref[...].astype(jnp.float32)
    table[voxels:, :] = jnp.zeros((table.shape[0] - voxels, chans), jnp.float32)
    send_copy.wait()
    for s in range(4):

        def step(t, carry, s=s):
            for n in range(32):
                i = t * 32 + n
                sent[pl.ds(s * width + i, 1), :] = table[pl.ds(send_ref[s, i], 1), :]
            return carry

        lax.fori_loop(0, width // 32, step, 0)
    lists = [sent[s * width : (s + 1) * width, :] for s in range(4)]
    picked = []
    for axis, (up, down) in zip(axes, ((2, 3), (0, 1))):
        picked.extend(over_edges(lists[down], lists[up], axis))
    for out_ref, value in zip(out_refs, picked):
        out_ref[...] = value.astype(jnp.bfloat16)


def outgoing(send_rows, features):
    voxels, chans = features.shape
    width = send_rows.shape[1]
    return pl.pallas_call(
        functools.partial(outgoing_kernel, ("ty", "tx")),
        out_shape=[jax.ShapeDtypeStruct((width, chans), jnp.bfloat16)] * 4,
        in_specs=[HBM, HBM],
        out_specs=[VMEM] * 4,
        scratch_shapes=[
            pltpu.SMEM(send_rows.shape, jnp.int32),
            pltpu.VMEM(features.shape, jnp.bfloat16),
            pltpu.SemaphoreType.DMA((2,)),
            pltpu.VMEM((voxels + 8, chans), jnp.float32),
            pltpu.VMEM((4 * width, chans), jnp.float32),
        ],
        compiler_params=pltpu.CompilerParams(vmem_limit_bytes=60 << 20),
        cost_estimate=pl.CostEstimate(flops=0, bytes_accessed=8 << 20, transcendentals=0),
        name="outgoing",
    )(send_rows, features)


def assemble_kernel(axes, scale, conv_rows, *refs):
    *piece_refs, conv_ref, head_ref = refs
    pieces = len(piece_refs)
    height = piece_refs[0].shape[0]
    mine = group_index(axes)
    for d, piece_ref in enumerate(piece_refs):
        for p in range(pieces):

            @pl.when((mine ^ d) == p)
            def _(p=p, piece_ref=piece_ref):
                start = p * height
                inside = max(0, min(height, conv_rows - start))
                if inside:
                    value = piece_ref[:inside, :].astype(jnp.float32) * scale
                    conv_ref[start : start + inside, :] = value
                if start <= conv_rows < start + height:
                    at = conv_rows - start
                    value = piece_ref[at : at + HEAD_ROWS, :].astype(jnp.float32) * scale
                    head_ref[...] = value[: head_ref.shape[0], :]


def assemble(pieces, axes, scale, conv_rows, classes):
    chans = pieces[0].shape[1]
    return pl.pallas_call(
        functools.partial(assemble_kernel, axes, scale, conv_rows),
        out_shape=(
            jax.ShapeDtypeStruct((conv_rows, chans), jnp.float32),
            jax.ShapeDtypeStruct((classes, chans), jnp.float32),
        ),
        in_specs=[VMEM] * len(pieces),
        out_specs=(VMEM, VMEM),
        compiler_params=pltpu.CompilerParams(vmem_limit_bytes=12 << 20),
        name="assemble",
    )(*pieces)


def group_index(axes):
    at = 0
    for axis in axes:
        at = at * lax.axis_size(axis) + lax.axis_index(axis)
    return at


def group_size(axes):
    return math.prod(lax.axis_size(axis) for axis in axes)


def exchange(shard, axes, distance):
    return lax.ppermute(shard, axes, [(i, i ^ distance) for i in range(group_size(axes))])


def edge_pairs(axis):
    devices = lax.axis_size(axis)
    even = [(i, i ^ 1) for i in range(devices) if (i ^ 1) < devices]
    odd = [(i, ((i + 1) ^ 1) - 1) for i in range(1, devices) if ((i + 1) ^ 1) - 1 < devices]
    return even, odd


def swap_edges(over_even, over_odd, axis):
    even_pairs, odd_pairs = edge_pairs(axis)
    got = [lax.ppermute(over_even, axis, even_pairs)]
    if odd_pairs:
        got.append(lax.ppermute(over_odd, axis, odd_pairs))
    return got


def on_device(features, conv_weight, classifier, send_rows, neighbour_map, labels):
    voxels, chans = features.shape
    width = send_rows.shape[1]
    offsets = conv_weight.shape[0]
    classes = classifier.shape[1]
    block = STREAMS * SEGMENT
    table_rows = -(-(voxels + 4 * width + 1) // 48) * 48
    square = ("ty", "rep")
    pieces = group_size(square)
    unit = 16 * pieces
    reduce_rows = -(-(offsets * chans + HEAD_ROWS) // unit) * unit
    height = reduce_rows // pieces

    even_y, odd_y, even_x, odd_x = outgoing(send_rows, features)
    from_y = swap_edges(even_y, odd_y, "ty")
    from_x = swap_edges(even_x, odd_x, "tx")

    zero_row = voxels + 4 * width
    moved = jnp.where(neighbour_map > voxels, neighbour_map - 1, neighbour_map)
    moved = jnp.where(neighbour_map == voxels, zero_row, moved)
    map_flat = moved.reshape(-1)
    sparse = (
        moved[offsets - BY_MATMUL :].reshape(BY_MATMUL, STREAMS, voxels // block, SEGMENT)
        .transpose(2, 0, 1, 3).reshape(voxels // block, BY_MATMUL, block)
    )
    weights = conv_weight.reshape(offsets * chans, chans)
    class_t = jnp.pad(classifier.T, ((0, HEAD_ROWS - classes), (0, 0)))
    label_blocks = (
        labels.reshape(STREAMS, voxels // block, SEGMENT).transpose(1, 0, 2)
        .reshape(voxels // block, 1, block)
    )
    dpre, dmixed, part, flipped = forward(
        map_flat, sparse, features, from_x, from_y, weights, class_t, label_blocks,
        classes, reduce_rows, table_rows,
    )

    chunks = [(c * offsets // CHUNKS, (c + 1) * offsets // CHUNKS) for c in range(CHUNKS)]

    halo = []

    def scatter_beside(sent, before):
        first, last = chunks.pop(0)
        held = (sent, dpre) if before is None else (sent, dpre, before)
        held = lax.optimization_barrier(held)
        dext, *blocks = scatter(
            map_flat, held[1], flipped, None if before is None else held[2],
            first, last - first, table_rows, width,
        )
        halo.extend(blocks)
        return held[0], dext

    mine = group_index(square)
    sent = []
    for d in range(1, pieces):
        piece = lax.dynamic_slice_in_dim(part, (mine ^ d) * height, height, axis=0)
        sent.append(piece.astype(jnp.bfloat16))
    own = lax.dynamic_slice_in_dim(part, mine * height, height, axis=0)
    sent, dext = scatter_beside(sent, None)
    got = [exchange(piece, square, d + 1) for d, piece in enumerate(sent)]
    got, dext = lax.optimization_barrier((got, dext))
    own = own + sum(piece.astype(jnp.float32) for piece in got)

    stride = 1
    while stride < lax.axis_size("tx"):
        radix = min(4, lax.axis_size("tx") // stride)
        own = own.astype(jnp.bfloat16)
        if chunks:
            own, dext = scatter_beside(own, dext)
        got = [own] + [exchange(own, ("tx",), m * stride) for m in range(1, radix)]
        got, dext, halo = lax.optimization_barrier((got, dext, halo))
        got = [piece.astype(jnp.float32) for piece in got]
        while len(got) > 1:
            got = [a + b for a, b in zip(got[::2], got[1::2])]
        own = got[0]
        stride *= radix
    while chunks:
        own, dext = scatter_beside(own, dext)

    from_y = swap_edges(halo[0], halo[1], "ty")
    from_x = swap_edges(halo[2], halo[3], "tx")
    everywhere = {0: own.astype(jnp.bfloat16)}
    bit = pieces // 2
    while bit:
        if bit == 1:
            everywhere, from_x, from_y = lax.optimization_barrier((everywhere, from_x, from_y))
        for d, piece in list(everywhere.items()):
            everywhere[d | bit] = exchange(piece, square, bit)
        bit //= 2
    grad_input = finish(dmixed, dext, send_rows.reshape(1, -1), from_x, from_y)
    everywhere = [everywhere[d] for d in range(pieces)]
    count = voxels * lax.axis_size("tx") * lax.axis_size("ty") * lax.axis_size("rep")
    conv, head = assemble(everywhere, square, 1.0 / math.sqrt(count), offsets * chans, classes)
    return grad_input, conv.reshape(offsets, chans, chans), head.T


def solution(mesh):
    placed = (
        P(("groups", "tx", "ty", "rep"), None),
        P(),
        P(),
        P(("groups", "tx", "ty", "rep"), None),
        P(None, ("groups", "tx", "ty", "rep")),
        P(("groups", "tx", "ty", "rep")),
    )
    return jax.shard_map(
        on_device,
        mesh=mesh,
        in_specs=placed,
        out_specs=(
            P(("groups", "tx", "ty", "rep"), None),
            P("groups", None, None),
            P("groups", None),
        ),
        check_vma=False,
    )
```

```python
import functools
import math

import jax
import jax.numpy as jnp
from jax import lax
from jax.experimental import pallas as pl
from jax.experimental.pallas import tpu as pltpu
from jax.sharding import PartitionSpec as P

STREAMS = 1
SCATTER_STREAMS = 2
SEGMENT = 256
BY_MATMUL = 8
SCATTER_STEPS = 64
FIRST_PART = 512
CHUNKS = 2
HEAD_ROWS = 32
VMEM = pl.BlockSpec(memory_space=pltpu.VMEM)
HBM = pl.BlockSpec(memory_space=pl.ANY)
NN = (((1,), (0,)), ((), ()))
NT = (((1,), (1,)), ((), ()))
TN = (((0,), (0,)), ((), ()))


def dot(a, b, dims):
    return lax.dot_general(a, b, dims, preferred_element_type=jnp.float32)


def from_neighbours(refs, axis):
    odd = (lax.axis_index(axis) & 1) != 0
    first = refs[0][...].astype(jnp.float32)
    second = refs[1][...].astype(jnp.float32) if len(refs) > 1 else jnp.zeros_like(first)
    return jnp.where(odd, first, second), jnp.where(odd, second, first)


def over_edges(down, up, axis):
    odd = (lax.axis_index(axis) & 1) != 0
    return jnp.where(odd, down, up), jnp.where(odd, up, down)


def fetch(map_hbm, index, sems, first, length, parts):
    stages = []
    for part, (start, stop) in enumerate(zip(parts[:-1], parts[1:])):
        stage = []
        for n, ref in enumerate(index):
            at = (first + n) * length + start
            stage.append(
                pltpu.make_async_copy(
                    map_hbm.at[pl.ds(at, stop - start)], ref.at[pl.ds(start, stop - start)],
                    sems.at[part, n],
                )
            )
        for copy in stage:
            copy.start()
        stages.append(stage)
    return stages


def forward_kernel(
    classes, map_hbm, sparse_ref, own_hbm, x_refs, y_refs, weight_hbm, class_ref, label_ref,
    dpre_ref, dmixed_ref, conv_ref, flipped_ref,
    own_ref, weight_ref, load_sems, table, turned, rows, wide, columns, side, total, sems, *index,
):
    voxels, chans = dpre_ref.shape
    looped = len(index) // STREAMS
    offsets = looped + BY_MATMUL
    stream = voxels // STREAMS
    block = STREAMS * SEGMENT
    share = SEGMENT // BY_MATMUL
    own_copy = pltpu.make_async_copy(own_hbm, own_ref, load_sems.at[0])
    own_copy.start()
    weight_copy = pltpu.make_async_copy(weight_hbm, weight_ref, load_sems.at[1])
    weight_copy.start()
    ready, later = fetch(map_hbm, index, sems, 0, stream, (0, FIRST_PART, stream))
    own_copy.wait()
    width = x_refs[0].shape[0]
    table[:voxels, :] = own_ref[...].astype(jnp.float32)
    halos = from_neighbours(x_refs, "tx") + from_neighbours(y_refs, "ty")
    for n, halo in enumerate(halos):
        start = voxels + n * width
        table[start : start + width, :] = halo
    filled = voxels + 4 * width
    table[filled:, :] = jnp.zeros((table.shape[0] - filled, chans), jnp.float32)
    for n in range(filled // chans):
        at = slice(n * chans, (n + 1) * chans)
        turned[:, at] = table[at, :].T.astype(jnp.bfloat16)
    total[...] = jnp.zeros_like(total)
    conv_ref[pl.ds(offsets * chans, conv_ref.shape[0] - offsets * chans), :] = jnp.zeros(
        (conv_ref.shape[0] - offsets * chans, chans), jnp.float32
    )
    weight_copy.wait()
    for k in range(offsets):
        at = slice(k * chans, (k + 1) * chans)
        turned_weight = weight_ref[at, :].T
        flipped_ref[at, :] = turned_weight
        if k >= looped:
            side[:, (k - looped) * chans : (k - looped + 1) * chans] = turned_weight
    for copy in ready:
        copy.wait()

    def block_step(b, carry):
        @pl.when(b == FIRST_PART // SEGMENT)
        def _():
            for copy in later:
                copy.wait()

        def gather_step(j, carry):
            row = lax.broadcasted_iota(jnp.int32, (filled, block), 0)
            chosen = (row == sparse_ref[b, pl.ds(j, 1), :]).astype(jnp.float32)
            at = pl.ds(pl.multiple_of(j * chans, chans), chans)
            columns[at, :] = dot(turned[...], chosen.astype(jnp.bfloat16), NN).astype(jnp.bfloat16)
            for n in range(share):
                to = j * share + n
                i = b * SEGMENT + to
                for u in range(STREAMS):
                    for k in range(looped):
                        rows[k, pl.ds(u * SEGMENT + to, 1), :] = table[
                            pl.ds(index[k * STREAMS + u][i], 1), :
                        ]
            return carry

        lax.fori_loop(0, BY_MATMUL, gather_step, 0)
        for k in range(looped):
            wide[:, k * chans : (k + 1) * chans] = rows[k].astype(jnp.bfloat16)
        pre = dot(wide[...], weight_ref[: looped * chans, :], NN)
        pre = pre + dot(side[...], columns[...], NN).T
        starts = [pl.multiple_of(u * stream + b * SEGMENT, SEGMENT) for u in range(STREAMS)]
        own = jnp.concatenate([table[pl.ds(s, SEGMENT), :] for s in starts], axis=0)
        sig = jax.nn.sigmoid(pre)
        mixed = (own + pre * sig).astype(jnp.bfloat16)
        logits = dot(class_ref[...], mixed, NT)
        which = lax.broadcasted_iota(jnp.int32, logits.shape, 0)
        logits = jnp.where(which < classes, logits, -1e30)
        high = jnp.max(logits, axis=0, keepdims=True)
        expd = jnp.exp(logits - high)
        probs = expd / jnp.sum(expd, axis=0, keepdims=True)
        onehot = (which == label_ref[b]).astype(jnp.float32)
        dlogits = (probs - onehot).astype(jnp.bfloat16)
        conv_ref[pl.ds(offsets * chans, HEAD_ROWS), :] += dot(dlogits, mixed, NN)
        dmixed = dot(dlogits, class_ref[...], TN)
        dpre = (dmixed * sig * (1.0 + pre * (1.0 - sig))).astype(jnp.bfloat16)
        full = dpre.astype(jnp.float32)
        for u, s in enumerate(starts):
            dmixed_ref[pl.ds(s, SEGMENT), :] = dmixed[u * SEGMENT : (u + 1) * SEGMENT]
            dpre_ref[pl.ds(s, SEGMENT), :] = full[u * SEGMENT : (u + 1) * SEGMENT]
        full_t = full.T.astype(jnp.bfloat16)
        total[:, : looped * chans] += dot(full_t, wide[...], NN)
        total[:, looped * chans :] += dot(full_t, columns[...], NT)
        return carry

    lax.fori_loop(0, voxels // block, block_step, 0)
    for k in range(offsets):
        conv_ref[k * chans : (k + 1) * chans, :] = total[:, k * chans : (k + 1) * chans].T


def forward(map_flat, sparse, features, from_x, from_y, weights, class_t, label_blocks, classes, reduce_rows, table_rows):
    voxels, chans = features.shape
    offsets = weights.shape[0] // chans
    looped = offsets - BY_MATMUL
    stream = voxels // STREAMS
    block = STREAMS * SEGMENT
    filled = voxels + 4 * from_x[0].shape[0]
    return pl.pallas_call(
        functools.partial(forward_kernel, classes),
        out_shape=(
            jax.ShapeDtypeStruct((voxels, chans), jnp.float32),
            jax.ShapeDtypeStruct((voxels, chans), jnp.float32),
            jax.ShapeDtypeStruct((reduce_rows, chans), jnp.float32),
            jax.ShapeDtypeStruct(weights.shape, jnp.bfloat16),
        ),
        in_specs=[HBM, VMEM, HBM, [VMEM] * len(from_x), [VMEM] * len(from_y), HBM, VMEM, VMEM],
        out_specs=(VMEM, VMEM, VMEM, VMEM),
        scratch_shapes=[
            pltpu.VMEM(features.shape, jnp.bfloat16),
            pltpu.VMEM(weights.shape, jnp.bfloat16),
            pltpu.SemaphoreType.DMA((2,)),
            pltpu.VMEM((table_rows, chans), jnp.float32),
            pltpu.VMEM((chans, filled), jnp.bfloat16),
            pltpu.VMEM((looped, block, chans), jnp.float32),
            pltpu.VMEM((block, looped * chans), jnp.bfloat16),
            pltpu.VMEM((BY_MATMUL * chans, block), jnp.bfloat16),
            pltpu.VMEM((chans, BY_MATMUL * chans), jnp.bfloat16),
            pltpu.VMEM((chans, offsets * chans), jnp.float32),
            pltpu.SemaphoreType.DMA((2, looped * STREAMS)),
        ]
        + [pltpu.SMEM((stream,), jnp.int32)] * (looped * STREAMS),
        compiler_params=pltpu.CompilerParams(vmem_limit_bytes=17 << 20),
        name="forward",
    )(map_flat, sparse, features, from_x, from_y, weights, class_t, label_blocks)


def scatter_kernel(first, offsets, has_before, map_hbm, dpre_ref, weight_ref, *refs):
    refs = list(refs)
    before = refs.pop(0) if has_before else None
    out_ref = refs.pop(0)
    back_refs = [refs.pop(0) for _ in range(4)] if has_before else []
    sems = refs.pop(0)
    tables = refs[:offsets]
    index = refs[offsets:]
    streams, stream, chans = dpre_ref.shape
    share = stream // SCATTER_STEPS
    copies, = fetch(map_hbm, index, sems, first * streams, stream, (0, stream))
    for table in tables:
        table[...] = jnp.zeros_like(table)
    for copy in copies:
        copy.wait()

    def step(j, carry):
        for n in range(share):
            i = j * share + n
            for u in range(streams):
                value = dpre_ref[u, pl.ds(i, 1), :]
                for k in range(offsets):
                    where = pl.ds(index[k * streams + u][i], 1)
                    tables[k][where, :] = tables[k][where, :] + value
        return carry

    lax.fori_loop(0, SCATTER_STEPS, step, 0)
    tiles = 3
    height = out_ref.shape[0] // tiles

    def finish(t, carry):
        at = pl.ds(pl.multiple_of(t * height, 16), height)
        wide = jnp.concatenate([table[at, :].astype(jnp.bfloat16) for table in tables], axis=1)
        result = dot(wide, weight_ref[first * chans : (first + offsets) * chans, :], NN)
        out_ref[at, :] = result + before[at, :] if has_before else result
        return carry

    lax.fori_loop(0, tiles, finish, 0)
    if back_refs:
        width = back_refs[0].shape[0]
        voxels = streams * stream
        halos = [out_ref[voxels + n * width : voxels + (n + 1) * width, :] for n in range(4)]
        picked = over_edges(halos[2], halos[3], "ty") + over_edges(halos[0], halos[1], "tx")
        for back_ref, value in zip(back_refs, picked):
            back_ref[...] = value.astype(jnp.bfloat16)


def scatter(map_flat, dpre, flipped, before, first, offsets, table_rows, width):
    voxels, chans = dpre.shape
    stream = voxels // SCATTER_STREAMS
    has_before = before is not None
    return pl.pallas_call(
        functools.partial(scatter_kernel, first, offsets, has_before),
        out_shape=[jax.ShapeDtypeStruct((table_rows, chans), jnp.float32)]
        + [jax.ShapeDtypeStruct((width, chans), jnp.bfloat16)] * (4 if has_before else 0),
        in_specs=[HBM, VMEM, VMEM] + ([VMEM] if has_before else []),
        out_specs=[VMEM] * (5 if has_before else 1),
        scratch_shapes=[
            pltpu.SemaphoreType.DMA((1, offsets * SCATTER_STREAMS)),
        ]
        + [pltpu.VMEM((table_rows, chans), jnp.float32)] * offsets
        + [pltpu.SMEM((stream,), jnp.int32)] * (offsets * SCATTER_STREAMS),
        compiler_params=pltpu.CompilerParams(vmem_limit_bytes=21 << 20),
        cost_estimate=pl.CostEstimate(
            flops=2 * voxels * offsets * chans * chans, bytes_accessed=40 << 20, transcendentals=0
        ),
        name=f"scatter_{first}",
    )(
        map_flat, dpre.reshape(SCATTER_STREAMS, stream, chans), flipped,
        *([before] if has_before else []),
    )


def finish_kernel(dmixed_ref, dext_ref, send_ref, x_refs, y_refs, out_ref, back_ref):
    voxels, chans = out_ref.shape
    width = x_refs[0].shape[0]
    low_x, high_x = from_neighbours(x_refs, "tx")
    low_y, high_y = from_neighbours(y_refs, "ty")
    for n, value in enumerate((high_x, low_x, high_y, low_y)):
        back_ref[n * width : (n + 1) * width, :] = value.astype(jnp.bfloat16)
    height = voxels // 8

    def step(t, carry):
        at = pl.ds(pl.multiple_of(t * height, height), height)
        row = lax.broadcasted_iota(jnp.int32, (height, send_ref.shape[1]), 0) + t * height
        chosen = (row == send_ref[...]).astype(jnp.float32).astype(jnp.bfloat16)
        out_ref[at, :] = dmixed_ref[at, :] + dext_ref[at, :] + dot(chosen, back_ref[...], NN)
        return carry

    lax.fori_loop(0, voxels // height, step, 0)


def finish(dmixed, dext, send_flat, from_x, from_y):
    return pl.pallas_call(
        finish_kernel,
        out_shape=jax.ShapeDtypeStruct(dmixed.shape, jnp.float32),
        in_specs=[VMEM, VMEM, VMEM, [VMEM] * len(from_x), [VMEM] * len(from_y)],
        out_specs=VMEM,
        scratch_shapes=[pltpu.VMEM((send_flat.shape[1], dmixed.shape[1]), jnp.bfloat16)],
        compiler_params=pltpu.CompilerParams(vmem_limit_bytes=12 << 20),
        cost_estimate=pl.CostEstimate(flops=1 << 28, bytes_accessed=4 << 20, transcendentals=0),
        name="finish",
    )(dmixed, dext, send_flat, from_x, from_y)


def outgoing_kernel(axes, send_hbm, own_hbm, *refs):
    *out_refs, send_ref, own_ref, sems, table, sent = refs
    voxels, chans = own_ref.shape
    send_copy = pltpu.make_async_copy(send_hbm, send_ref, sems.at[0])
    send_copy.start()
    own_copy = pltpu.make_async_copy(own_hbm, own_ref, sems.at[1])
    own_copy.start()
    own_copy.wait()
    width = send_ref.shape[1]
    table[:voxels, :] = own_ref[...].astype(jnp.float32)
    table[voxels:, :] = jnp.zeros((table.shape[0] - voxels, chans), jnp.float32)
    send_copy.wait()
    for s in range(4):

        def step(t, carry, s=s):
            for n in range(32):
                i = t * 32 + n
                sent[pl.ds(s * width + i, 1), :] = table[pl.ds(send_ref[s, i], 1), :]
            return carry

        lax.fori_loop(0, width // 32, step, 0)
    lists = [sent[s * width : (s + 1) * width, :] for s in range(4)]
    picked = []
    for axis, (up, down) in zip(axes, ((2, 3), (0, 1))):
        picked.extend(over_edges(lists[down], lists[up], axis))
    for out_ref, value in zip(out_refs, picked):
        out_ref[...] = value.astype(jnp.bfloat16)


def outgoing(send_rows, features):
    voxels, chans = features.shape
    width = send_rows.shape[1]
    return pl.pallas_call(
        functools.partial(outgoing_kernel, ("ty", "tx")),
        out_shape=[jax.ShapeDtypeStruct((width, chans), jnp.bfloat16)] * 4,
        in_specs=[HBM, HBM],
        out_specs=[VMEM] * 4,
        scratch_shapes=[
            pltpu.SMEM(send_rows.shape, jnp.int32),
            pltpu.VMEM(features.shape, jnp.bfloat16),
            pltpu.SemaphoreType.DMA((2,)),
            pltpu.VMEM((voxels + 8, chans), jnp.float32),
            pltpu.VMEM((4 * width, chans), jnp.float32),
        ],
        compiler_params=pltpu.CompilerParams(vmem_limit_bytes=60 << 20),
        cost_estimate=pl.CostEstimate(flops=0, bytes_accessed=8 << 20, transcendentals=0),
        name="outgoing",
    )(send_rows, features)


def assemble_kernel(axes, scale, conv_rows, *refs):
    *piece_refs, conv_ref, head_ref = refs
    pieces = len(piece_refs)
    height = piece_refs[0].shape[0]
    mine = group_index(axes)
    for d, piece_ref in enumerate(piece_refs):
        for p in range(pieces):

            @pl.when((mine ^ d) == p)
            def _(p=p, piece_ref=piece_ref):
                start = p * height
                inside = max(0, min(height, conv_rows - start))
                if inside:
                    value = piece_ref[:inside, :].astype(jnp.float32) * scale
                    conv_ref[start : start + inside, :] = value
                if start <= conv_rows < start + height:
                    at = conv_rows - start
                    value = piece_ref[at : at + HEAD_ROWS, :].astype(jnp.float32) * scale
                    head_ref[...] = value[: head_ref.shape[0], :]


def assemble(pieces, axes, scale, conv_rows, classes):
    chans = pieces[0].shape[1]
    return pl.pallas_call(
        functools.partial(assemble_kernel, axes, scale, conv_rows),
        out_shape=(
            jax.ShapeDtypeStruct((conv_rows, chans), jnp.float32),
            jax.ShapeDtypeStruct((classes, chans), jnp.float32),
        ),
        in_specs=[VMEM] * len(pieces),
        out_specs=(VMEM, VMEM),
        compiler_params=pltpu.CompilerParams(vmem_limit_bytes=12 << 20),
        name="assemble",
    )(*pieces)


def group_index(axes):
    at = 0
    for axis in axes:
        at = at * lax.axis_size(axis) + lax.axis_index(axis)
    return at


def group_size(axes):
    return math.prod(lax.axis_size(axis) for axis in axes)


def exchange(shard, axes, distance):
    return lax.ppermute(shard, axes, [(i, i ^ distance) for i in range(group_size(axes))])


def edge_pairs(axis):
    devices = lax.axis_size(axis)
    even = [(i, i ^ 1) for i in range(devices) if (i ^ 1) < devices]
    odd = [(i, ((i + 1) ^ 1) - 1) for i in range(1, devices) if ((i + 1) ^ 1) - 1 < devices]
    return even, odd


def swap_edges(over_even, over_odd, axis):
    even_pairs, odd_pairs = edge_pairs(axis)
    got = [lax.ppermute(over_even, axis, even_pairs)]
    if odd_pairs:
        got.append(lax.ppermute(over_odd, axis, odd_pairs))
    return got


def on_device(features, conv_weight, classifier, send_rows, neighbour_map, labels):
    voxels, chans = features.shape
    width = send_rows.shape[1]
    offsets = conv_weight.shape[0]
    classes = classifier.shape[1]
    block = STREAMS * SEGMENT
    table_rows = -(-(voxels + 4 * width + 1) // 48) * 48
    square = ("ty", "rep")
    pieces = group_size(square)
    unit = 16 * pieces
    reduce_rows = -(-(offsets * chans + HEAD_ROWS) // unit) * unit
    height = reduce_rows // pieces

    even_y, odd_y, even_x, odd_x = outgoing(send_rows, features)
    from_y = swap_edges(even_y, odd_y, "ty")
    from_x = swap_edges(even_x, odd_x, "tx")

    zero_row = voxels + 4 * width
    moved = jnp.where(neighbour_map > voxels, neighbour_map - 1, neighbour_map)
    moved = jnp.where(neighbour_map == voxels, zero_row, moved)
    map_flat = moved.reshape(-1)
    sparse = (
        moved[offsets - BY_MATMUL :].reshape(BY_MATMUL, STREAMS, voxels // block, SEGMENT)
        .transpose(2, 0, 1, 3).reshape(voxels // block, BY_MATMUL, block)
    )
    weights = conv_weight.reshape(offsets * chans, chans)
    class_t = jnp.pad(classifier.T, ((0, HEAD_ROWS - classes), (0, 0)))
    label_blocks = (
        labels.reshape(STREAMS, voxels // block, SEGMENT).transpose(1, 0, 2)
        .reshape(voxels // block, 1, block)
    )
    dpre, dmixed, part, flipped = forward(
        map_flat, sparse, features, from_x, from_y, weights, class_t, label_blocks,
        classes, reduce_rows, table_rows,
    )

    chunks = [(c * offsets // CHUNKS, (c + 1) * offsets // CHUNKS) for c in range(CHUNKS)]

    halo = []

    def scatter_beside(sent, before):
        first, last = chunks.pop(0)
        held = (sent, dpre) if before is None else (sent, dpre, before)
        held = lax.optimization_barrier(held)
        dext, *blocks = scatter(
            map_flat, held[1], flipped, None if before is None else held[2],
            first, last - first, table_rows, width,
        )
        halo.extend(blocks)
        return held[0], dext

    mine = group_index(square)
    sent = []
    for d in range(1, pieces):
        piece = lax.dynamic_slice_in_dim(part, (mine ^ d) * height, height, axis=0)
        sent.append(piece.astype(jnp.bfloat16))
    own = lax.dynamic_slice_in_dim(part, mine * height, height, axis=0)
    (sent, own), dext = scatter_beside((sent, own), None)
    got = [exchange(piece, square, d + 1) for d, piece in enumerate(sent)]
    got, dext = lax.optimization_barrier((got, dext))
    own = own + sum(piece.astype(jnp.float32) for piece in got)

    stride = 1
    while stride < lax.axis_size("tx"):
        radix = min(4, lax.axis_size("tx") // stride)
        own = own.astype(jnp.bfloat16)
        if chunks:
            own, dext = scatter_beside(own, dext)
        got = [own] + [exchange(own, ("tx",), m * stride) for m in range(1, radix)]
        got, dext, halo = lax.optimization_barrier((got, dext, halo))
        got = [piece.astype(jnp.float32) for piece in got]
        while len(got) > 1:
            got = [a + b for a, b in zip(got[::2], got[1::2])]
        own = got[0]
        stride *= radix
    while chunks:
        own, dext = scatter_beside(own, dext)

    from_y = swap_edges(halo[0], halo[1], "ty")
    from_x = swap_edges(halo[2], halo[3], "tx")
    everywhere = {0: own.astype(jnp.bfloat16)}
    bit = pieces // 2
    while bit:
        if bit == 1:
            everywhere, from_x, from_y = lax.optimization_barrier((everywhere, from_x, from_y))
        for d, piece in list(everywhere.items()):
            everywhere[d | bit] = exchange(piece, square, bit)
        bit //= 2
    grad_input = finish(dmixed, dext, send_rows.reshape(1, -1), from_x, from_y)
    everywhere = [everywhere[d] for d in range(pieces)]
    count = voxels * lax.axis_size("tx") * lax.axis_size("ty") * lax.axis_size("rep")
    conv, head = assemble(everywhere, square, 1.0 / math.sqrt(count), offsets * chans, classes)
    return grad_input, conv.reshape(offsets, chans, chans), head.T


def solution(mesh):
    placed = (
        P(("groups", "tx", "ty", "rep"), None),
        P(),
        P(),
        P(("groups", "tx", "ty", "rep"), None),
        P(None, ("groups", "tx", "ty", "rep")),
        P(("groups", "tx", "ty", "rep")),
    )
    return jax.shard_map(
        on_device,
        mesh=mesh,
        in_specs=placed,
        out_specs=(
            P(("groups", "tx", "ty", "rep"), None),
            P("groups", None, None),
            P("groups", None),
        ),
        check_vma=False,
    )
```

```python
import functools
import math

import jax
import jax.numpy as jnp
from jax import lax
from jax.experimental import pallas as pl
from jax.experimental.pallas import tpu as pltpu
from jax.sharding import PartitionSpec as P

STREAMS = 1
SCATTER_STREAMS = 2
SEGMENT = 256
BY_MATMUL = 8
SCATTER_STEPS = 64
FIRST_PART = 512
CHUNKS = 2
HEAD_ROWS = 32
VMEM = pl.BlockSpec(memory_space=pltpu.VMEM)
HBM = pl.BlockSpec(memory_space=pl.ANY)
NN = (((1,), (0,)), ((), ()))
NT = (((1,), (1,)), ((), ()))
TN = (((0,), (0,)), ((), ()))


def dot(a, b, dims):
    return lax.dot_general(a, b, dims, preferred_element_type=jnp.float32)


def from_neighbours(refs, axis):
    odd = (lax.axis_index(axis) & 1) != 0
    first = refs[0][...].astype(jnp.float32)
    second = refs[1][...].astype(jnp.float32) if len(refs) > 1 else jnp.zeros_like(first)
    return jnp.where(odd, first, second), jnp.where(odd, second, first)


def over_edges(down, up, axis):
    odd = (lax.axis_index(axis) & 1) != 0
    return jnp.where(odd, down, up), jnp.where(odd, up, down)


def fetch(map_hbm, index, sems, first, length, parts):
    stages = []
    for part, (start, stop) in enumerate(zip(parts[:-1], parts[1:])):
        stage = []
        for n, ref in enumerate(index):
            at = (first + n) * length + start
            stage.append(
                pltpu.make_async_copy(
                    map_hbm.at[pl.ds(at, stop - start)], ref.at[pl.ds(start, stop - start)],
                    sems.at[part, n],
                )
            )
        for copy in stage:
            copy.start()
        stages.append(stage)
    return stages


def forward_kernel(
    classes, map_hbm, sparse_ref, own_hbm, x_refs, y_refs, weight_hbm, class_ref, label_ref,
    dpre_ref, dmixed_ref, conv_ref, flipped_ref,
    own_ref, weight_ref, load_sems, table, turned, rows, wide, columns, side, total, sems, *index,
):
    voxels, chans = dpre_ref.shape
    looped = len(index) // STREAMS
    offsets = looped + BY_MATMUL
    stream = voxels // STREAMS
    block = STREAMS * SEGMENT
    share = SEGMENT // BY_MATMUL
    own_copy = pltpu.make_async_copy(own_hbm, own_ref, load_sems.at[0])
    own_copy.start()
    weight_copy = pltpu.make_async_copy(weight_hbm, weight_ref, load_sems.at[1])
    weight_copy.start()
    ready, later = fetch(map_hbm, index, sems, 0, stream, (0, FIRST_PART, stream))
    own_copy.wait()
    width = x_refs[0].shape[0]
    table[:voxels, :] = own_ref[...].astype(jnp.float32)
    halos = from_neighbours(x_refs, "tx") + from_neighbours(y_refs, "ty")
    for n, halo in enumerate(halos):
        start = voxels + n * width
        table[start : start + width, :] = halo
    filled = voxels + 4 * width
    table[filled:, :] = jnp.zeros((table.shape[0] - filled, chans), jnp.float32)
    for n in range(filled // chans):
        at = slice(n * chans, (n + 1) * chans)
        turned[:, at] = table[at, :].T.astype(jnp.bfloat16)
    total[...] = jnp.zeros_like(total)
    conv_ref[pl.ds(offsets * chans, conv_ref.shape[0] - offsets * chans), :] = jnp.zeros(
        (conv_ref.shape[0] - offsets * chans, chans), jnp.float32
    )
    weight_copy.wait()
    for k in range(offsets):
        at = slice(k * chans, (k + 1) * chans)
        turned_weight = weight_ref[at, :].T
        flipped_ref[at, :] = turned_weight
        if k >= looped:
            side[:, (k - looped) * chans : (k - looped + 1) * chans] = turned_weight
    for copy in ready:
        copy.wait()

    def block_step(b, carry):
        @pl.when(b == FIRST_PART // SEGMENT)
        def _():
            for copy in later:
                copy.wait()

        def gather_step(j, carry):
            row = lax.broadcasted_iota(jnp.int32, (filled, block), 0)
            chosen = (row == sparse_ref[b, pl.ds(j, 1), :]).astype(jnp.float32)
            at = pl.ds(pl.multiple_of(j * chans, chans), chans)
            columns[at, :] = dot(turned[...], chosen.astype(jnp.bfloat16), NN).astype(jnp.bfloat16)
            for n in range(share):
                to = j * share + n
                i = b * SEGMENT + to
                for u in range(STREAMS):
                    for k in range(looped):
                        rows[k, pl.ds(u * SEGMENT + to, 1), :] = table[
                            pl.ds(index[k * STREAMS + u][i], 1), :
                        ]
            return carry

        lax.fori_loop(0, BY_MATMUL, gather_step, 0)
        for k in range(looped):
            wide[:, k * chans : (k + 1) * chans] = rows[k].astype(jnp.bfloat16)
        pre = dot(wide[...], weight_ref[: looped * chans, :], NN)
        pre = pre + dot(side[...], columns[...], NN).T
        starts = [pl.multiple_of(u * stream + b * SEGMENT, SEGMENT) for u in range(STREAMS)]
        own = jnp.concatenate([table[pl.ds(s, SEGMENT), :] for s in starts], axis=0)
        sig = jax.nn.sigmoid(pre)
        mixed = (own + pre * sig).astype(jnp.bfloat16)
        logits = dot(class_ref[...], mixed, NT)
        which = lax.broadcasted_iota(jnp.int32, logits.shape, 0)
        logits = jnp.where(which < classes, logits, -1e30)
        high = jnp.max(logits, axis=0, keepdims=True)
        expd = jnp.exp(logits - high)
        probs = expd / jnp.sum(expd, axis=0, keepdims=True)
        onehot = (which == label_ref[b]).astype(jnp.float32)
        dlogits = (probs - onehot).astype(jnp.bfloat16)
        conv_ref[pl.ds(offsets * chans, HEAD_ROWS), :] += dot(dlogits, mixed, NN)
        dmixed = dot(dlogits, class_ref[...], TN)
        dpre = (dmixed * sig * (1.0 + pre * (1.0 - sig))).astype(jnp.bfloat16)
        full = dpre.astype(jnp.float32)
        for u, s in enumerate(starts):
            dmixed_ref[pl.ds(s, SEGMENT), :] = dmixed[u * SEGMENT : (u + 1) * SEGMENT]
            dpre_ref[pl.ds(s, SEGMENT), :] = full[u * SEGMENT : (u + 1) * SEGMENT]
        full_t = full.T.astype(jnp.bfloat16)
        total[:, : looped * chans] += dot(full_t, wide[...], NN)
        total[:, looped * chans :] += dot(full_t, columns[...], NT)
        return carry

    lax.fori_loop(0, voxels // block, block_step, 0)
    for k in range(offsets):
        conv_ref[k * chans : (k + 1) * chans, :] = total[:, k * chans : (k + 1) * chans].T


def forward(map_flat, sparse, features, from_x, from_y, weights, class_t, label_blocks, classes, reduce_rows, table_rows):
    voxels, chans = features.shape
    offsets = weights.shape[0] // chans
    looped = offsets - BY_MATMUL
    stream = voxels // STREAMS
    block = STREAMS * SEGMENT
    filled = voxels + 4 * from_x[0].shape[0]
    return pl.pallas_call(
        functools.partial(forward_kernel, classes),
        out_shape=(
            jax.ShapeDtypeStruct((voxels, chans), jnp.float32),
            jax.ShapeDtypeStruct((voxels, chans), jnp.float32),
            jax.ShapeDtypeStruct((reduce_rows, chans), jnp.float32),
            jax.ShapeDtypeStruct(weights.shape, jnp.bfloat16),
        ),
        in_specs=[HBM, VMEM, HBM, [VMEM] * len(from_x), [VMEM] * len(from_y), HBM, VMEM, VMEM],
        out_specs=(VMEM, VMEM, VMEM, VMEM),
        scratch_shapes=[
            pltpu.VMEM(features.shape, jnp.bfloat16),
            pltpu.VMEM(weights.shape, jnp.bfloat16),
            pltpu.SemaphoreType.DMA((2,)),
            pltpu.VMEM((table_rows, chans), jnp.float32),
            pltpu.VMEM((chans, filled), jnp.bfloat16),
            pltpu.VMEM((looped, block, chans), jnp.float32),
            pltpu.VMEM((block, looped * chans), jnp.bfloat16),
            pltpu.VMEM((BY_MATMUL * chans, block), jnp.bfloat16),
            pltpu.VMEM((chans, BY_MATMUL * chans), jnp.bfloat16),
            pltpu.VMEM((chans, offsets * chans), jnp.float32),
            pltpu.SemaphoreType.DMA((2, looped * STREAMS)),
        ]
        + [pltpu.SMEM((stream,), jnp.int32)] * (looped * STREAMS),
        compiler_params=pltpu.CompilerParams(vmem_limit_bytes=17 << 20),
        name="forward",
    )(map_flat, sparse, features, from_x, from_y, weights, class_t, label_blocks)


def scatter_kernel(first, offsets, has_before, map_hbm, dpre_ref, weight_ref, *refs):
    refs = list(refs)
    before = refs.pop(0) if has_before else None
    out_ref = refs.pop(0)
    back_refs = [refs.pop(0) for _ in range(4)] if has_before else []
    sems = refs.pop(0)
    tables = refs[:offsets]
    index = refs[offsets:]
    streams, stream, chans = dpre_ref.shape
    share = stream // SCATTER_STEPS
    copies, = fetch(map_hbm, index, sems, first * streams, stream, (0, stream))
    for table in tables:
        table[...] = jnp.zeros_like(table)
    for copy in copies:
        copy.wait()

    def step(j, carry):
        for n in range(share):
            i = j * share + n
            for u in range(streams):
                value = dpre_ref[u, pl.ds(i, 1), :]
                for k in range(offsets):
                    where = pl.ds(index[k * streams + u][i], 1)
                    tables[k][where, :] = tables[k][where, :] + value
        return carry

    lax.fori_loop(0, SCATTER_STEPS, step, 0)
    tiles = 3
    height = out_ref.shape[0] // tiles

    def finish(t, carry):
        at = pl.ds(pl.multiple_of(t * height, 16), height)
        wide = jnp.concatenate([table[at, :].astype(jnp.bfloat16) for table in tables], axis=1)
        result = dot(wide, weight_ref[first * chans : (first + offsets) * chans, :], NN)
        out_ref[at, :] = result + before[at, :] if has_before else result
        return carry

    lax.fori_loop(0, tiles, finish, 0)
    if back_refs:
        width = back_refs[0].shape[0]
        voxels = streams * stream
        halos = [out_ref[voxels + n * width : voxels + (n + 1) * width, :] for n in range(4)]
        picked = over_edges(halos[2], halos[3], "ty") + over_edges(halos[0], halos[1], "tx")
        for back_ref, value in zip(back_refs, picked):
            back_ref[...] = value.astype(jnp.bfloat16)


def scatter(map_flat, dpre, flipped, before, first, offsets, table_rows, width):
    voxels, chans = dpre.shape
    stream = voxels // SCATTER_STREAMS
    has_before = before is not None
    return pl.pallas_call(
        functools.partial(scatter_kernel, first, offsets, has_before),
        out_shape=[jax.ShapeDtypeStruct((table_rows, chans), jnp.float32)]
        + [jax.ShapeDtypeStruct((width, chans), jnp.bfloat16)] * (4 if has_before else 0),
        in_specs=[HBM, VMEM, VMEM] + ([VMEM] if has_before else []),
        out_specs=[VMEM] * (5 if has_before else 1),
        scratch_shapes=[
            pltpu.SemaphoreType.DMA((1, offsets * SCATTER_STREAMS)),
        ]
        + [pltpu.VMEM((table_rows, chans), jnp.float32)] * offsets
        + [pltpu.SMEM((stream,), jnp.int32)] * (offsets * SCATTER_STREAMS),
        compiler_params=pltpu.CompilerParams(vmem_limit_bytes=21 << 20),
        cost_estimate=pl.CostEstimate(
            flops=2 * voxels * offsets * chans * chans, bytes_accessed=40 << 20, transcendentals=0
        ),
        name=f"scatter_{first}",
    )(
        map_flat, dpre.reshape(SCATTER_STREAMS, stream, chans), flipped,
        *([before] if has_before else []),
    )


def finish_kernel(dmixed_ref, dext_ref, send_ref, x_refs, y_refs, out_ref, back_ref):
    voxels, chans = out_ref.shape
    width = x_refs[0].shape[0]
    low_x, high_x = from_neighbours(x_refs, "tx")
    low_y, high_y = from_neighbours(y_refs, "ty")
    for n, value in enumerate((high_x, low_x, high_y, low_y)):
        back_ref[n * width : (n + 1) * width, :] = value.astype(jnp.bfloat16)
    height = voxels // 2

    def step(t, carry):
        at = pl.ds(pl.multiple_of(t * height, height), height)
        row = lax.broadcasted_iota(jnp.int32, (height, send_ref.shape[1]), 0) + t * height
        chosen = (row == send_ref[...]).astype(jnp.float32).astype(jnp.bfloat16)
        out_ref[at, :] = dmixed_ref[at, :] + dext_ref[at, :] + dot(chosen, back_ref[...], NN)
        return carry

    lax.fori_loop(0, voxels // height, step, 0)


def finish(dmixed, dext, send_flat, from_x, from_y):
    return pl.pallas_call(
        finish_kernel,
        out_shape=jax.ShapeDtypeStruct(dmixed.shape, jnp.float32),
        in_specs=[VMEM, VMEM, VMEM, [VMEM] * len(from_x), [VMEM] * len(from_y)],
        out_specs=VMEM,
        scratch_shapes=[pltpu.VMEM((send_flat.shape[1], dmixed.shape[1]), jnp.bfloat16)],
        compiler_params=pltpu.CompilerParams(vmem_limit_bytes=12 << 20),
        cost_estimate=pl.CostEstimate(flops=1 << 28, bytes_accessed=4 << 20, transcendentals=0),
        name="finish",
    )(dmixed, dext, send_flat, from_x, from_y)


def outgoing_kernel(axes, send_hbm, own_hbm, *refs):
    *out_refs, send_ref, own_ref, sems, table, sent = refs
    voxels, chans = own_ref.shape
    send_copy = pltpu.make_async_copy(send_hbm, send_ref, sems.at[0])
    send_copy.start()
    own_copy = pltpu.make_async_copy(own_hbm, own_ref, sems.at[1])
    own_copy.start()
    own_copy.wait()
    width = send_ref.shape[1]
    table[:voxels, :] = own_ref[...].astype(jnp.float32)
    table[voxels:, :] = jnp.zeros((table.shape[0] - voxels, chans), jnp.float32)
    send_copy.wait()
    for s in range(4):

        def step(t, carry, s=s):
            for n in range(32):
                i = t * 32 + n
                sent[pl.ds(s * width + i, 1), :] = table[pl.ds(send_ref[s, i], 1), :]
            return carry

        lax.fori_loop(0, width // 32, step, 0)
    lists = [sent[s * width : (s + 1) * width, :] for s in range(4)]
    picked = []
    for axis, (up, down) in zip(axes, ((2, 3), (0, 1))):
        picked.extend(over_edges(lists[down], lists[up], axis))
    for out_ref, value in zip(out_refs, picked):
        out_ref[...] = value.astype(jnp.bfloat16)


def outgoing(send_rows, features):
    voxels, chans = features.shape
    width = send_rows.shape[1]
    return pl.pallas_call(
        functools.partial(outgoing_kernel, ("ty", "tx")),
        out_shape=[jax.ShapeDtypeStruct((width, chans), jnp.bfloat16)] * 4,
        in_specs=[HBM, HBM],
        out_specs=[VMEM] * 4,
        scratch_shapes=[
            pltpu.SMEM(send_rows.shape, jnp.int32),
            pltpu.VMEM(features.shape, jnp.bfloat16),
            pltpu.SemaphoreType.DMA((2,)),
            pltpu.VMEM((voxels + 8, chans), jnp.float32),
            pltpu.VMEM((4 * width, chans), jnp.float32),
        ],
        compiler_params=pltpu.CompilerParams(vmem_limit_bytes=60 << 20),
        cost_estimate=pl.CostEstimate(flops=0, bytes_accessed=8 << 20, transcendentals=0),
        name="outgoing",
    )(send_rows, features)


def assemble_kernel(axes, scale, conv_rows, *refs):
    *piece_refs, conv_ref, head_ref = refs
    pieces = len(piece_refs)
    height = piece_refs[0].shape[0]
    mine = group_index(axes)
    for d, piece_ref in enumerate(piece_refs):
        for p in range(pieces):

            @pl.when((mine ^ d) == p)
            def _(p=p, piece_ref=piece_ref):
                start = p * height
                inside = max(0, min(height, conv_rows - start))
                if inside:
                    value = piece_ref[:inside, :].astype(jnp.float32) * scale
                    conv_ref[start : start + inside, :] = value
                if start <= conv_rows < start + height:
                    at = conv_rows - start
                    value = piece_ref[at : at + HEAD_ROWS, :].astype(jnp.float32) * scale
                    head_ref[...] = value[: head_ref.shape[0], :]


def assemble(pieces, axes, scale, conv_rows, classes):
    chans = pieces[0].shape[1]
    return pl.pallas_call(
        functools.partial(assemble_kernel, axes, scale, conv_rows),
        out_shape=(
            jax.ShapeDtypeStruct((conv_rows, chans), jnp.float32),
            jax.ShapeDtypeStruct((classes, chans), jnp.float32),
        ),
        in_specs=[VMEM] * len(pieces),
        out_specs=(VMEM, VMEM),
        compiler_params=pltpu.CompilerParams(vmem_limit_bytes=12 << 20),
        name="assemble",
    )(*pieces)


def group_index(axes):
    at = 0
    for axis in axes:
        at = at * lax.axis_size(axis) + lax.axis_index(axis)
    return at


def group_size(axes):
    return math.prod(lax.axis_size(axis) for axis in axes)


def exchange(shard, axes, distance):
    return lax.ppermute(shard, axes, [(i, i ^ distance) for i in range(group_size(axes))])


def edge_pairs(axis):
    devices = lax.axis_size(axis)
    even = [(i, i ^ 1) for i in range(devices) if (i ^ 1) < devices]
    odd = [(i, ((i + 1) ^ 1) - 1) for i in range(1, devices) if ((i + 1) ^ 1) - 1 < devices]
    return even, odd


def swap_edges(over_even, over_odd, axis):
    even_pairs, odd_pairs = edge_pairs(axis)
    got = [lax.ppermute(over_even, axis, even_pairs)]
    if odd_pairs:
        got.append(lax.ppermute(over_odd, axis, odd_pairs))
    return got


def on_device(features, conv_weight, classifier, send_rows, neighbour_map, labels):
    voxels, chans = features.shape
    width = send_rows.shape[1]
    offsets = conv_weight.shape[0]
    classes = classifier.shape[1]
    block = STREAMS * SEGMENT
    table_rows = -(-(voxels + 4 * width + 1) // 48) * 48
    square = ("ty", "rep")
    pieces = group_size(square)
    unit = 16 * pieces
    reduce_rows = -(-(offsets * chans + HEAD_ROWS) // unit) * unit
    height = reduce_rows // pieces

    even_y, odd_y, even_x, odd_x = outgoing(send_rows, features)
    from_y = swap_edges(even_y, odd_y, "ty")
    from_x = swap_edges(even_x, odd_x, "tx")

    zero_row = voxels + 4 * width
    moved = jnp.where(neighbour_map > voxels, neighbour_map - 1, neighbour_map)
    moved = jnp.where(neighbour_map == voxels, zero_row, moved)
    map_flat = moved.reshape(-1)
    sparse = (
        moved[offsets - BY_MATMUL :].reshape(BY_MATMUL, STREAMS, voxels // block, SEGMENT)
        .transpose(2, 0, 1, 3).reshape(voxels // block, BY_MATMUL, block)
    )
    weights = conv_weight.reshape(offsets * chans, chans)
    class_t = jnp.pad(classifier.T, ((0, HEAD_ROWS - classes), (0, 0)))
    label_blocks = (
        jnp.minimum(labels, classes).reshape(STREAMS, voxels // block, SEGMENT).transpose(1, 0, 2)
        .reshape(voxels // block, 1, block)
    )
    dpre, dmixed, part, flipped = forward(
        map_flat, sparse, features, from_x, from_y, weights, class_t, label_blocks,
        classes, reduce_rows, table_rows,
    )

    chunks = [(c * offsets // CHUNKS, (c + 1) * offsets // CHUNKS) for c in range(CHUNKS)]

    halo = []

    def scatter_beside(sent, before):
        first, last = chunks.pop(0)
        held = (sent, dpre) if before is None else (sent, dpre, before)
        held = lax.optimization_barrier(held)
        dext, *blocks = scatter(
            map_flat, held[1], flipped, None if before is None else held[2],
            first, last - first, table_rows, width,
        )
        halo.extend(blocks)
        return held[0], dext

    mine = group_index(square)
    sent = []
    for d in range(1, pieces):
        piece = lax.dynamic_slice_in_dim(part, (mine ^ d) * height, height, axis=0)
        sent.append(piece.astype(jnp.bfloat16))
    own = lax.dynamic_slice_in_dim(part, mine * height, height, axis=0)
    (sent, own), dext = scatter_beside((sent, own), None)
    got = [exchange(piece, square, d + 1) for d, piece in enumerate(sent)]
    got, dext = lax.optimization_barrier((got, dext))
    own = own + sum(piece.astype(jnp.float32) for piece in got)

    stride = 1
    while stride < lax.axis_size("tx"):
        radix = min(4, lax.axis_size("tx") // stride)
        own = own.astype(jnp.bfloat16)
        if chunks:
            own, dext = scatter_beside(own, dext)
        got = [own] + [exchange(own, ("tx",), m * stride) for m in range(1, radix)]
        got, dext, halo = lax.optimization_barrier((got, dext, halo))
        got = [piece.astype(jnp.float32) for piece in got]
        while len(got) > 1:
            got = [a + b for a, b in zip(got[::2], got[1::2])]
        own = got[0]
        stride *= radix
    while chunks:
        own, dext = scatter_beside(own, dext)

    from_y = swap_edges(halo[0], halo[1], "ty")
    from_x = swap_edges(halo[2], halo[3], "tx")
    everywhere = {0: own.astype(jnp.bfloat16)}
    bit = pieces // 2
    while bit:
        if bit == 1:
            everywhere, from_x, from_y = lax.optimization_barrier((everywhere, from_x, from_y))
        for d, piece in list(everywhere.items()):
            everywhere[d | bit] = exchange(piece, square, bit)
        bit //= 2
    grad_input = finish(dmixed, dext, send_rows.reshape(1, -1), from_x, from_y)
    everywhere = [everywhere[d] for d in range(pieces)]
    count = voxels * lax.axis_size("tx") * lax.axis_size("ty") * lax.axis_size("rep")
    conv, head = assemble(everywhere, square, 1.0 / math.sqrt(count), offsets * chans, classes)
    return grad_input, conv.reshape(offsets, chans, chans), head.T


def solution(mesh):
    placed = (
        P(("groups", "tx", "ty", "rep"), None),
        P(),
        P(),
        P(("groups", "tx", "ty", "rep"), None),
        P(None, ("groups", "tx", "ty", "rep")),
        P(("groups", "tx", "ty", "rep")),
    )
    return jax.shard_map(
        on_device,
        mesh=mesh,
        in_specs=placed,
        out_specs=(
            P(("groups", "tx", "ty", "rep"), None),
            P("groups", None, None),
            P("groups", None),
        ),
        check_vma=False,
    )
```

```python
import functools
import math

import jax
import jax.numpy as jnp
from jax import lax
from jax.experimental import pallas as pl
from jax.experimental.pallas import tpu as pltpu
from jax.sharding import PartitionSpec as P

STREAMS = 1
SCATTER_STREAMS = 2
SEGMENT = 256
BY_MATMUL = 8
SCATTER_STEPS = 32
FIRST_PART = 512
CHUNKS = 2
HEAD_ROWS = 32
VMEM = pl.BlockSpec(memory_space=pltpu.VMEM)
HBM = pl.BlockSpec(memory_space=pl.ANY)
NN = (((1,), (0,)), ((), ()))
NT = (((1,), (1,)), ((), ()))
TN = (((0,), (0,)), ((), ()))


def dot(a, b, dims):
    return lax.dot_general(a, b, dims, preferred_element_type=jnp.float32)


def from_neighbours(refs, axis):
    odd = (lax.axis_index(axis) & 1) != 0
    first = refs[0][...].astype(jnp.float32)
    second = refs[1][...].astype(jnp.float32) if len(refs) > 1 else jnp.zeros_like(first)
    return jnp.where(odd, first, second), jnp.where(odd, second, first)


def over_edges(down, up, axis):
    odd = (lax.axis_index(axis) & 1) != 0
    return jnp.where(odd, down, up), jnp.where(odd, up, down)


def fetch(map_hbm, index, sems, first, length, parts):
    stages = []
    for part, (start, stop) in enumerate(zip(parts[:-1], parts[1:])):
        stage = []
        for n, ref in enumerate(index):
            at = (first + n) * length + start
            stage.append(
                pltpu.make_async_copy(
                    map_hbm.at[pl.ds(at, stop - start)], ref.at[pl.ds(start, stop - start)],
                    sems.at[part, n],
                )
            )
        for copy in stage:
            copy.start()
        stages.append(stage)
    return stages


def forward_kernel(
    classes, map_hbm, sparse_ref, own_hbm, x_refs, y_refs, weight_hbm, class_ref, label_ref,
    dpre_ref, dmixed_ref, conv_ref, flipped_ref,
    own_ref, weight_ref, load_sems, table, turned, rows, wide, columns, side, total, sems, *index,
):
    voxels, chans = dpre_ref.shape
    looped = len(index) // STREAMS
    offsets = looped + BY_MATMUL
    stream = voxels // STREAMS
    block = STREAMS * SEGMENT
    share = SEGMENT // BY_MATMUL
    own_copy = pltpu.make_async_copy(own_hbm, own_ref, load_sems.at[0])
    own_copy.start()
    weight_copy = pltpu.make_async_copy(weight_hbm, weight_ref, load_sems.at[1])
    weight_copy.start()
    ready, later = fetch(map_hbm, index, sems, 0, stream, (0, FIRST_PART, stream))
    own_copy.wait()
    width = x_refs[0].shape[0]
    table[:voxels, :] = own_ref[...].astype(jnp.float32)
    halos = from_neighbours(x_refs, "tx") + from_neighbours(y_refs, "ty")
    for n, halo in enumerate(halos):
        start = voxels + n * width
        table[start : start + width, :] = halo
    filled = voxels + 4 * width
    table[filled:, :] = jnp.zeros((table.shape[0] - filled, chans), jnp.float32)
    for n in range(filled // chans):
        at = slice(n * chans, (n + 1) * chans)
        turned[:, at] = table[at, :].T.astype(jnp.bfloat16)
    total[...] = jnp.zeros_like(total)
    conv_ref[pl.ds(offsets * chans, conv_ref.shape[0] - offsets * chans), :] = jnp.zeros(
        (conv_ref.shape[0] - offsets * chans, chans), jnp.float32
    )
    weight_copy.wait()
    for k in range(offsets):
        at = slice(k * chans, (k + 1) * chans)
        turned_weight = weight_ref[at, :].T
        flipped_ref[at, :] = turned_weight
        if k >= looped:
            side[:, (k - looped) * chans : (k - looped + 1) * chans] = turned_weight
    for copy in ready:
        copy.wait()

    def block_step(b, carry):
        @pl.when(b == FIRST_PART // SEGMENT)
        def _():
            for copy in later:
                copy.wait()

        def gather_step(j, carry):
            row = lax.broadcasted_iota(jnp.int32, (filled, block), 0)
            chosen = (row == sparse_ref[b, pl.ds(j, 1), :]).astype(jnp.float32)
            at = pl.ds(pl.multiple_of(j * chans, chans), chans)
            columns[at, :] = dot(turned[...], chosen.astype(jnp.bfloat16), NN).astype(jnp.bfloat16)
            for n in range(share):
                to = j * share + n
                i = b * SEGMENT + to
                for u in range(STREAMS):
                    for k in range(looped):
                        rows[k, pl.ds(u * SEGMENT + to, 1), :] = table[
                            pl.ds(index[k * STREAMS + u][i], 1), :
                        ]
            return carry

        lax.fori_loop(0, BY_MATMUL, gather_step, 0)
        for k in range(looped):
            wide[:, k * chans : (k + 1) * chans] = rows[k].astype(jnp.bfloat16)
        pre = dot(wide[...], weight_ref[: looped * chans, :], NN)
        pre = pre + dot(side[...], columns[...], NN).T
        starts = [pl.multiple_of(u * stream + b * SEGMENT, SEGMENT) for u in range(STREAMS)]
        own = jnp.concatenate([table[pl.ds(s, SEGMENT), :] for s in starts], axis=0)
        sig = jax.nn.sigmoid(pre)
        mixed = (own + pre * sig).astype(jnp.bfloat16)
        logits = dot(class_ref[...], mixed, NT)
        which = lax.broadcasted_iota(jnp.int32, logits.shape, 0)
        logits = jnp.where(which < classes, logits, -1e30)
        high = jnp.max(logits, axis=0, keepdims=True)
        expd = jnp.exp(logits - high)
        probs = expd / jnp.sum(expd, axis=0, keepdims=True)
        onehot = (which == label_ref[b]).astype(jnp.float32)
        dlogits = (probs - onehot).astype(jnp.bfloat16)
        conv_ref[pl.ds(offsets * chans, HEAD_ROWS), :] += dot(dlogits, mixed, NN)
        dmixed = dot(dlogits, class_ref[...], TN)
        dpre = (dmixed * sig * (1.0 + pre * (1.0 - sig))).astype(jnp.bfloat16)
        full = dpre.astype(jnp.float32)
        for u, s in enumerate(starts):
            dmixed_ref[pl.ds(s, SEGMENT), :] = dmixed[u * SEGMENT : (u + 1) * SEGMENT]
            dpre_ref[pl.ds(s, SEGMENT), :] = full[u * SEGMENT : (u + 1) * SEGMENT]
        full_t = full.T.astype(jnp.bfloat16)
        total[:, : looped * chans] += dot(full_t, wide[...], NN)
        total[:, looped * chans :] += dot(full_t, columns[...], NT)
        return carry

    lax.fori_loop(0, voxels // block, block_step, 0)
    for k in range(offsets):
        conv_ref[k * chans : (k + 1) * chans, :] = total[:, k * chans : (k + 1) * chans].T


def forward(map_flat, sparse, features, from_x, from_y, weights, class_t, label_blocks, classes, reduce_rows, table_rows):
    voxels, chans = features.shape
    offsets = weights.shape[0] // chans
    looped = offsets - BY_MATMUL
    stream = voxels // STREAMS
    block = STREAMS * SEGMENT
    filled = voxels + 4 * from_x[0].shape[0]
    return pl.pallas_call(
        functools.partial(forward_kernel, classes),
        out_shape=(
            jax.ShapeDtypeStruct((voxels, chans), jnp.float32),
            jax.ShapeDtypeStruct((voxels, chans), jnp.float32),
            jax.ShapeDtypeStruct((reduce_rows, chans), jnp.float32),
            jax.ShapeDtypeStruct(weights.shape, jnp.bfloat16),
        ),
        in_specs=[HBM, VMEM, HBM, [VMEM] * len(from_x), [VMEM] * len(from_y), HBM, VMEM, VMEM],
        out_specs=(VMEM, VMEM, VMEM, VMEM),
        scratch_shapes=[
            pltpu.VMEM(features.shape, jnp.bfloat16),
            pltpu.VMEM(weights.shape, jnp.bfloat16),
            pltpu.SemaphoreType.DMA((2,)),
            pltpu.VMEM((table_rows, chans), jnp.float32),
            pltpu.VMEM((chans, filled), jnp.bfloat16),
            pltpu.VMEM((looped, block, chans), jnp.float32),
            pltpu.VMEM((block, looped * chans), jnp.bfloat16),
            pltpu.VMEM((BY_MATMUL * chans, block), jnp.bfloat16),
            pltpu.VMEM((chans, BY_MATMUL * chans), jnp.bfloat16),
            pltpu.VMEM((chans, offsets * chans), jnp.float32),
            pltpu.SemaphoreType.DMA((2, looped * STREAMS)),
        ]
        + [pltpu.SMEM((stream,), jnp.int32)] * (looped * STREAMS),
        compiler_params=pltpu.CompilerParams(vmem_limit_bytes=17 << 20),
        name="forward",
    )(map_flat, sparse, features, from_x, from_y, weights, class_t, label_blocks)


def scatter_kernel(first, offsets, has_before, map_hbm, dpre_ref, weight_ref, *refs):
    refs = list(refs)
    before = refs.pop(0) if has_before else None
    out_ref = refs.pop(0)
    back_refs = [refs.pop(0) for _ in range(4)] if has_before else []
    sems = refs.pop(0)
    tables = refs[:offsets]
    index = refs[offsets:]
    streams, stream, chans = dpre_ref.shape
    share = stream // SCATTER_STEPS
    part = stream // 4
    ready, later = fetch(map_hbm, index, sems, first * streams, stream, (0, part, stream))
    for table in tables:
        table[...] = jnp.zeros_like(table)
    for copy in ready:
        copy.wait()

    def step(j, carry):
        for n in range(share):
            i = j * share + n
            for u in range(streams):
                value = dpre_ref[u, pl.ds(i, 1), :]
                for k in range(offsets):
                    where = pl.ds(index[k * streams + u][i], 1)
                    tables[k][where, :] = tables[k][where, :] + value
        return carry

    lax.fori_loop(0, SCATTER_STEPS // 4, step, 0)
    for copy in later:
        copy.wait()
    lax.fori_loop(SCATTER_STEPS // 4, SCATTER_STEPS, step, 0)
    tiles = 3
    height = out_ref.shape[0] // tiles

    def finish(t, carry):
        at = pl.ds(pl.multiple_of(t * height, 16), height)
        wide = jnp.concatenate([table[at, :].astype(jnp.bfloat16) for table in tables], axis=1)
        result = dot(wide, weight_ref[first * chans : (first + offsets) * chans, :], NN)
        out_ref[at, :] = result + before[at, :] if has_before else result
        return carry

    lax.fori_loop(0, tiles, finish, 0)
    if back_refs:
        width = back_refs[0].shape[0]
        voxels = streams * stream
        halos = [out_ref[voxels + n * width : voxels + (n + 1) * width, :] for n in range(4)]
        picked = over_edges(halos[2], halos[3], "ty") + over_edges(halos[0], halos[1], "tx")
        for back_ref, value in zip(back_refs, picked):
            back_ref[...] = value.astype(jnp.bfloat16)


def scatter(map_flat, dpre, flipped, before, first, offsets, table_rows, width):
    voxels, chans = dpre.shape
    stream = voxels // SCATTER_STREAMS
    has_before = before is not None
    return pl.pallas_call(
        functools.partial(scatter_kernel, first, offsets, has_before),
        out_shape=[jax.ShapeDtypeStruct((table_rows, chans), jnp.float32)]
        + [jax.ShapeDtypeStruct((width, chans), jnp.bfloat16)] * (4 if has_before else 0),
        in_specs=[HBM, VMEM, VMEM] + ([VMEM] if has_before else []),
        out_specs=[VMEM] * (5 if has_before else 1),
        scratch_shapes=[
            pltpu.SemaphoreType.DMA((2, offsets * SCATTER_STREAMS)),
        ]
        + [pltpu.VMEM((table_rows, chans), jnp.float32)] * offsets
        + [pltpu.SMEM((stream,), jnp.int32)] * (offsets * SCATTER_STREAMS),
        compiler_params=pltpu.CompilerParams(vmem_limit_bytes=21 << 20),
        cost_estimate=pl.CostEstimate(
            flops=2 * voxels * offsets * chans * chans, bytes_accessed=40 << 20, transcendentals=0
        ),
        name=f"scatter_{first}",
    )(
        map_flat, dpre.reshape(SCATTER_STREAMS, stream, chans), flipped,
        *([before] if has_before else []),
    )


def finish_kernel(dmixed_ref, dext_ref, send_ref, x_refs, y_refs, out_ref, back_ref):
    voxels, chans = out_ref.shape
    width = x_refs[0].shape[0]
    low_x, high_x = from_neighbours(x_refs, "tx")
    low_y, high_y = from_neighbours(y_refs, "ty")
    for n, value in enumerate((high_x, low_x, high_y, low_y)):
        back_ref[n * width : (n + 1) * width, :] = value.astype(jnp.bfloat16)
    height = voxels // 2

    def step(t, carry):
        at = pl.ds(pl.multiple_of(t * height, height), height)
        row = lax.broadcasted_iota(jnp.int32, (height, send_ref.shape[1]), 0) + t * height
        chosen = (row == send_ref[...]).astype(jnp.float32).astype(jnp.bfloat16)
        out_ref[at, :] = dmixed_ref[at, :] + dext_ref[at, :] + dot(chosen, back_ref[...], NN)
        return carry

    lax.fori_loop(0, voxels // height, step, 0)


def finish(dmixed, dext, send_flat, from_x, from_y):
    return pl.pallas_call(
        finish_kernel,
        out_shape=jax.ShapeDtypeStruct(dmixed.shape, jnp.float32),
        in_specs=[VMEM, VMEM, VMEM, [VMEM] * len(from_x), [VMEM] * len(from_y)],
        out_specs=VMEM,
        scratch_shapes=[pltpu.VMEM((send_flat.shape[1], dmixed.shape[1]), jnp.bfloat16)],
        compiler_params=pltpu.CompilerParams(vmem_limit_bytes=12 << 20),
        cost_estimate=pl.CostEstimate(flops=1 << 28, bytes_accessed=4 << 20, transcendentals=0),
        name="finish",
    )(dmixed, dext, send_flat, from_x, from_y)


def outgoing_kernel(axes, send_hbm, own_hbm, *refs):
    *out_refs, send_ref, own_ref, sems, table, sent = refs
    voxels, chans = own_ref.shape
    send_copy = pltpu.make_async_copy(send_hbm, send_ref, sems.at[0])
    send_copy.start()
    own_copy = pltpu.make_async_copy(own_hbm, own_ref, sems.at[1])
    own_copy.start()
    own_copy.wait()
    width = send_ref.shape[1]
    table[:voxels, :] = own_ref[...].astype(jnp.float32)
    table[voxels:, :] = jnp.zeros((table.shape[0] - voxels, chans), jnp.float32)
    send_copy.wait()
    for s in range(4):

        def step(t, carry, s=s):
            for n in range(32):
                i = t * 32 + n
                sent[pl.ds(s * width + i, 1), :] = table[pl.ds(send_ref[s, i], 1), :]
            return carry

        lax.fori_loop(0, width // 32, step, 0)
    lists = [sent[s * width : (s + 1) * width, :] for s in range(4)]
    picked = []
    for axis, (up, down) in zip(axes, ((2, 3), (0, 1))):
        picked.extend(over_edges(lists[down], lists[up], axis))
    for out_ref, value in zip(out_refs, picked):
        out_ref[...] = value.astype(jnp.bfloat16)


def outgoing(send_rows, features):
    voxels, chans = features.shape
    width = send_rows.shape[1]
    return pl.pallas_call(
        functools.partial(outgoing_kernel, ("ty", "tx")),
        out_shape=[jax.ShapeDtypeStruct((width, chans), jnp.bfloat16)] * 4,
        in_specs=[HBM, HBM],
        out_specs=[VMEM] * 4,
        scratch_shapes=[
            pltpu.SMEM(send_rows.shape, jnp.int32),
            pltpu.VMEM(features.shape, jnp.bfloat16),
            pltpu.SemaphoreType.DMA((2,)),
            pltpu.VMEM((voxels + 8, chans), jnp.float32),
            pltpu.VMEM((4 * width, chans), jnp.float32),
        ],
        compiler_params=pltpu.CompilerParams(vmem_limit_bytes=60 << 20),
        cost_estimate=pl.CostEstimate(flops=0, bytes_accessed=8 << 20, transcendentals=0),
        name="outgoing",
    )(send_rows, features)


def assemble_kernel(axes, scale, conv_rows, *refs):
    *piece_refs, conv_ref, head_ref = refs
    pieces = len(piece_refs)
    height = piece_refs[0].shape[0]
    mine = group_index(axes)
    for d, piece_ref in enumerate(piece_refs):
        for p in range(pieces):

            @pl.when((mine ^ d) == p)
            def _(p=p, piece_ref=piece_ref):
                start = p * height
                inside = max(0, min(height, conv_rows - start))
                if inside:
                    value = piece_ref[:inside, :].astype(jnp.float32) * scale
                    conv_ref[start : start + inside, :] = value
                if start <= conv_rows < start + height:
                    at = conv_rows - start
                    value = piece_ref[at : at + HEAD_ROWS, :].astype(jnp.float32) * scale
                    head_ref[...] = value[: head_ref.shape[0], :]


def assemble(pieces, axes, scale, conv_rows, classes):
    chans = pieces[0].shape[1]
    return pl.pallas_call(
        functools.partial(assemble_kernel, axes, scale, conv_rows),
        out_shape=(
            jax.ShapeDtypeStruct((conv_rows, chans), jnp.float32),
            jax.ShapeDtypeStruct((classes, chans), jnp.float32),
        ),
        in_specs=[VMEM] * len(pieces),
        out_specs=(VMEM, VMEM),
        compiler_params=pltpu.CompilerParams(vmem_limit_bytes=12 << 20),
        name="assemble",
    )(*pieces)


def group_index(axes):
    at = 0
    for axis in axes:
        at = at * lax.axis_size(axis) + lax.axis_index(axis)
    return at


def group_size(axes):
    return math.prod(lax.axis_size(axis) for axis in axes)


def exchange(shard, axes, distance):
    return lax.ppermute(shard, axes, [(i, i ^ distance) for i in range(group_size(axes))])


def edge_pairs(axis):
    devices = lax.axis_size(axis)
    even = [(i, i ^ 1) for i in range(devices) if (i ^ 1) < devices]
    odd = [(i, ((i + 1) ^ 1) - 1) for i in range(1, devices) if ((i + 1) ^ 1) - 1 < devices]
    return even, odd


def swap_edges(over_even, over_odd, axis):
    even_pairs, odd_pairs = edge_pairs(axis)
    got = [lax.ppermute(over_even, axis, even_pairs)]
    if odd_pairs:
        got.append(lax.ppermute(over_odd, axis, odd_pairs))
    return got


def on_device(features, conv_weight, classifier, send_rows, neighbour_map, labels):
    voxels, chans = features.shape
    width = send_rows.shape[1]
    offsets = conv_weight.shape[0]
    classes = classifier.shape[1]
    block = STREAMS * SEGMENT
    table_rows = -(-(voxels + 4 * width + 1) // 48) * 48
    square = ("ty", "rep")
    pieces = group_size(square)
    unit = 16 * pieces
    reduce_rows = -(-(offsets * chans + HEAD_ROWS) // unit) * unit
    height = reduce_rows // pieces

    even_y, odd_y, even_x, odd_x = outgoing(send_rows, features)
    from_y = swap_edges(even_y, odd_y, "ty")
    from_x = swap_edges(even_x, odd_x, "tx")

    zero_row = voxels + 4 * width
    moved = jnp.where(neighbour_map > voxels, neighbour_map - 1, neighbour_map)
    moved = jnp.where(neighbour_map == voxels, zero_row, moved)
    map_flat = moved.reshape(-1)
    sparse = (
        moved[offsets - BY_MATMUL :].reshape(BY_MATMUL, STREAMS, voxels // block, SEGMENT)
        .transpose(2, 0, 1, 3).reshape(voxels // block, BY_MATMUL, block)
    )
    weights = conv_weight.reshape(offsets * chans, chans)
    class_t = jnp.pad(classifier.T, ((0, HEAD_ROWS - classes), (0, 0)))
    label_blocks = (
        jnp.minimum(labels, classes).reshape(STREAMS, voxels // block, SEGMENT).transpose(1, 0, 2)
        .reshape(voxels // block, 1, block)
    )
    dpre, dmixed, part, flipped = forward(
        map_flat, sparse, features, from_x, from_y, weights, class_t, label_blocks,
        classes, reduce_rows, table_rows,
    )

    chunks = [(c * offsets // CHUNKS, (c + 1) * offsets // CHUNKS) for c in range(CHUNKS)]

    halo = []

    def scatter_beside(sent, before):
        first, last = chunks.pop(0)
        held = (sent, dpre) if before is None else (sent, dpre, before)
        held = lax.optimization_barrier(held)
        dext, *blocks = scatter(
            map_flat, held[1], flipped, None if before is None else held[2],
            first, last - first, table_rows, width,
        )
        halo.extend(blocks)
        return held[0], dext

    mine = group_index(square)
    sent = []
    for d in range(1, pieces):
        piece = lax.dynamic_slice_in_dim(part, (mine ^ d) * height, height, axis=0)
        sent.append(piece.astype(jnp.bfloat16))
    own = lax.dynamic_slice_in_dim(part, mine * height, height, axis=0)
    (sent, own), dext = scatter_beside((sent, own), None)
    got = [exchange(piece, square, d + 1) for d, piece in enumerate(sent)]
    got, dext = lax.optimization_barrier((got, dext))
    own = own + sum(piece.astype(jnp.float32) for piece in got)

    stride = 1
    while stride < lax.axis_size("tx"):
        radix = min(4, lax.axis_size("tx") // stride)
        own = own.astype(jnp.bfloat16)
        if chunks:
            own, dext = scatter_beside(own, dext)
        got = [own] + [exchange(own, ("tx",), m * stride) for m in range(1, radix)]
        got, dext, halo = lax.optimization_barrier((got, dext, halo))
        got = [piece.astype(jnp.float32) for piece in got]
        while len(got) > 1:
            got = [a + b for a, b in zip(got[::2], got[1::2])]
        own = got[0]
        stride *= radix
    while chunks:
        own, dext = scatter_beside(own, dext)

    from_y = swap_edges(halo[0], halo[1], "ty")
    from_x = swap_edges(halo[2], halo[3], "tx")
    everywhere = {0: own.astype(jnp.bfloat16)}
    bit = pieces // 2
    while bit:
        if bit == 1:
            everywhere, from_x, from_y = lax.optimization_barrier((everywhere, from_x, from_y))
        for d, piece in list(everywhere.items()):
            everywhere[d | bit] = exchange(piece, square, bit)
        bit //= 2
    grad_input = finish(dmixed, dext, send_rows.reshape(1, -1), from_x, from_y)
    everywhere = [everywhere[d] for d in range(pieces)]
    count = voxels * lax.axis_size("tx") * lax.axis_size("ty") * lax.axis_size("rep")
    conv, head = assemble(everywhere, square, 1.0 / math.sqrt(count), offsets * chans, classes)
    return grad_input, conv.reshape(offsets, chans, chans), head.T


def solution(mesh):
    placed = (
        P(("groups", "tx", "ty", "rep"), None),
        P(),
        P(),
        P(("groups", "tx", "ty", "rep"), None),
        P(None, ("groups", "tx", "ty", "rep")),
        P(("groups", "tx", "ty", "rep")),
    )
    return jax.shard_map(
        on_device,
        mesh=mesh,
        in_specs=placed,
        out_specs=(
            P(("groups", "tx", "ty", "rep"), None),
            P("groups", None, None),
            P("groups", None),
        ),
        check_vma=False,
    )
```

```python
import functools
import math

import jax
import jax.numpy as jnp
from jax import lax
from jax.experimental import pallas as pl
from jax.experimental.pallas import tpu as pltpu
from jax.sharding import PartitionSpec as P

STREAMS = 1
SCATTER_STREAMS = 2
SEGMENT = 256
BY_MATMUL = 8
SCATTER_STEPS = 32
STEPS_BEFORE = 24
FIRST_PART = 512
CHUNKS = 2
HEAD_ROWS = 32
VMEM = pl.BlockSpec(memory_space=pltpu.VMEM)
HBM = pl.BlockSpec(memory_space=pl.ANY)
NN = (((1,), (0,)), ((), ()))
NT = (((1,), (1,)), ((), ()))
TN = (((0,), (0,)), ((), ()))


def dot(a, b, dims):
    return lax.dot_general(a, b, dims, preferred_element_type=jnp.float32)


def from_neighbours(refs, axis):
    odd = (lax.axis_index(axis) & 1) != 0
    first = refs[0][...].astype(jnp.float32)
    second = refs[1][...].astype(jnp.float32) if len(refs) > 1 else jnp.zeros_like(first)
    return jnp.where(odd, first, second), jnp.where(odd, second, first)


def over_edges(down, up, axis):
    odd = (lax.axis_index(axis) & 1) != 0
    return jnp.where(odd, down, up), jnp.where(odd, up, down)


def fetch(map_hbm, index, sems, first, length, parts):
    stages = []
    for part, (start, stop) in enumerate(zip(parts[:-1], parts[1:])):
        stage = []
        for n, ref in enumerate(index):
            at = (first + n) * length + start
            stage.append(
                pltpu.make_async_copy(
                    map_hbm.at[pl.ds(at, stop - start)], ref.at[pl.ds(start, stop - start)],
                    sems.at[part, n],
                )
            )
        for copy in stage:
            copy.start()
        stages.append(stage)
    return stages


def forward_kernel(
    classes, map_hbm, sparse_ref, own_hbm, x_refs, y_refs, weight_hbm, class_ref, label_ref,
    dpre_ref, dmixed_ref, conv_ref, flipped_ref,
    own_ref, weight_ref, load_sems, table, turned, rows, wide, columns, side, total, sems, *index,
):
    voxels, chans = dpre_ref.shape
    looped = len(index) // STREAMS
    offsets = looped + BY_MATMUL
    stream = voxels // STREAMS
    block = STREAMS * SEGMENT
    share = SEGMENT // BY_MATMUL
    own_copy = pltpu.make_async_copy(own_hbm, own_ref, load_sems.at[0])
    own_copy.start()
    weight_copy = pltpu.make_async_copy(weight_hbm, weight_ref, load_sems.at[1])
    weight_copy.start()
    ready, later = fetch(map_hbm, index, sems, 0, stream, (0, FIRST_PART, stream))
    own_copy.wait()
    width = x_refs[0].shape[0]
    table[:voxels, :] = own_ref[...].astype(jnp.float32)
    halos = from_neighbours(x_refs, "tx") + from_neighbours(y_refs, "ty")
    for n, halo in enumerate(halos):
        start = voxels + n * width
        table[start : start + width, :] = halo
    filled = voxels + 4 * width
    table[filled:, :] = jnp.zeros((table.shape[0] - filled, chans), jnp.float32)
    for n in range(filled // chans):
        at = slice(n * chans, (n + 1) * chans)
        turned[:, at] = table[at, :].T.astype(jnp.bfloat16)
    total[...] = jnp.zeros_like(total)
    conv_ref[pl.ds(offsets * chans, conv_ref.shape[0] - offsets * chans), :] = jnp.zeros(
        (conv_ref.shape[0] - offsets * chans, chans), jnp.float32
    )
    weight_copy.wait()
    for k in range(offsets):
        at = slice(k * chans, (k + 1) * chans)
        turned_weight = weight_ref[at, :].T
        flipped_ref[at, :] = turned_weight
        if k >= looped:
            side[:, (k - looped) * chans : (k - looped + 1) * chans] = turned_weight
    for copy in ready:
        copy.wait()

    def block_step(b, carry):
        @pl.when(b == FIRST_PART // SEGMENT)
        def _():
            for copy in later:
                copy.wait()

        def gather_step(j, carry):
            row = lax.broadcasted_iota(jnp.int32, (filled, block), 0)
            chosen = (row == sparse_ref[b, pl.ds(j, 1), :]).astype(jnp.float32)
            at = pl.ds(pl.multiple_of(j * chans, chans), chans)
            columns[at, :] = dot(turned[...], chosen.astype(jnp.bfloat16), NN).astype(jnp.bfloat16)
            for n in range(share):
                to = j * share + n
                i = b * SEGMENT + to
                for u in range(STREAMS):
                    for k in range(looped):
                        rows[k, pl.ds(u * SEGMENT + to, 1), :] = table[
                            pl.ds(index[k * STREAMS + u][i], 1), :
                        ]
            return carry

        lax.fori_loop(0, BY_MATMUL, gather_step, 0)
        for k in range(looped):
            wide[:, k * chans : (k + 1) * chans] = rows[k].astype(jnp.bfloat16)
        pre = dot(wide[...], weight_ref[: looped * chans, :], NN)
        pre = pre + dot(side[...], columns[...], NN).T
        starts = [pl.multiple_of(u * stream + b * SEGMENT, SEGMENT) for u in range(STREAMS)]
        own = jnp.concatenate([table[pl.ds(s, SEGMENT), :] for s in starts], axis=0)
        sig = jax.nn.sigmoid(pre)
        mixed = (own + pre * sig).astype(jnp.bfloat16)
        logits = dot(class_ref[...], mixed, NT)
        which = lax.broadcasted_iota(jnp.int32, logits.shape, 0)
        logits = jnp.where(which < classes, logits, -1e30)
        high = jnp.max(logits, axis=0, keepdims=True)
        expd = jnp.exp(logits - high)
        probs = expd / jnp.sum(expd, axis=0, keepdims=True)
        onehot = (which == label_ref[b]).astype(jnp.float32)
        dlogits = (probs - onehot).astype(jnp.bfloat16)
        conv_ref[pl.ds(offsets * chans, HEAD_ROWS), :] += dot(dlogits, mixed, NN)
        dmixed = dot(dlogits, class_ref[...], TN)
        dpre = (dmixed * sig * (1.0 + pre * (1.0 - sig))).astype(jnp.bfloat16)
        full = dpre.astype(jnp.float32)
        for u, s in enumerate(starts):
            dmixed_ref[pl.ds(s, SEGMENT), :] = dmixed[u * SEGMENT : (u + 1) * SEGMENT]
            dpre_ref[pl.ds(s, SEGMENT), :] = full[u * SEGMENT : (u + 1) * SEGMENT]
        full_t = full.T.astype(jnp.bfloat16)
        total[:, : looped * chans] += dot(full_t, wide[...], NN)
        total[:, looped * chans :] += dot(full_t, columns[...], NT)
        return carry

    lax.fori_loop(0, voxels // block, block_step, 0)
    for k in range(offsets):
        conv_ref[k * chans : (k + 1) * chans, :] = total[:, k * chans : (k + 1) * chans].T


def forward(map_flat, sparse, features, from_x, from_y, weights, class_t, label_blocks, classes, reduce_rows, table_rows):
    voxels, chans = features.shape
    offsets = weights.shape[0] // chans
    looped = offsets - BY_MATMUL
    stream = voxels // STREAMS
    block = STREAMS * SEGMENT
    filled = voxels + 4 * from_x[0].shape[0]
    return pl.pallas_call(
        functools.partial(forward_kernel, classes),
        out_shape=(
            jax.ShapeDtypeStruct((voxels, chans), jnp.float32),
            jax.ShapeDtypeStruct((voxels, chans), jnp.float32),
            jax.ShapeDtypeStruct((reduce_rows, chans), jnp.float32),
            jax.ShapeDtypeStruct(weights.shape, jnp.bfloat16),
        ),
        in_specs=[HBM, VMEM, HBM, [VMEM] * len(from_x), [VMEM] * len(from_y), HBM, VMEM, VMEM],
        out_specs=(VMEM, VMEM, VMEM, VMEM),
        scratch_shapes=[
            pltpu.VMEM(features.shape, jnp.bfloat16),
            pltpu.VMEM(weights.shape, jnp.bfloat16),
            pltpu.SemaphoreType.DMA((2,)),
            pltpu.VMEM((table_rows, chans), jnp.float32),
            pltpu.VMEM((chans, filled), jnp.bfloat16),
            pltpu.VMEM((looped, block, chans), jnp.float32),
            pltpu.VMEM((block, looped * chans), jnp.bfloat16),
            pltpu.VMEM((BY_MATMUL * chans, block), jnp.bfloat16),
            pltpu.VMEM((chans, BY_MATMUL * chans), jnp.bfloat16),
            pltpu.VMEM((chans, offsets * chans), jnp.float32),
            pltpu.SemaphoreType.DMA((2, looped * STREAMS)),
        ]
        + [pltpu.SMEM((stream,), jnp.int32)] * (looped * STREAMS),
        compiler_params=pltpu.CompilerParams(vmem_limit_bytes=17 << 20),
        name="forward",
    )(map_flat, sparse, features, from_x, from_y, weights, class_t, label_blocks)


def add_rows(tables, index, dpre_ref, low, high):
    offsets = len(tables)
    streams, stream, chans = dpre_ref.shape
    share = stream // SCATTER_STEPS

    def step(j, carry):
        for n in range(share):
            i = j * share + n
            for u in range(streams):
                value = dpre_ref[u, pl.ds(i, 1), :]
                for k in range(offsets):
                    where = pl.ds(index[k * streams + u][i], 1)
                    tables[k][where, :] = tables[k][where, :] + value
        return carry

    lax.fori_loop(low, high, step, 0)


def open_kernel(first, steps, map_hbm, dpre_ref, *refs):
    streams, stream, chans = dpre_ref.shape
    offsets = len(refs) // (1 + streams)
    tables, sems, index = refs[:offsets], refs[offsets], refs[offsets + 1 :]
    parts = (0, stream // 4, stream * steps // SCATTER_STEPS)
    ready, later = fetch(map_hbm, index, sems, first * streams, stream, parts)
    for table in tables:
        table[...] = jnp.zeros_like(table)
    for copy in ready:
        copy.wait()
    add_rows(tables, index, dpre_ref, 0, SCATTER_STEPS // 4)
    for copy in later:
        copy.wait()
    add_rows(tables, index, dpre_ref, SCATTER_STEPS // 4, steps)


def close_kernel(first, offsets, steps, has_before, map_hbm, dpre_ref, weight_ref, *refs):
    refs = list(refs)
    before = refs.pop(0) if has_before else None
    streams, stream, chans = dpre_ref.shape
    given = steps > 0
    if given:
        refs = refs[offsets:]
    out_ref = refs.pop(0)
    back_refs = [refs.pop(0) for _ in range(4)] if has_before else []
    if given:
        tables = refs[:offsets]
        refs = refs[offsets:]
    sems = refs.pop(0)
    if not given:
        tables = refs[:offsets]
        refs = refs[offsets:]
    index = refs
    low = stream * steps // SCATTER_STEPS
    middle = steps + (SCATTER_STEPS - steps) // (2 if given else 4)
    parts = (low, stream * middle // SCATTER_STEPS, stream)
    ready, later = fetch(map_hbm, index, sems, first * streams, stream, parts)
    if not given:
        for table in tables:
            table[...] = jnp.zeros_like(table)
    for copy in ready:
        copy.wait()
    add_rows(tables, index, dpre_ref, steps, middle)
    for copy in later:
        copy.wait()
    add_rows(tables, index, dpre_ref, middle, SCATTER_STEPS)
    tiles = 3
    height = out_ref.shape[0] // tiles

    def finish(t, carry):
        at = pl.ds(pl.multiple_of(t * height, 16), height)
        wide = jnp.concatenate([table[at, :].astype(jnp.bfloat16) for table in tables], axis=1)
        result = dot(wide, weight_ref[first * chans : (first + offsets) * chans, :], NN)
        out_ref[at, :] = result + before[at, :] if has_before else result
        return carry

    lax.fori_loop(0, tiles, finish, 0)
    if back_refs:
        width = back_refs[0].shape[0]
        voxels = streams * stream
        halos = [out_ref[voxels + n * width : voxels + (n + 1) * width, :] for n in range(4)]
        picked = over_edges(halos[2], halos[3], "ty") + over_edges(halos[0], halos[1], "tx")
        for back_ref, value in zip(back_refs, picked):
            back_ref[...] = value.astype(jnp.bfloat16)


def scatter_open(map_flat, dpre, first, offsets, table_rows):
    voxels, chans = dpre.shape
    stream = voxels // SCATTER_STREAMS
    return pl.pallas_call(
        functools.partial(open_kernel, first, STEPS_BEFORE),
        out_shape=[jax.ShapeDtypeStruct((table_rows, chans), jnp.float32)] * offsets,
        in_specs=[HBM, VMEM],
        out_specs=[VMEM] * offsets,
        scratch_shapes=[pltpu.SemaphoreType.DMA((2, offsets * SCATTER_STREAMS))]
        + [pltpu.SMEM((stream,), jnp.int32)] * (offsets * SCATTER_STREAMS),
        compiler_params=pltpu.CompilerParams(vmem_limit_bytes=8 << 20),
        cost_estimate=pl.CostEstimate(flops=0, bytes_accessed=40 << 20, transcendentals=0),
        name=f"scatter_open_{first}",
    )(map_flat, dpre.reshape(SCATTER_STREAMS, stream, chans))


def scatter(map_flat, dpre, flipped, before, first, offsets, table_rows, width, tables=()):
    voxels, chans = dpre.shape
    stream = voxels // SCATTER_STREAMS
    has_before = before is not None
    steps = STEPS_BEFORE if tables else 0
    outs = 5 if has_before else 1
    table_shape = jax.ShapeDtypeStruct((table_rows, chans), jnp.float32)
    result = pl.pallas_call(
        functools.partial(close_kernel, first, offsets, steps, has_before),
        out_shape=[table_shape]
        + [jax.ShapeDtypeStruct((width, chans), jnp.bfloat16)] * (outs - 1)
        + [table_shape] * len(tables),
        in_specs=[HBM, VMEM, VMEM] + ([VMEM] if has_before else []) + [VMEM] * len(tables),
        out_specs=[VMEM] * (outs + len(tables)),
        scratch_shapes=[pltpu.SemaphoreType.DMA((2, offsets * SCATTER_STREAMS))]
        + ([] if tables else [pltpu.VMEM((table_rows, chans), jnp.float32)] * offsets)
        + [pltpu.SMEM((stream,), jnp.int32)] * (offsets * SCATTER_STREAMS),
        input_output_aliases={
            3 + has_before + n: outs + n for n in range(len(tables))
        },
        compiler_params=pltpu.CompilerParams(vmem_limit_bytes=(8 if tables else 21) << 20),
        cost_estimate=pl.CostEstimate(
            flops=2 * voxels * offsets * chans * chans, bytes_accessed=20 << 20, transcendentals=0
        ),
        name=f"scatter_{first}",
    )(
        map_flat, dpre.reshape(SCATTER_STREAMS, stream, chans), flipped,
        *([before] if has_before else []), *tables,
    )
    return result[:outs]


def finish_kernel(dmixed_ref, dext_ref, send_ref, x_refs, y_refs, out_ref, back_ref):
    voxels, chans = out_ref.shape
    width = x_refs[0].shape[0]
    low_x, high_x = from_neighbours(x_refs, "tx")
    low_y, high_y = from_neighbours(y_refs, "ty")
    for n, value in enumerate((high_x, low_x, high_y, low_y)):
        back_ref[n * width : (n + 1) * width, :] = value.astype(jnp.bfloat16)
    height = voxels // 2

    def step(t, carry):
        at = pl.ds(pl.multiple_of(t * height, height), height)
        row = lax.broadcasted_iota(jnp.int32, (height, send_ref.shape[1]), 0) + t * height
        chosen = (row == send_ref[...]).astype(jnp.float32).astype(jnp.bfloat16)
        out_ref[at, :] = dmixed_ref[at, :] + dext_ref[at, :] + dot(chosen, back_ref[...], NN)
        return carry

    lax.fori_loop(0, voxels // height, step, 0)


def finish(dmixed, dext, send_flat, from_x, from_y):
    return pl.pallas_call(
        finish_kernel,
        out_shape=jax.ShapeDtypeStruct(dmixed.shape, jnp.float32),
        in_specs=[VMEM, VMEM, VMEM, [VMEM] * len(from_x), [VMEM] * len(from_y)],
        out_specs=VMEM,
        scratch_shapes=[pltpu.VMEM((send_flat.shape[1], dmixed.shape[1]), jnp.bfloat16)],
        compiler_params=pltpu.CompilerParams(vmem_limit_bytes=12 << 20),
        cost_estimate=pl.CostEstimate(flops=1 << 28, bytes_accessed=4 << 20, transcendentals=0),
        name="finish",
    )(dmixed, dext, send_flat, from_x, from_y)


def outgoing_kernel(axes, send_hbm, own_hbm, *refs):
    *out_refs, send_ref, own_ref, sems, table, sent = refs
    voxels, chans = own_ref.shape
    send_copy = pltpu.make_async_copy(send_hbm, send_ref, sems.at[0])
    send_copy.start()
    own_copy = pltpu.make_async_copy(own_hbm, own_ref, sems.at[1])
    own_copy.start()
    own_copy.wait()
    width = send_ref.shape[1]
    table[:voxels, :] = own_ref[...].astype(jnp.float32)
    table[voxels:, :] = jnp.zeros((table.shape[0] - voxels, chans), jnp.float32)
    send_copy.wait()
    for s in range(4):

        def step(t, carry, s=s):
            for n in range(32):
                i = t * 32 + n
                sent[pl.ds(s * width + i, 1), :] = table[pl.ds(send_ref[s, i], 1), :]
            return carry

        lax.fori_loop(0, width // 32, step, 0)
    lists = [sent[s * width : (s + 1) * width, :] for s in range(4)]
    picked = []
    for axis, (up, down) in zip(axes, ((2, 3), (0, 1))):
        picked.extend(over_edges(lists[down], lists[up], axis))
    for out_ref, value in zip(out_refs, picked):
        out_ref[...] = value.astype(jnp.bfloat16)


def outgoing(send_rows, features):
    voxels, chans = features.shape
    width = send_rows.shape[1]
    return pl.pallas_call(
        functools.partial(outgoing_kernel, ("ty", "tx")),
        out_shape=[jax.ShapeDtypeStruct((width, chans), jnp.bfloat16)] * 4,
        in_specs=[HBM, HBM],
        out_specs=[VMEM] * 4,
        scratch_shapes=[
            pltpu.SMEM(send_rows.shape, jnp.int32),
            pltpu.VMEM(features.shape, jnp.bfloat16),
            pltpu.SemaphoreType.DMA((2,)),
            pltpu.VMEM((voxels + 8, chans), jnp.float32),
            pltpu.VMEM((4 * width, chans), jnp.float32),
        ],
        compiler_params=pltpu.CompilerParams(vmem_limit_bytes=60 << 20),
        cost_estimate=pl.CostEstimate(flops=0, bytes_accessed=8 << 20, transcendentals=0),
        name="outgoing",
    )(send_rows, features)


def assemble_kernel(axes, scale, conv_rows, *refs):
    *piece_refs, conv_ref, head_ref = refs
    pieces = len(piece_refs)
    height = piece_refs[0].shape[0]
    mine = group_index(axes)
    for d, piece_ref in enumerate(piece_refs):
        for p in range(pieces):

            @pl.when((mine ^ d) == p)
            def _(p=p, piece_ref=piece_ref):
                start = p * height
                inside = max(0, min(height, conv_rows - start))
                if inside:
                    value = piece_ref[:inside, :].astype(jnp.float32) * scale
                    conv_ref[start : start + inside, :] = value
                if start <= conv_rows < start + height:
                    at = conv_rows - start
                    value = piece_ref[at : at + HEAD_ROWS, :].astype(jnp.float32) * scale
                    head_ref[...] = value[: head_ref.shape[0], :]


def assemble(pieces, axes, scale, conv_rows, classes):
    chans = pieces[0].shape[1]
    return pl.pallas_call(
        functools.partial(assemble_kernel, axes, scale, conv_rows),
        out_shape=(
            jax.ShapeDtypeStruct((conv_rows, chans), jnp.float32),
            jax.ShapeDtypeStruct((classes, chans), jnp.float32),
        ),
        in_specs=[VMEM] * len(pieces),
        out_specs=(VMEM, VMEM),
        compiler_params=pltpu.CompilerParams(vmem_limit_bytes=12 << 20),
        name="assemble",
    )(*pieces)


def group_index(axes):
    at = 0
    for axis in axes:
        at = at * lax.axis_size(axis) + lax.axis_index(axis)
    return at


def group_size(axes):
    return math.prod(lax.axis_size(axis) for axis in axes)


def exchange(shard, axes, distance):
    return lax.ppermute(shard, axes, [(i, i ^ distance) for i in range(group_size(axes))])


def edge_pairs(axis):
    devices = lax.axis_size(axis)
    even = [(i, i ^ 1) for i in range(devices) if (i ^ 1) < devices]
    odd = [(i, ((i + 1) ^ 1) - 1) for i in range(1, devices) if ((i + 1) ^ 1) - 1 < devices]
    return even, odd


def swap_edges(over_even, over_odd, axis):
    even_pairs, odd_pairs = edge_pairs(axis)
    got = [lax.ppermute(over_even, axis, even_pairs)]
    if odd_pairs:
        got.append(lax.ppermute(over_odd, axis, odd_pairs))
    return got


def on_device(features, conv_weight, classifier, send_rows, neighbour_map, labels):
    voxels, chans = features.shape
    width = send_rows.shape[1]
    offsets = conv_weight.shape[0]
    classes = classifier.shape[1]
    block = STREAMS * SEGMENT
    table_rows = -(-(voxels + 4 * width + 1) // 48) * 48
    square = ("ty", "rep")
    pieces = group_size(square)
    unit = 16 * pieces
    reduce_rows = -(-(offsets * chans + HEAD_ROWS) // unit) * unit
    height = reduce_rows // pieces

    even_y, odd_y, even_x, odd_x = outgoing(send_rows, features)
    from_y = swap_edges(even_y, odd_y, "ty")
    from_x = swap_edges(even_x, odd_x, "tx")

    zero_row = voxels + 4 * width
    moved = jnp.where(neighbour_map > voxels, neighbour_map - 1, neighbour_map)
    moved = jnp.where(neighbour_map == voxels, zero_row, moved)
    map_flat = moved.reshape(-1)
    sparse = (
        moved[offsets - BY_MATMUL :].reshape(BY_MATMUL, STREAMS, voxels // block, SEGMENT)
        .transpose(2, 0, 1, 3).reshape(voxels // block, BY_MATMUL, block)
    )
    weights = conv_weight.reshape(offsets * chans, chans)
    class_t = jnp.pad(classifier.T, ((0, HEAD_ROWS - classes), (0, 0)))
    label_blocks = (
        jnp.minimum(labels, classes).reshape(STREAMS, voxels // block, SEGMENT).transpose(1, 0, 2)
        .reshape(voxels // block, 1, block)
    )
    dpre, dmixed, part, flipped = forward(
        map_flat, sparse, features, from_x, from_y, weights, class_t, label_blocks,
        classes, reduce_rows, table_rows,
    )

    chunks = [(c * offsets // CHUNKS, (c + 1) * offsets // CHUNKS) for c in range(CHUNKS)]

    halo = []

    def scatter_beside(sent, before):
        first, last = chunks.pop(0)
        held = (sent, dpre) if before is None else (sent, dpre, before)
        held = lax.optimization_barrier(held)
        dext, *blocks = scatter(
            map_flat, held[1], flipped, None if before is None else held[2],
            first, last - first, table_rows, width,
        )
        halo.extend(blocks)
        return held[0], dext

    mine = group_index(square)
    sent = []
    for d in range(1, pieces):
        piece = lax.dynamic_slice_in_dim(part, (mine ^ d) * height, height, axis=0)
        sent.append(piece.astype(jnp.bfloat16))
    own = lax.dynamic_slice_in_dim(part, mine * height, height, axis=0)
    (sent, own), dext = scatter_beside((sent, own), None)
    got = [exchange(piece, square, d + 1) for d, piece in enumerate(sent)]
    got, dext = lax.optimization_barrier((got, dext))
    own = own + sum(piece.astype(jnp.float32) for piece in got)

    (first, last), = chunks
    own = own.astype(jnp.bfloat16)
    tables = None
    stride = 1
    while stride < lax.axis_size("tx"):
        radix = min(4, lax.axis_size("tx") // stride)
        own = own.astype(jnp.bfloat16)
        if tables is None:
            own, held = lax.optimization_barrier((own, dpre))
            tables = scatter_open(map_flat, held, first, last - first, table_rows)
        got = [own] + [exchange(own, ("tx",), m * stride) for m in range(1, radix)]
        got, tables = lax.optimization_barrier((got, tables))
        got = [piece.astype(jnp.float32) for piece in got]
        while len(got) > 1:
            got = [a + b for a, b in zip(got[::2], got[1::2])]
        own = got[0]
        stride *= radix

    everywhere = {0: own.astype(jnp.bfloat16)}
    bit = pieces // 2
    while bit:
        if bit == 1:
            everywhere[0], tables = lax.optimization_barrier((everywhere[0], tables))
            dext, *halo = scatter(
                map_flat, dpre, flipped, dext, first, last - first, table_rows, width, tables
            )
            everywhere, dext, halo = lax.optimization_barrier((everywhere, dext, halo))
        elif bit == pieces // 2:
            everywhere[0], tables = lax.optimization_barrier((everywhere[0], tables))
        for d, piece in list(everywhere.items()):
            everywhere[d | bit] = exchange(piece, square, bit)
        bit //= 2
    from_y = swap_edges(halo[0], halo[1], "ty")
    from_x = swap_edges(halo[2], halo[3], "tx")
    grad_input = finish(dmixed, dext, send_rows.reshape(1, -1), from_x, from_y)
    everywhere = [everywhere[d] for d in range(pieces)]
    count = voxels * lax.axis_size("tx") * lax.axis_size("ty") * lax.axis_size("rep")
    conv, head = assemble(everywhere, square, 1.0 / math.sqrt(count), offsets * chans, classes)
    return grad_input, conv.reshape(offsets, chans, chans), head.T


def solution(mesh):
    placed = (
        P(("groups", "tx", "ty", "rep"), None),
        P(),
        P(),
        P(("groups", "tx", "ty", "rep"), None),
        P(None, ("groups", "tx", "ty", "rep")),
        P(("groups", "tx", "ty", "rep")),
    )
    return jax.shard_map(
        on_device,
        mesh=mesh,
        in_specs=placed,
        out_specs=(
            P(("groups", "tx", "ty", "rep"), None),
            P("groups", None, None),
            P("groups", None),
        ),
        check_vma=False,
    )
```

```python
import functools
import math

import jax
import jax.numpy as jnp
from jax import lax
from jax.experimental import pallas as pl
from jax.experimental.pallas import tpu as pltpu
from jax.sharding import PartitionSpec as P

STREAMS = 2
SCATTER_STREAMS = 2
SEGMENT = 128
BY_MATMUL = 8
SCATTER_STEPS = 32
FIRST_PART = 256
CHUNKS = 2
HEAD_ROWS = 32
VMEM = pl.BlockSpec(memory_space=pltpu.VMEM)
HBM = pl.BlockSpec(memory_space=pl.ANY)
NN = (((1,), (0,)), ((), ()))
NT = (((1,), (1,)), ((), ()))
TN = (((0,), (0,)), ((), ()))


def dot(a, b, dims):
    return lax.dot_general(a, b, dims, preferred_element_type=jnp.float32)


def from_neighbours(refs, axis):
    odd = (lax.axis_index(axis) & 1) != 0
    first = refs[0][...].astype(jnp.float32)
    second = refs[1][...].astype(jnp.float32) if len(refs) > 1 else jnp.zeros_like(first)
    return jnp.where(odd, first, second), jnp.where(odd, second, first)


def over_edges(down, up, axis):
    odd = (lax.axis_index(axis) & 1) != 0
    return jnp.where(odd, down, up), jnp.where(odd, up, down)


def fetch(map_hbm, index, sems, first, length, parts):
    stages = []
    for part, (start, stop) in enumerate(zip(parts[:-1], parts[1:])):
        stage = []
        for n, ref in enumerate(index):
            at = (first + n) * length + start
            stage.append(
                pltpu.make_async_copy(
                    map_hbm.at[pl.ds(at, stop - start)], ref.at[pl.ds(start, stop - start)],
                    sems.at[part, n],
                )
            )
        for copy in stage:
            copy.start()
        stages.append(stage)
    return stages


def forward_kernel(
    classes, map_hbm, sparse_ref, own_hbm, x_refs, y_refs, weight_hbm, class_ref, label_ref,
    dpre_ref, dmixed_ref, conv_ref, flipped_ref,
    own_ref, weight_ref, load_sems, table, turned, rows, wide, columns, side, total, sems, *index,
):
    voxels, chans = dpre_ref.shape
    looped = len(index) // STREAMS
    offsets = looped + BY_MATMUL
    stream = voxels // STREAMS
    block = STREAMS * SEGMENT
    share = SEGMENT // BY_MATMUL
    own_copy = pltpu.make_async_copy(own_hbm, own_ref, load_sems.at[0])
    own_copy.start()
    weight_copy = pltpu.make_async_copy(weight_hbm, weight_ref, load_sems.at[1])
    weight_copy.start()
    ready, later = fetch(map_hbm, index, sems, 0, stream, (0, FIRST_PART, stream))
    own_copy.wait()
    width = x_refs[0].shape[0]
    table[:voxels, :] = own_ref[...].astype(jnp.float32)
    halos = from_neighbours(x_refs, "tx") + from_neighbours(y_refs, "ty")
    for n, halo in enumerate(halos):
        start = voxels + n * width
        table[start : start + width, :] = halo
    filled = voxels + 4 * width
    table[filled:, :] = jnp.zeros((table.shape[0] - filled, chans), jnp.float32)
    for n in range(filled // chans):
        at = slice(n * chans, (n + 1) * chans)
        turned[:, at] = table[at, :].T.astype(jnp.bfloat16)
    total[...] = jnp.zeros_like(total)
    conv_ref[pl.ds(offsets * chans, conv_ref.shape[0] - offsets * chans), :] = jnp.zeros(
        (conv_ref.shape[0] - offsets * chans, chans), jnp.float32
    )
    weight_copy.wait()
    for k in range(offsets):
        at = slice(k * chans, (k + 1) * chans)
        turned_weight = weight_ref[at, :].T
        flipped_ref[at, :] = turned_weight
        if k >= looped:
            side[:, (k - looped) * chans : (k - looped + 1) * chans] = turned_weight
    for copy in ready:
        copy.wait()

    def block_step(b, carry):
        @pl.when(b == FIRST_PART // SEGMENT)
        def _():
            for copy in later:
                copy.wait()

        def gather_step(j, carry):
            row = lax.broadcasted_iota(jnp.int32, (filled, block), 0)
            chosen = (row == sparse_ref[b, pl.ds(j, 1), :]).astype(jnp.float32)
            at = pl.ds(pl.multiple_of(j * chans, chans), chans)
            columns[at, :] = dot(turned[...], chosen.astype(jnp.bfloat16), NN).astype(jnp.bfloat16)
            for n in range(share):
                to = j * share + n
                i = b * SEGMENT + to
                for u in range(STREAMS):
                    for k in range(looped):
                        rows[k, pl.ds(u * SEGMENT + to, 1), :] = table[
                            pl.ds(index[k * STREAMS + u][i], 1), :
                        ]
            return carry

        lax.fori_loop(0, BY_MATMUL, gather_step, 0)
        for k in range(looped):
            wide[:, k * chans : (k + 1) * chans] = rows[k].astype(jnp.bfloat16)
        pre = dot(wide[...], weight_ref[: looped * chans, :], NN)
        pre = pre + dot(side[...], columns[...], NN).T
        starts = [pl.multiple_of(u * stream + b * SEGMENT, SEGMENT) for u in range(STREAMS)]
        own = jnp.concatenate([table[pl.ds(s, SEGMENT), :] for s in starts], axis=0)
        sig = jax.nn.sigmoid(pre)
        mixed = (own + pre * sig).astype(jnp.bfloat16)
        logits = dot(class_ref[...], mixed, NT)
        which = lax.broadcasted_iota(jnp.int32, logits.shape, 0)
        logits = jnp.where(which < classes, logits, -1e30)
        high = jnp.max(logits, axis=0, keepdims=True)
        expd = jnp.exp(logits - high)
        probs = expd / jnp.sum(expd, axis=0, keepdims=True)
        onehot = (which == label_ref[b]).astype(jnp.float32)
        dlogits = (probs - onehot).astype(jnp.bfloat16)
        conv_ref[pl.ds(offsets * chans, HEAD_ROWS), :] += dot(dlogits, mixed, NN)
        dmixed = dot(dlogits, class_ref[...], TN)
        dpre = (dmixed * sig * (1.0 + pre * (1.0 - sig))).astype(jnp.bfloat16)
        full = dpre.astype(jnp.float32)
        for u, s in enumerate(starts):
            dmixed_ref[pl.ds(s, SEGMENT), :] = dmixed[u * SEGMENT : (u + 1) * SEGMENT]
            dpre_ref[pl.ds(s, SEGMENT), :] = full[u * SEGMENT : (u + 1) * SEGMENT]
        full_t = full.T.astype(jnp.bfloat16)
        total[:, : looped * chans] += dot(full_t, wide[...], NN)
        total[:, looped * chans :] += dot(full_t, columns[...], NT)
        return carry

    lax.fori_loop(0, voxels // block, block_step, 0)
    for k in range(offsets):
        conv_ref[k * chans : (k + 1) * chans, :] = total[:, k * chans : (k + 1) * chans].T


def forward(map_flat, sparse, features, from_x, from_y, weights, class_t, label_blocks, classes, reduce_rows, table_rows):
    voxels, chans = features.shape
    offsets = weights.shape[0] // chans
    looped = offsets - BY_MATMUL
    stream = voxels // STREAMS
    block = STREAMS * SEGMENT
    filled = voxels + 4 * from_x[0].shape[0]
    return pl.pallas_call(
        functools.partial(forward_kernel, classes),
        out_shape=(
            jax.ShapeDtypeStruct((voxels, chans), jnp.float32),
            jax.ShapeDtypeStruct((voxels, chans), jnp.float32),
            jax.ShapeDtypeStruct((reduce_rows, chans), jnp.float32),
            jax.ShapeDtypeStruct(weights.shape, jnp.bfloat16),
        ),
        in_specs=[HBM, VMEM, HBM, [VMEM] * len(from_x), [VMEM] * len(from_y), HBM, VMEM, VMEM],
        out_specs=(VMEM, VMEM, VMEM, VMEM),
        scratch_shapes=[
            pltpu.VMEM(features.shape, jnp.bfloat16),
            pltpu.VMEM(weights.shape, jnp.bfloat16),
            pltpu.SemaphoreType.DMA((2,)),
            pltpu.VMEM((table_rows, chans), jnp.float32),
            pltpu.VMEM((chans, filled), jnp.bfloat16),
            pltpu.VMEM((looped, block, chans), jnp.float32),
            pltpu.VMEM((block, looped * chans), jnp.bfloat16),
            pltpu.VMEM((BY_MATMUL * chans, block), jnp.bfloat16),
            pltpu.VMEM((chans, BY_MATMUL * chans), jnp.bfloat16),
            pltpu.VMEM((chans, offsets * chans), jnp.float32),
            pltpu.SemaphoreType.DMA((2, looped * STREAMS)),
        ]
        + [pltpu.SMEM((stream,), jnp.int32)] * (looped * STREAMS),
        compiler_params=pltpu.CompilerParams(vmem_limit_bytes=17 << 20),
        name="forward",
    )(map_flat, sparse, features, from_x, from_y, weights, class_t, label_blocks)


def scatter_kernel(first, offsets, has_before, map_hbm, dpre_ref, weight_ref, *refs):
    refs = list(refs)
    before = refs.pop(0) if has_before else None
    out_ref = refs.pop(0)
    back_refs = [refs.pop(0) for _ in range(4)] if has_before else []
    sems = refs.pop(0)
    tables = refs[:offsets]
    index = refs[offsets:]
    streams, stream, chans = dpre_ref.shape
    share = stream // SCATTER_STEPS
    part = stream // 4
    ready, later = fetch(map_hbm, index, sems, first * streams, stream, (0, part, stream))
    for table in tables:
        table[...] = jnp.zeros_like(table)
    for copy in ready:
        copy.wait()

    def step(j, carry):
        for n in range(share):
            i = j * share + n
            for u in range(streams):
                value = dpre_ref[u, pl.ds(i, 1), :]
                for k in range(offsets):
                    where = pl.ds(index[k * streams + u][i], 1)
                    tables[k][where, :] = tables[k][where, :] + value
        return carry

    lax.fori_loop(0, SCATTER_STEPS // 4, step, 0)
    for copy in later:
        copy.wait()
    lax.fori_loop(SCATTER_STEPS // 4, SCATTER_STEPS, step, 0)
    tiles = 3
    height = out_ref.shape[0] // tiles

    def finish(t, carry):
        at = pl.ds(pl.multiple_of(t * height, 16), height)
        wide = jnp.concatenate([table[at, :].astype(jnp.bfloat16) for table in tables], axis=1)
        result = dot(wide, weight_ref[first * chans : (first + offsets) * chans, :], NN)
        out_ref[at, :] = result + before[at, :] if has_before else result
        return carry

    lax.fori_loop(0, tiles, finish, 0)
    if back_refs:
        width = back_refs[0].shape[0]
        voxels = streams * stream
        halos = [out_ref[voxels + n * width : voxels + (n + 1) * width, :] for n in range(4)]
        picked = over_edges(halos[2], halos[3], "ty") + over_edges(halos[0], halos[1], "tx")
        for back_ref, value in zip(back_refs, picked):
            back_ref[...] = value.astype(jnp.bfloat16)


def scatter(map_flat, dpre, flipped, before, first, offsets, table_rows, width):
    voxels, chans = dpre.shape
    stream = voxels // SCATTER_STREAMS
    has_before = before is not None
    return pl.pallas_call(
        functools.partial(scatter_kernel, first, offsets, has_before),
        out_shape=[jax.ShapeDtypeStruct((table_rows, chans), jnp.float32)]
        + [jax.ShapeDtypeStruct((width, chans), jnp.bfloat16)] * (4 if has_before else 0),
        in_specs=[HBM, VMEM, VMEM] + ([VMEM] if has_before else []),
        out_specs=[VMEM] * (5 if has_before else 1),
        scratch_shapes=[
            pltpu.SemaphoreType.DMA((2, offsets * SCATTER_STREAMS)),
        ]
        + [pltpu.VMEM((table_rows, chans), jnp.float32)] * offsets
        + [pltpu.SMEM((stream,), jnp.int32)] * (offsets * SCATTER_STREAMS),
        compiler_params=pltpu.CompilerParams(vmem_limit_bytes=21 << 20),
        cost_estimate=pl.CostEstimate(
            flops=2 * voxels * offsets * chans * chans, bytes_accessed=40 << 20, transcendentals=0
        ),
        name=f"scatter_{first}",
    )(
        map_flat, dpre.reshape(SCATTER_STREAMS, stream, chans), flipped,
        *([before] if has_before else []),
    )


def finish_kernel(dmixed_ref, dext_ref, send_ref, x_refs, y_refs, out_ref, back_ref):
    voxels, chans = out_ref.shape
    width = x_refs[0].shape[0]
    low_x, high_x = from_neighbours(x_refs, "tx")
    low_y, high_y = from_neighbours(y_refs, "ty")
    for n, value in enumerate((high_x, low_x, high_y, low_y)):
        back_ref[n * width : (n + 1) * width, :] = value.astype(jnp.bfloat16)
    height = voxels // 2

    def step(t, carry):
        at = pl.ds(pl.multiple_of(t * height, height), height)
        row = lax.broadcasted_iota(jnp.int32, (height, send_ref.shape[1]), 0) + t * height
        chosen = (row == send_ref[...]).astype(jnp.float32).astype(jnp.bfloat16)
        out_ref[at, :] = dmixed_ref[at, :] + dext_ref[at, :] + dot(chosen, back_ref[...], NN)
        return carry

    lax.fori_loop(0, voxels // height, step, 0)


def finish(dmixed, dext, send_flat, from_x, from_y):
    return pl.pallas_call(
        finish_kernel,
        out_shape=jax.ShapeDtypeStruct(dmixed.shape, jnp.float32),
        in_specs=[VMEM, VMEM, VMEM, [VMEM] * len(from_x), [VMEM] * len(from_y)],
        out_specs=VMEM,
        scratch_shapes=[pltpu.VMEM((send_flat.shape[1], dmixed.shape[1]), jnp.bfloat16)],
        compiler_params=pltpu.CompilerParams(vmem_limit_bytes=12 << 20),
        cost_estimate=pl.CostEstimate(flops=1 << 28, bytes_accessed=4 << 20, transcendentals=0),
        name="finish",
    )(dmixed, dext, send_flat, from_x, from_y)


def outgoing_kernel(axes, send_hbm, own_hbm, *refs):
    *out_refs, send_ref, own_ref, sems, table, sent = refs
    voxels, chans = own_ref.shape
    send_copy = pltpu.make_async_copy(send_hbm, send_ref, sems.at[0])
    send_copy.start()
    own_copy = pltpu.make_async_copy(own_hbm, own_ref, sems.at[1])
    own_copy.start()
    own_copy.wait()
    width = send_ref.shape[1]
    table[:voxels, :] = own_ref[...].astype(jnp.float32)
    table[voxels:, :] = jnp.zeros((table.shape[0] - voxels, chans), jnp.float32)
    send_copy.wait()
    for s in range(4):

        def step(t, carry, s=s):
            for n in range(32):
                i = t * 32 + n
                sent[pl.ds(s * width + i, 1), :] = table[pl.ds(send_ref[s, i], 1), :]
            return carry

        lax.fori_loop(0, width // 32, step, 0)
    lists = [sent[s * width : (s + 1) * width, :] for s in range(4)]
    picked = []
    for axis, (up, down) in zip(axes, ((2, 3), (0, 1))):
        picked.extend(over_edges(lists[down], lists[up], axis))
    for out_ref, value in zip(out_refs, picked):
        out_ref[...] = value.astype(jnp.bfloat16)


def outgoing(send_rows, features):
    voxels, chans = features.shape
    width = send_rows.shape[1]
    return pl.pallas_call(
        functools.partial(outgoing_kernel, ("ty", "tx")),
        out_shape=[jax.ShapeDtypeStruct((width, chans), jnp.bfloat16)] * 4,
        in_specs=[HBM, HBM],
        out_specs=[VMEM] * 4,
        scratch_shapes=[
            pltpu.SMEM(send_rows.shape, jnp.int32),
            pltpu.VMEM(features.shape, jnp.bfloat16),
            pltpu.SemaphoreType.DMA((2,)),
            pltpu.VMEM((voxels + 8, chans), jnp.float32),
            pltpu.VMEM((4 * width, chans), jnp.float32),
        ],
        compiler_params=pltpu.CompilerParams(vmem_limit_bytes=60 << 20),
        cost_estimate=pl.CostEstimate(flops=0, bytes_accessed=8 << 20, transcendentals=0),
        name="outgoing",
    )(send_rows, features)


def assemble_kernel(axes, scale, conv_rows, *refs):
    *piece_refs, conv_ref, head_ref = refs
    pieces = len(piece_refs)
    height = piece_refs[0].shape[0]
    mine = group_index(axes)
    for d, piece_ref in enumerate(piece_refs):
        for p in range(pieces):

            @pl.when((mine ^ d) == p)
            def _(p=p, piece_ref=piece_ref):
                start = p * height
                inside = max(0, min(height, conv_rows - start))
                if inside:
                    value = piece_ref[:inside, :].astype(jnp.float32) * scale
                    conv_ref[start : start + inside, :] = value
                if start <= conv_rows < start + height:
                    at = conv_rows - start
                    value = piece_ref[at : at + HEAD_ROWS, :].astype(jnp.float32) * scale
                    head_ref[...] = value[: head_ref.shape[0], :]


def assemble(pieces, axes, scale, conv_rows, classes):
    chans = pieces[0].shape[1]
    return pl.pallas_call(
        functools.partial(assemble_kernel, axes, scale, conv_rows),
        out_shape=(
            jax.ShapeDtypeStruct((conv_rows, chans), jnp.float32),
            jax.ShapeDtypeStruct((classes, chans), jnp.float32),
        ),
        in_specs=[VMEM] * len(pieces),
        out_specs=(VMEM, VMEM),
        compiler_params=pltpu.CompilerParams(vmem_limit_bytes=12 << 20),
        name="assemble",
    )(*pieces)


def group_index(axes):
    at = 0
    for axis in axes:
        at = at * lax.axis_size(axis) + lax.axis_index(axis)
    return at


def group_size(axes):
    return math.prod(lax.axis_size(axis) for axis in axes)


def exchange(shard, axes, distance):
    return lax.ppermute(shard, axes, [(i, i ^ distance) for i in range(group_size(axes))])


def edge_pairs(axis):
    devices = lax.axis_size(axis)
    even = [(i, i ^ 1) for i in range(devices) if (i ^ 1) < devices]
    odd = [(i, ((i + 1) ^ 1) - 1) for i in range(1, devices) if ((i + 1) ^ 1) - 1 < devices]
    return even, odd


def swap_edges(over_even, over_odd, axis):
    even_pairs, odd_pairs = edge_pairs(axis)
    got = [lax.ppermute(over_even, axis, even_pairs)]
    if odd_pairs:
        got.append(lax.ppermute(over_odd, axis, odd_pairs))
    return got


def on_device(features, conv_weight, classifier, send_rows, neighbour_map, labels):
    voxels, chans = features.shape
    width = send_rows.shape[1]
    offsets = conv_weight.shape[0]
    classes = classifier.shape[1]
    block = STREAMS * SEGMENT
    table_rows = -(-(voxels + 4 * width + 1) // 48) * 48
    square = ("ty", "rep")
    pieces = group_size(square)
    unit = 16 * pieces
    reduce_rows = -(-(offsets * chans + HEAD_ROWS) // unit) * unit
    height = reduce_rows // pieces

    even_y, odd_y, even_x, odd_x = outgoing(send_rows, features)
    from_y = swap_edges(even_y, odd_y, "ty")
    from_x = swap_edges(even_x, odd_x, "tx")

    zero_row = voxels + 4 * width
    moved = jnp.where(neighbour_map > voxels, neighbour_map - 1, neighbour_map)
    moved = jnp.where(neighbour_map == voxels, zero_row, moved)
    map_flat = moved.reshape(-1)
    sparse = (
        moved[offsets - BY_MATMUL :].reshape(BY_MATMUL, STREAMS, voxels // block, SEGMENT)
        .transpose(2, 0, 1, 3).reshape(voxels // block, BY_MATMUL, block)
    )
    weights = conv_weight.reshape(offsets * chans, chans)
    class_t = jnp.pad(classifier.T, ((0, HEAD_ROWS - classes), (0, 0)))
    label_blocks = (
        jnp.minimum(labels, classes).reshape(STREAMS, voxels // block, SEGMENT).transpose(1, 0, 2)
        .reshape(voxels // block, 1, block)
    )
    dpre, dmixed, part, flipped = forward(
        map_flat, sparse, features, from_x, from_y, weights, class_t, label_blocks,
        classes, reduce_rows, table_rows,
    )

    chunks = [(c * offsets // CHUNKS, (c + 1) * offsets // CHUNKS) for c in range(CHUNKS)]

    halo = []

    def scatter_beside(sent, before):
        first, last = chunks.pop(0)
        held = (sent, dpre) if before is None else (sent, dpre, before)
        held = lax.optimization_barrier(held)
        dext, *blocks = scatter(
            map_flat, held[1], flipped, None if before is None else held[2],
            first, last - first, table_rows, width,
        )
        halo.extend(blocks)
        return held[0], dext

    mine = group_index(square)
    sent = []
    for d in range(1, pieces):
        piece = lax.dynamic_slice_in_dim(part, (mine ^ d) * height, height, axis=0)
        sent.append(piece.astype(jnp.bfloat16))
    own = lax.dynamic_slice_in_dim(part, mine * height, height, axis=0)
    (sent, own), dext = scatter_beside((sent, own), None)
    got = [exchange(piece, square, d + 1) for d, piece in enumerate(sent)]
    got, dext = lax.optimization_barrier((got, dext))
    own = own + sum(piece.astype(jnp.float32) for piece in got)

    stride = 1
    while stride < lax.axis_size("tx"):
        radix = min(4, lax.axis_size("tx") // stride)
        own = own.astype(jnp.bfloat16)
        if chunks:
            own, dext = scatter_beside(own, dext)
        got = [own] + [exchange(own, ("tx",), m * stride) for m in range(1, radix)]
        got, dext, halo = lax.optimization_barrier((got, dext, halo))
        got = [piece.astype(jnp.float32) for piece in got]
        while len(got) > 1:
            got = [a + b for a, b in zip(got[::2], got[1::2])]
        own = got[0]
        stride *= radix
    while chunks:
        own, dext = scatter_beside(own, dext)

    from_y = swap_edges(halo[0], halo[1], "ty")
    from_x = swap_edges(halo[2], halo[3], "tx")
    everywhere = {0: own.astype(jnp.bfloat16)}
    bit = pieces // 2
    while bit:
        if bit == 1:
            everywhere, from_x, from_y = lax.optimization_barrier((everywhere, from_x, from_y))
        for d, piece in list(everywhere.items()):
            everywhere[d | bit] = exchange(piece, square, bit)
        bit //= 2
    grad_input = finish(dmixed, dext, send_rows.reshape(1, -1), from_x, from_y)
    everywhere = [everywhere[d] for d in range(pieces)]
    count = voxels * lax.axis_size("tx") * lax.axis_size("ty") * lax.axis_size("rep")
    conv, head = assemble(everywhere, square, 1.0 / math.sqrt(count), offsets * chans, classes)
    return grad_input, conv.reshape(offsets, chans, chans), head.T


def solution(mesh):
    placed = (
        P(("groups", "tx", "ty", "rep"), None),
        P(),
        P(),
        P(("groups", "tx", "ty", "rep"), None),
        P(None, ("groups", "tx", "ty", "rep")),
        P(("groups", "tx", "ty", "rep")),
    )
    return jax.shard_map(
        on_device,
        mesh=mesh,
        in_specs=placed,
        out_specs=(
            P(("groups", "tx", "ty", "rep"), None),
            P("groups", None, None),
            P("groups", None),
        ),
        check_vma=False,
    )
```
